32 devices in a mesh: tile: 16 (over z, x, core), tm: 2 (over y).
Axes of the slice: x: 2, y: 2, z: 4, core: 2. Of those that a mesh axis runs over, the one named last changes fastest.
Arguments:
- controls: float32 [4, 128, 8, 512], P('tm', 'tile'), may hold values from -6 to 6
- perturbations: bfloat16 [2, 4, 4, 128, 8, 512], P('tm', None, None, 'tile'), may hold values from -6 to 6
- owner: int32 [4], replicated, may hold values from 0 to 3, each once
- land_mask: int32 [128, 512], P('tile'), may hold values 0 or 1
- diffusivity: float32 [2, 8], replicated, may hold values from 0.2 to 0.24
Outputs:
- increment: float32 [2, 4, 128, 8, 512], P('tm', None, 'tile')
The draws below stay inside these ranges and needn't reach their ends.
Inputs may be any that keep to these rules, and one draw needn't show every extreme that they name: owner names every member exactly once.
All inputs are finite; a program needn't handle non-finite values. No bound on the sum of `land_mask` on one device may be relied on, other than what follows from the above.
Results may differ from the reference program's by a relative error of at most 0.0029.
Values may be sent and summed in bfloat16 or wider, within the bound.
No kernel may reach another device: no remote copies, remote signals or barrier semaphores. Data moves between devices by JAX's collectives and lax.ppermute only.
A program may use at most 64 MiB of HBM per device.

```python
import math
import jax
import jax.numpy as jnp
from jax import lax

NY = 512
LEV = 8
VARS = 4
SWEEPS = 4
MEMBERS = 4
TIMES = 2
NX = 128


def draw_controls(key, part):
    sign_key = jax.random.fold_in(key, 11)
    noise_key = jax.random.fold_in(key, 12)
    member_sign = 1.0 - 2.0 * jax.random.randint(sign_key, (MEMBERS,), 0, 2).astype(jnp.float32)
    row_sign = 1.0 - 2.0 * (jnp.arange(NX, dtype=jnp.int32) % 2).astype(jnp.float32)
    noise = jax.random.normal(noise_key, (MEMBERS, NX, LEV, NY), jnp.float32)
    field = 5.5 * member_sign[:, None, None, None] * row_sign[None, :, None, None] + 0.3 * noise
    return jnp.clip(field, -6.0, 6.0).astype(jnp.float32)


def place_ends(values, stream_key, least, largest):
    longest = values.shape.index(max(values.shape))
    spots = []
    for shift in (0, 1):
        where = [jax.random.randint(jax.random.fold_in(stream_key, axis), (), 0, length) for axis, length in enumerate(values.shape)]
        where[longest] = (where[longest] + shift) % values.shape[longest]
        spots.append(tuple(where))
    return values.at[spots[0]].set(least).at[spots[1]].set(largest)


def level_of(rng, dims, cuts, smallest, largest):
    factor_of, own = 1.0, jax.random.fold_in(rng, 6)
    for position, parts in cuts:
        heights = jnp.exp(jax.random.uniform(jax.random.fold_in(own, position), (parts,), jnp.float32, smallest / len(cuts), largest / len(cuts)))
        factor_of = factor_of * jnp.repeat(heights, dims[position] // parts).reshape([-1 if axis == position else 1 for axis in range(len(dims))])
    return factor_of


def bell_draw(stream_key, shape, scale, most, shards=(), held_as=jnp.bfloat16):
    gain = level_of(stream_key, shape, shards, -0.22, 0.18) if shards else 1.0
    values = jax.random.normal(stream_key, shape, jnp.float32) * scale * gain
    return jnp.minimum(jnp.maximum(values, -most), most).astype(held_as)


def setup_inputs(seed: int = 0) -> dict:
    arg_keys = jax.random.split(jax.random.key(seed), 6)
    controls = draw_controls(jax.random.fold_in(arg_keys[5], 71), 0)
    perturbations = bell_draw(arg_keys[1], (TIMES, MEMBERS, VARS, NX, LEV, NY), 1.0, 6.0, ((0, 2), (3, 16)))
    owner = jax.random.permutation(arg_keys[2], MEMBERS).astype(jnp.int32)
    land_mask = place_ends((jax.random.randint(arg_keys[3], (NX, NY), 0, 5) < 2).astype(jnp.int32), jax.random.fold_in(arg_keys[3], 1), 0, 1)
    diffusivity = jnp.clip(jnp.exp(jax.random.uniform(arg_keys[4], (2, LEV), jnp.float32, math.log(0.2), math.log(0.24))), 0.2, 0.24)
    return dict(controls=controls, perturbations=perturbations, owner=owner, land_mask=land_mask, diffusivity=diffusivity)


def weight_sweep(field, coef):
    padded = jnp.pad(field, ((0, 0), (1, 1), (0, 0), (1, 1)))
    coef_pad = jnp.pad(coef, ((1, 1), (0, 0), (1, 1)))
    flux = 0.5 * (coef + coef_pad[:-2, :, 1:-1]) * (padded[:, :-2, :, 1:-1] - field)
    flux = flux + 0.5 * (coef + coef_pad[2:, :, 1:-1]) * (padded[:, 2:, :, 1:-1] - field)
    flux = flux + 0.5 * (coef + coef_pad[1:-1, :, :-2]) * (padded[:, 1:-1, :, :-2] - field)
    flux = flux + 0.5 * (coef + coef_pad[1:-1, :, 2:]) * (padded[:, 1:-1, :, 2:] - field)
    return field + flux

def reference(controls, perturbations, owner, land_mask, diffusivity):
    diffuse_coef = jnp.where(land_mask[:, None, :] == 1, diffusivity[1][None, :, None], diffusivity[0][None, :, None])
    smooth = controls
    for sweep_index in range(SWEEPS):
        smooth = weight_sweep(smooth, diffuse_coef)
    weights = smooth.astype(jnp.bfloat16)
    by_member = jnp.zeros_like(weights).at[owner].set(weights)
    factor = 1.0 / math.sqrt(MEMBERS - 1)

    def one_time(pert_time):
        summed = jnp.zeros(pert_time.shape[1:], jnp.float32)
        for member in range(MEMBERS):
            summed = summed + pert_time[member].astype(jnp.float32) * by_member[member].astype(jnp.float32)[None]
        return summed * factor
    return lax.map(one_time, perturbations)
```

```python
import math

import jax
import jax.numpy as jnp
from jax import lax
from jax.sharding import PartitionSpec as P

SWEEPS = 4


def swap(value, axis, first):
    count = lax.axis_size(axis)
    pairs = [(i, i + 1) for i in range(first, count - 1, 2)]
    return lax.ppermute(value, axis, pairs + [(b, a) for a, b in pairs])


def packed(controls, code, start):
    slots, _, levels, columns = controls.shape
    rows = lax.dynamic_slice_in_dim(controls, start, SWEEPS, axis=1)
    marks = lax.dynamic_slice_in_dim(code, start, SWEEPS, axis=0)
    marks = jnp.pad(marks, ((0, levels - SWEEPS), (0, 0)))
    return jnp.concatenate([rows.reshape(slots * SWEEPS, levels, columns), marks[None]], axis=0)


def unpacked(packet, slots):
    _, levels, columns = packet.shape
    rows = packet[: slots * SWEEPS].reshape(slots, SWEEPS, levels, columns)
    return rows, packet[slots * SWEEPS, :SWEEPS]


def on_device(controls, perturbations, owner, land_mask, diffusivity):
    slots, height, levels, columns = controls.shape
    odd = lax.axis_index("tile") % 2
    code = land_mask.astype(jnp.float32) + 1.0
    tail = height - SWEEPS
    across = swap(packed(controls, code, tail * odd), "tile", 1)
    within = swap(packed(controls, code, tail * (1 - odd)), "tile", 0)
    low, low_code = unpacked(jnp.where(odd == 1, within, across), slots)
    high, high_code = unpacked(jnp.where(odd == 1, across, within), slots)
    field = jnp.concatenate([low, controls, high], axis=1)
    code = jnp.concatenate([low_code, code, high_code], axis=0)[:, None, :]
    kappa = jnp.where(code == 2.0, diffusivity[1][None, :, None], diffusivity[0][None, :, None])
    inside = code > 0.0
    kappa = jnp.where(inside, kappa, 0.0)

    east = 0.5 * (kappa + jnp.pad(kappa, ((0, 0), (0, 0), (0, 1)))[:, :, 1:])
    west = 0.5 * (kappa + jnp.pad(kappa, ((0, 0), (0, 0), (1, 0)))[:, :, :-1])
    south = 0.5 * (kappa[:-1] + kappa[1:])
    for _ in range(SWEEPS):
        wide = jnp.pad(field, ((0, 0), (0, 0), (0, 0), (1, 1)))[:, 1:-1]
        here = field[:, 1:-1]
        flux = south[:-1] * (field[:, :-2] - here) + south[1:] * (field[:, 2:] - here)
        flux = flux + west[1:-1] * (wide[..., :-2] - here) + east[1:-1] * (wide[..., 2:] - here)
        field = jnp.where(inside[1:-1], here + flux, 0.0)
        east, west, south, inside = east[1:-1], west[1:-1], south[1:-1], inside[1:-1]
    weights = field.astype(jnp.bfloat16)

    factor = 1.0 / math.sqrt(owner.shape[0] - 1)
    count = lax.axis_size("tm")
    here = lax.axis_index("tm")
    summed = None
    for step in range(count):
        if step == 0:
            arrived = weights
        else:
            arrived = lax.ppermute(weights, "tm", [(i, (i + step) % count) for i in range(count)])
        chosen = lax.dynamic_slice_in_dim(owner, (here - step) % count * slots, slots)
        for slot in range(slots):
            pert = lax.dynamic_index_in_dim(perturbations[0], chosen[slot], 0, keepdims=False)
            term = pert.astype(jnp.float32) * arrived[slot].astype(jnp.float32)[None]
            summed = term if summed is None else summed + term
    return (summed * factor)[None]


def solution(mesh):
    return jax.shard_map(
        on_device,
        mesh=mesh,
        in_specs=(
            P("tm", "tile", None, None),
            P("tm", None, None, "tile", None, None),
            P(),
            P("tile", None),
            P(),
        ),
        out_specs=P("tm", None, "tile", None, None),
        check_vma=False,
    )
```

```python
import math

import jax
import jax.numpy as jnp
from jax import lax
from jax.experimental import pallas as pl
from jax.experimental.pallas import tpu as pltpu
from jax.sharding import PartitionSpec as P

SWEEPS = 4
VMEM = pl.BlockSpec(memory_space=pltpu.VMEM)
SMEM = pl.BlockSpec(memory_space=pltpu.SMEM)
ANY = pl.BlockSpec(memory_space=pl.ANY)
PARAMS = pltpu.CompilerParams(vmem_limit_bytes=16 * 1024 * 1024)


def parity():
    return lax.rem(lax.axis_index("tile"), 2)


def own_row(odd, j):
    return j + odd * (2 * SWEEPS - 1 - 2 * j)


def half_row(odd, j):
    return j % SWEEPS + odd * (SWEEPS - 1 - 2 * (j % SWEEPS))


def outer_start(odd):
    return SWEEPS * odd


def inner_start(odd):
    return SWEEPS * (1 - odd)


def swap(value, axis, first):
    count = lax.axis_size(axis)
    pairs = [(i, i + 1) for i in range(first, count - 1, 2)]
    return lax.ppermute(value, axis, pairs + [(b, a) for a, b in pairs])


def pack_kernel(controls, mask, within, across, rows, sems):
    odd = parity()
    slots = controls.shape[0]
    copies = [pltpu.make_async_copy(mask, rows, sems.at[2 * slots])]
    for slot in range(slots):
        for side, (start, packet) in enumerate(((outer_start(odd), across), (inner_start(odd), within))):
            copies.append(
                pltpu.make_async_copy(
                    controls.at[slot, pl.ds(start, SWEEPS)],
                    packet.at[pl.ds(SWEEPS * slot, SWEEPS)],
                    sems.at[2 * slot + side],
                )
            )
    for copy in copies:
        copy.start()
    copies[0].wait()
    code = rows[...].astype(jnp.float32) + 1.0
    within[SWEEPS * slots] = code
    across[SWEEPS * slots] = code
    for copy in copies[1:]:
        copy.wait()


def by_level(diffusivity, kind, shape):
    level = lax.broadcasted_iota(jnp.int32, shape, 0)
    value = jnp.full(shape, diffusivity[kind, 0], jnp.float32)
    for index in range(1, shape[0]):
        value = jnp.where(level == index, diffusivity[kind, index], value)
    return value


def kappa_of(code, sea, land):
    code = jnp.broadcast_to(code, sea.shape)
    return jnp.where(code == 2.0, land, jnp.where(code == 1.0, sea, 0.0))


def along_row(kappa):
    columns = kappa.shape[1]
    lane = lax.broadcasted_iota(jnp.int32, kappa.shape, 1)
    last = lane == columns - 1
    loss = 0.5 * (kappa + jnp.where(last, 0.0, pltpu.roll(kappa, columns - 1, 1)))
    east = jnp.where(last, 0.0, loss)
    west = pltpu.roll(east, 1, 1)
    return east, west, loss + jnp.where(lane == 0, 0.5 * kappa, west)


def update(centre, east, west, below, above, here, before, after):
    columns = here.shape[1]
    value = centre * here + below * before + above * after
    value = value + east * pltpu.roll(here, columns - 1, 1)
    return value + west * pltpu.roll(here, 1, 1)


FACE, EAST, WEST, CENTRE, KAPPA = 0, 4, 8, 12, 16


def inner_kernel(controls, packet, mask, diffusivity, weights, kept, coef, face, centre, east, west, field):
    odd = parity()
    slots, _, levels, columns = controls.shape
    shape = (levels, columns)
    sea, land = by_level(diffusivity, 0, shape), by_level(diffusivity, 1, shape)
    total = 3 * SWEEPS

    def far_row(k):
        return k + odd * (SWEEPS - 1 - 2 * k)

    def kappa_at(j):
        if j < 2 * SWEEPS:
            code = mask[pl.ds(own_row(odd, j), 1), :].astype(jnp.float32) + 1.0
        else:
            place = far_row(j - 2 * SWEEPS) + SWEEPS * odd
            code = packet[slots * SWEEPS, pl.ds(place, 1), :]
        return kappa_of(code, sea, land)

    previous = kappa_at(0)
    coef[KAPPA] = previous
    e, w, loss = along_row(previous)
    coef[EAST], coef[WEST] = e, w
    lost = loss
    for j in range(1, total):
        kappa = kappa_at(j)
        step = 0.5 * (previous + kappa)
        face[j] = step
        centre[j - 1] = 1.0 - (lost + step)
        if j <= SWEEPS:
            coef[FACE + j - 1] = step
            coef[CENTRE + j - 1] = 1.0 - (lost + step)
        if j < total - 1:
            e, w, loss = along_row(kappa)
            east[j], west[j] = e, w
            if j < SWEEPS:
                coef[EAST + j], coef[WEST + j] = e, w
            lost = loss + step
        previous = kappa

    for slot in range(slots):
        def start(j):
            if j < 2 * SWEEPS:
                return controls[slot, own_row(odd, j)]
            return packet[SWEEPS * slot + far_row(j - 2 * SWEEPS)]

        for sweep in range(1, SWEEPS + 1):
            def read(j):
                return start(j) if sweep == 1 else field[sweep - 2, slot, j]

            low, high = sweep, total - sweep
            before, here = read(low - 1), read(low)
            for j in range(low, high):
                after = read(j + 1)
                value = update(centre[j], east[j], west[j], face[j], face[j + 1], here, before, after)
                if sweep == SWEEPS:
                    weights[slot, half_row(odd, j)] = value.astype(weights.dtype)
                else:
                    field[sweep - 1, slot, j] = value
                    if j - sweep < 2:
                        kept[slot, 2 * (sweep - 1) + j - sweep] = value
                before, here = here, after


def outer_kernel(controls, packet, kept, coef, diffusivity, weights, face, centre, east, west, field):
    odd = parity()
    tile, tiles = lax.axis_index("tile"), lax.axis_size("tile")
    slots, _, levels, columns = controls.shape
    shape = (levels, columns)
    sea, land = by_level(diffusivity, 0, shape), by_level(diffusivity, 1, shape)
    edge = jnp.where(odd == 1, tile == tiles - 1, tile == 0)
    inside = jnp.where(edge, 0.0, 1.0).astype(jnp.float32)

    def far_row(k):
        return SWEEPS - 1 - k + odd * (2 * k - SWEEPS + 1)

    previous = None
    lost = None
    for j in range(-SWEEPS, 1):
        if j < 0:
            place = far_row(-1 - j) + SWEEPS * (1 - odd)
            kappa = kappa_of(packet[slots * SWEEPS, pl.ds(place, 1), :], sea, land)
        else:
            kappa = coef[KAPPA]
        if previous is not None:
            step = 0.5 * (previous + kappa)
            face[j + SWEEPS] = step
            if lost is not None:
                centre[j - 1 + SWEEPS] = 1.0 - (lost + step)
            if j < 0:
                e, w, loss = along_row(kappa)
                east[j + SWEEPS], west[j + SWEEPS] = e, w
                lost = loss + step
            else:
                centre[SWEEPS] = coef[CENTRE] - step
        previous = kappa

    def coefficients(j):
        if j < 0:
            i = j + SWEEPS
            return centre[i], east[i], west[i], face[i], face[i + 1]
        if j == 0:
            return centre[SWEEPS], coef[EAST], coef[WEST], face[SWEEPS], coef[FACE]
        return coef[CENTRE + j], coef[EAST + j], coef[WEST + j], coef[FACE + j - 1], coef[FACE + j]

    for slot in range(slots):
        for sweep in range(1, SWEEPS + 1):
            def read(j):
                if sweep == 1:
                    if j >= 0:
                        return controls[slot, own_row(odd, j)]
                    return packet[SWEEPS * slot + far_row(-1 - j)]
                if j >= sweep - 1:
                    return kept[slot, 2 * (sweep - 2) + j - (sweep - 1)]
                return field[sweep - 2, slot, j + SWEEPS]

            low = sweep - SWEEPS
            before, here = read(low - 1), read(low)
            for j in range(low, sweep):
                after = read(j + 1)
                value = update(*coefficients(j), here, before, after)
                if j < 0:
                    value = value * inside
                if sweep == SWEEPS:
                    weights[slot, half_row(odd, j)] = value.astype(weights.dtype)
                else:
                    field[sweep - 1, slot, j + SWEEPS] = value
                before, here = here, after


def early_kernel(arrivals, factor, *refs):
    pert, owner, inner, outer = refs[:4]
    arrived = refs[4 : 4 + arrivals]
    out, partial, chosen, ready, sems, out_sems = refs[4 + arrivals :]
    odd = parity()
    count, here = lax.axis_size("tm"), lax.axis_index("tm")
    slots = inner.shape[0]
    variables = pert.shape[1]

    def member(step, slot):
        return owner[lax.rem(here - step + count, count) * slots + slot]

    copies = []
    for step in range(1, count):
        for slot in range(slots):
            place = (step - 1) * slots + slot
            copies.append(
                pltpu.make_async_copy(
                    pert.at[member(step, slot), :, pl.ds(outer_start(odd), SWEEPS)],
                    chosen.at[place],
                    sems.at[place],
                )
            )
            copies[-1].start()

    for row in range(SWEEPS):
        total = [None] * variables
        for step in range(count):
            source = inner if step == 0 else arrived[step - 1]
            for slot in range(slots):
                weight = source[slot, row].astype(jnp.float32) * factor
                who = member(step, slot)
                for v in range(variables):
                    term = pert[who, v, inner_start(odd) + row].astype(jnp.float32) * weight
                    total[v] = term if total[v] is None else total[v] + term
        for v in range(variables):
            ready[v, row] = total[v]
    writes = []
    for v in range(variables):
        writes.append(
            pltpu.make_async_copy(ready.at[v], out.at[v, pl.ds(inner_start(odd), SWEEPS)], out_sems.at[v])
        )
        writes[-1].start()
    for row in range(SWEEPS):
        total = [None] * variables
        for slot in range(slots):
            weight = outer[slot, row].astype(jnp.float32) * factor
            who = member(0, slot)
            for v in range(variables):
                term = pert[who, v, outer_start(odd) + row].astype(jnp.float32) * weight
                total[v] = term if total[v] is None else total[v] + term
        for v in range(variables):
            partial[v, row] = total[v]
    for copy in copies + writes:
        copy.wait()


def late_kernel(arrivals, factor, *refs):
    partial, chosen = refs[:2]
    arrived = refs[2 : 2 + arrivals]
    _, out, ready, sems = refs[2 + arrivals :]
    odd = parity()
    variables = partial.shape[0]
    slots = arrived[0].shape[0] if arrivals else 0
    writes = []
    for v in range(variables):
        for row in range(SWEEPS):
            total = partial[v, row]
            for index in range(arrivals):
                for slot in range(slots):
                    weight = arrived[index][slot, row].astype(jnp.float32) * factor
                    total = total + chosen[index * slots + slot, v, row].astype(jnp.float32) * weight
            ready[v, row] = total
        writes.append(
            pltpu.make_async_copy(ready.at[v], out.at[v, pl.ds(outer_start(odd), SWEEPS)], sems.at[v])
        )
        writes[-1].start()
    for copy in writes:
        copy.wait()


def cost(flops, moved):
    return pl.CostEstimate(flops=flops, bytes_accessed=moved, transcendentals=0)


def on_device(controls, perturbations, owner, land_mask, diffusivity):
    slots, height, levels, columns = controls.shape
    members, variables = perturbations.shape[1:3]
    count = lax.axis_size("tm")
    factor = 1.0 / math.sqrt(owner.shape[0] - 1)
    row = (levels, columns)
    f32, bf16 = jnp.float32, jnp.bfloat16
    packet = pltpu.VMEM((slots * SWEEPS + 1, *row), f32)
    half = pltpu.VMEM((slots, SWEEPS, *row), bf16)
    dma = pltpu.SemaphoreType.DMA

    within, across = pl.pallas_call(
        pack_kernel,
        out_shape=(packet, packet),
        in_specs=[ANY, ANY],
        out_specs=(VMEM, VMEM),
        scratch_shapes=[pltpu.VMEM((height, columns), land_mask.dtype), dma((2 * slots + 1,))],
        compiler_params=PARAMS,
        name="pack",
    )(controls, land_mask)
    within = swap(within, "tile", 0)
    across = swap(across, "tile", 1)

    mine = pltpu.with_memory_space_constraint(controls, pltpu.VMEM)
    inner, kept, coef = pl.pallas_call(
        inner_kernel,
        out_shape=(half, pltpu.VMEM((slots, 6, *row), f32), pltpu.VMEM((17, *row), f32)),
        in_specs=[VMEM, VMEM, VMEM, SMEM],
        out_specs=(VMEM, VMEM, VMEM),
        scratch_shapes=[pltpu.VMEM((3 * SWEEPS, *row), f32)] * 4
        + [pltpu.VMEM((SWEEPS - 1, slots, 3 * SWEEPS, *row), f32)],
        compiler_params=PARAMS,
        cost_estimate=cost(4_000_000, 1_000_000),
        name="inner_rows",
    )(mine, pltpu.with_memory_space_constraint(within, pltpu.VMEM), land_mask, diffusivity)

    def shift(value):
        return [
            lax.ppermute(value, "tm", [(i, (i + step) % count) for i in range(count)])
            for step in range(1, count)
        ]

    inner_arrived = shift(inner)
    outer = pl.pallas_call(
        outer_kernel,
        out_shape=half,
        in_specs=[VMEM, VMEM, VMEM, VMEM, SMEM],
        out_specs=VMEM,
        scratch_shapes=[pltpu.VMEM((SWEEPS + 1, *row), f32)] * 4
        + [pltpu.VMEM((SWEEPS - 1, slots, 2 * SWEEPS, *row), f32)],
        compiler_params=PARAMS,
        cost_estimate=cost(2_000_000, 1_000_000),
        name="outer_rows",
    )(mine, pltpu.with_memory_space_constraint(across, pltpu.VMEM), kept, coef, diffusivity)
    outer_arrived = shift(outer)

    def near(value):
        return pltpu.with_memory_space_constraint(value, pltpu.VMEM)

    arrivals = count - 1
    result = jax.ShapeDtypeStruct((variables, height, *row), f32)
    part = pltpu.VMEM((variables, SWEEPS, *row), f32)
    others = max(arrivals, 1) * slots
    out, partial, chosen = pl.pallas_call(
        lambda *refs: early_kernel(arrivals, factor, *refs),
        out_shape=(result, part, pltpu.VMEM((others, variables, SWEEPS, *row), bf16)),
        in_specs=[VMEM, SMEM, VMEM, VMEM] + [VMEM] * arrivals,
        out_specs=(ANY, VMEM, VMEM),
        scratch_shapes=[pltpu.VMEM(part.shape, f32), dma((others,)), dma((variables,))],
        compiler_params=PARAMS,
        cost_estimate=cost(4_000_000, 2_000_000),
        name="early_products",
    )(near(perturbations[0]), owner, inner, outer, *map(near, inner_arrived))
    out = pl.pallas_call(
        lambda *refs: late_kernel(arrivals, factor, *refs),
        out_shape=result,
        in_specs=[VMEM, VMEM] + [VMEM] * arrivals + [ANY],
        out_specs=ANY,
        scratch_shapes=[pltpu.VMEM(part.shape, f32), dma((variables,))],
        input_output_aliases={2 + arrivals: 0},
        compiler_params=PARAMS,
        cost_estimate=cost(1_000_000, 1_000_000),
        name="late_products",
    )(partial, chosen, *map(near, outer_arrived), out)
    return out[None]


def solution(mesh):
    return jax.shard_map(
        on_device,
        mesh=mesh,
        in_specs=(
            P("tm", "tile", None, None),
            P("tm", None, None, "tile", None, None),
            P(),
            P("tile", None),
            P(),
        ),
        out_specs=P("tm", None, "tile", None, None),
        check_vma=False,
    )
```

```python
import math

import jax
import jax.numpy as jnp
from jax import lax
from jax.experimental import pallas as pl
from jax.experimental.pallas import tpu as pltpu
from jax.sharding import PartitionSpec as P

SWEEPS = 4
VMEM = pl.BlockSpec(memory_space=pltpu.VMEM)
SMEM = pl.BlockSpec(memory_space=pltpu.SMEM)
ANY = pl.BlockSpec(memory_space=pl.ANY)
PARAMS = pltpu.CompilerParams(vmem_limit_bytes=16 * 1024 * 1024)


def parity():
    return lax.rem(lax.axis_index("tile"), 2)


def own_row(odd, j):
    return j + odd * (2 * SWEEPS - 1 - 2 * j)


def half_row(odd, j):
    return j % SWEEPS + odd * (SWEEPS - 1 - 2 * (j % SWEEPS))


def outer_start(odd):
    return SWEEPS * odd


def inner_start(odd):
    return SWEEPS * (1 - odd)


def swap(value, axis, first):
    count = lax.axis_size(axis)
    pairs = [(i, i + 1) for i in range(first, count - 1, 2)]
    return lax.ppermute(value, axis, pairs + [(b, a) for a, b in pairs])


def swap_across(value):
    tiles, times = lax.axis_size("tile"), lax.axis_size("tm")
    pairs = [((i, t), (i + 1, t)) for i in range(1, tiles - 1, 2) for t in range(times)]
    pairs += [((i, t), (i, t + 1)) for i in (0, tiles - 1) for t in range(0, times, 2)]
    flat = [(a * times + t, b * times + u) for (a, t), (b, u) in pairs]
    return lax.ppermute(value, ("tile", "tm"), flat + [(b, a) for a, b in flat])


def pack_kernel(controls, mask, diffusivity, within, across, by_level, rows, scalars, sems):
    odd = parity()
    slots = controls.shape[0]
    copies = [
        pltpu.make_async_copy(mask, rows, sems.at[2 * slots]),
        pltpu.make_async_copy(diffusivity, scalars, sems.at[2 * slots + 1]),
    ]
    for slot in range(slots):
        for side, (start, packet) in enumerate(((outer_start(odd), across), (inner_start(odd), within))):
            copies.append(
                pltpu.make_async_copy(
                    controls.at[slot, pl.ds(start, SWEEPS)],
                    packet.at[pl.ds(SWEEPS * slot, SWEEPS)],
                    sems.at[2 * slot + side],
                )
            )
    for copy in copies:
        copy.start()
    copies[0].wait()
    code = rows[...].astype(jnp.float32) + 1.0
    within[SWEEPS * slots] = code
    across[SWEEPS * slots] = code
    copies[1].wait()
    shape = by_level.shape[1:]
    level = lax.broadcasted_iota(jnp.int32, shape, 0)
    for kind in range(2):
        value = jnp.full(shape, scalars[kind, 0], jnp.float32)
        for index in range(1, shape[0]):
            value = jnp.where(level == index, scalars[kind, index], value)
        by_level[kind] = value
    for copy in copies[2:]:
        copy.wait()


def kappa_of(code, sea, land):
    return jnp.where(jnp.broadcast_to(code, sea.shape) == 2.0, land, sea)


def along_row(kappa):
    columns = kappa.shape[1]
    lane = lax.broadcasted_iota(jnp.int32, kappa.shape, 1)
    last = lane == columns - 1
    loss = 0.5 * (kappa + jnp.where(last, 0.0, pltpu.roll(kappa, columns - 1, 1)))
    east = jnp.where(last, 0.0, loss)
    west = pltpu.roll(east, 1, 1)
    return east, west, loss + jnp.where(lane == 0, 0.5 * kappa, west)


def update(centre, east, west, below, above, here, before, after):
    columns = here.shape[1]
    value = centre * here + below * before + above * after
    value = value + east * pltpu.roll(here, columns - 1, 1)
    return value + west * pltpu.roll(here, 1, 1)


FACE, EAST, WEST, CENTRE, KAPPA = 0, 4, 8, 12, 16


def inner_kernel(controls, packet, mine, by_level, weights, kept, coef, face, centre, east, west, field):
    odd = parity()
    slots, _, levels, columns = controls.shape
    sea, land = by_level[0], by_level[1]
    total = 3 * SWEEPS

    def far_row(k):
        return k + odd * (SWEEPS - 1 - 2 * k)

    def kappa_at(j):
        if j < 2 * SWEEPS:
            code = mine[slots * SWEEPS, pl.ds(own_row(odd, j), 1), :]
        else:
            place = far_row(j - 2 * SWEEPS) + SWEEPS * odd
            code = packet[slots * SWEEPS, pl.ds(place, 1), :]
        return kappa_of(code, sea, land)

    previous = kappa_at(0)
    coef[KAPPA] = previous
    e, w, loss = along_row(previous)
    coef[EAST], coef[WEST] = e, w
    lost = loss
    for j in range(1, total):
        kappa = kappa_at(j)
        step = 0.5 * (previous + kappa)
        face[j] = step
        centre[j - 1] = 1.0 - (lost + step)
        if j <= SWEEPS:
            coef[FACE + j - 1] = step
            coef[CENTRE + j - 1] = 1.0 - (lost + step)
        if j < total - 1:
            e, w, loss = along_row(kappa)
            east[j], west[j] = e, w
            if j < SWEEPS:
                coef[EAST + j], coef[WEST + j] = e, w
            lost = loss + step
        previous = kappa

    for slot in range(slots):
        def start(j):
            if j < 2 * SWEEPS:
                return controls[slot, own_row(odd, j)]
            return packet[SWEEPS * slot + far_row(j - 2 * SWEEPS)]

        for sweep in range(1, SWEEPS + 1):
            def read(j):
                return start(j) if sweep == 1 else field[sweep - 2, slot, j]

            low, high = sweep, total - sweep
            before, here = read(low - 1), read(low)
            for j in range(low, high):
                after = read(j + 1)
                value = update(centre[j], east[j], west[j], face[j], face[j + 1], here, before, after)
                if sweep == SWEEPS:
                    weights[slot, half_row(odd, j)] = value.astype(weights.dtype)
                else:
                    field[sweep - 1, slot, j] = value
                    if j - sweep < 2:
                        kept[slot, 2 * (sweep - 1) + j - sweep] = value
                before, here = here, after


def outer_kernel(controls, packet, kept, coef, by_level, weights, face, centre, east, west, field):
    odd = parity()
    tile, tiles = lax.axis_index("tile"), lax.axis_size("tile")
    slots, _, levels, columns = controls.shape
    sea, land = by_level[0], by_level[1]
    edge = jnp.where(odd == 1, tile == tiles - 1, tile == 0)
    inside = jnp.where(edge, 0.0, 1.0).astype(jnp.float32)

    def far_row(k):
        return SWEEPS - 1 - k + odd * (2 * k - SWEEPS + 1)

    previous = None
    lost = None
    for j in range(-SWEEPS, 1):
        if j < 0:
            place = far_row(-1 - j) + SWEEPS * (1 - odd)
            kappa = kappa_of(packet[slots * SWEEPS, pl.ds(place, 1), :], sea, land) * inside
        else:
            kappa = coef[KAPPA]
        if previous is not None:
            step = 0.5 * (previous + kappa)
            face[j + SWEEPS] = step
            if lost is not None:
                centre[j - 1 + SWEEPS] = 1.0 - (lost + step)
            if j < 0:
                e, w, loss = along_row(kappa)
                east[j + SWEEPS], west[j + SWEEPS] = e, w
                lost = loss + step
            else:
                centre[SWEEPS] = coef[CENTRE] - step
        previous = kappa

    def coefficients(j):
        if j < 0:
            i = j + SWEEPS
            return centre[i], east[i], west[i], face[i], face[i + 1]
        if j == 0:
            return centre[SWEEPS], coef[EAST], coef[WEST], face[SWEEPS], coef[FACE]
        return coef[CENTRE + j], coef[EAST + j], coef[WEST + j], coef[FACE + j - 1], coef[FACE + j]

    for slot in range(slots):
        for sweep in range(1, SWEEPS + 1):
            def read(j):
                if sweep == 1:
                    if j >= 0:
                        return controls[slot, own_row(odd, j)]
                    return packet[SWEEPS * slot + far_row(-1 - j)] * inside
                if j >= sweep - 1:
                    return kept[slot, 2 * (sweep - 2) + j - (sweep - 1)]
                return field[sweep - 2, slot, j + SWEEPS]

            low = sweep - SWEEPS
            before, here = read(low - 1), read(low)
            for j in range(low, sweep):
                after = read(j + 1)
                value = update(*coefficients(j), here, before, after)
                if j < 0:
                    value = value * inside
                if sweep == SWEEPS:
                    weights[slot, half_row(odd, j)] = value.astype(weights.dtype)
                else:
                    field[sweep - 1, slot, j + SWEEPS] = value
                before, here = here, after


def early_kernel(arrivals, factor, *refs):
    pert, owner, inner, outer = refs[:4]
    arrived = refs[4 : 4 + arrivals]
    out, partial, chosen, ready, sems, out_sems = refs[4 + arrivals :]
    odd = parity()
    count, here = lax.axis_size("tm"), lax.axis_index("tm")
    slots = inner.shape[0]
    variables = pert.shape[1]

    def member(step, slot):
        return owner[lax.rem(here - step + count, count) * slots + slot]

    copies = []
    for step in range(1, count):
        for slot in range(slots):
            place = (step - 1) * slots + slot
            copies.append(
                pltpu.make_async_copy(
                    pert.at[member(step, slot), :, pl.ds(outer_start(odd), SWEEPS)],
                    chosen.at[place],
                    sems.at[place],
                )
            )
            copies[-1].start()

    for row in range(SWEEPS):
        total = [None] * variables
        for step in range(count):
            source = inner if step == 0 else arrived[step - 1]
            for slot in range(slots):
                weight = source[slot, row].astype(jnp.float32) * factor
                who = member(step, slot)
                for v in range(variables):
                    term = pert[who, v, inner_start(odd) + row].astype(jnp.float32) * weight
                    total[v] = term if total[v] is None else total[v] + term
        for v in range(variables):
            ready[v, row] = total[v]
    writes = []
    for v in range(variables):
        writes.append(
            pltpu.make_async_copy(ready.at[v], out.at[v, pl.ds(inner_start(odd), SWEEPS)], out_sems.at[v])
        )
        writes[-1].start()
    for row in range(SWEEPS):
        total = [None] * variables
        for slot in range(slots):
            weight = outer[slot, row].astype(jnp.float32) * factor
            who = member(0, slot)
            for v in range(variables):
                term = pert[who, v, outer_start(odd) + row].astype(jnp.float32) * weight
                total[v] = term if total[v] is None else total[v] + term
        for v in range(variables):
            partial[v, row] = total[v]
    for copy in copies + writes:
        copy.wait()


def late_kernel(arrivals, factor, *refs):
    partial, chosen = refs[:2]
    arrived = refs[2 : 2 + arrivals]
    _, out, ready, sems = refs[2 + arrivals :]
    odd = parity()
    variables = partial.shape[0]
    slots = arrived[0].shape[0] if arrivals else 0
    writes = []
    for v in range(variables):
        for row in range(SWEEPS):
            total = partial[v, row]
            for index in range(arrivals):
                for slot in range(slots):
                    weight = arrived[index][slot, row].astype(jnp.float32) * factor
                    total = total + chosen[index * slots + slot, v, row].astype(jnp.float32) * weight
            ready[v, row] = total
        writes.append(
            pltpu.make_async_copy(ready.at[v], out.at[v, pl.ds(outer_start(odd), SWEEPS)], sems.at[v])
        )
        writes[-1].start()
    for copy in writes:
        copy.wait()


def cost(flops, moved):
    return pl.CostEstimate(flops=flops, bytes_accessed=moved, transcendentals=0)


def on_device(controls, perturbations, owner, land_mask, diffusivity):
    slots, height, levels, columns = controls.shape
    members, variables = perturbations.shape[1:3]
    count = lax.axis_size("tm")
    factor = 1.0 / math.sqrt(owner.shape[0] - 1)
    row = (levels, columns)
    f32, bf16 = jnp.float32, jnp.bfloat16
    packet = pltpu.VMEM((slots * SWEEPS + 1, *row), f32)
    half = pltpu.VMEM((slots, SWEEPS, *row), bf16)
    dma = pltpu.SemaphoreType.DMA

    def near(value):
        return pltpu.with_memory_space_constraint(value, pltpu.VMEM)

    def far(value):
        return pltpu.with_memory_space_constraint(value, pltpu.HBM)

    my_within, my_across, by_level = pl.pallas_call(
        pack_kernel,
        out_shape=(packet, packet, pltpu.VMEM((2, *row), f32)),
        in_specs=[ANY, ANY, ANY],
        out_specs=(VMEM, VMEM, VMEM),
        scratch_shapes=[
            pltpu.VMEM((height, columns), land_mask.dtype),
            pltpu.SMEM((2, levels), f32),
            dma((2 * slots + 2,)),
        ],
        compiler_params=PARAMS,
        name="pack",
    )(far(controls), far(land_mask), far(diffusivity))
    across = swap_across(my_across)
    within = swap(my_within, "tile", 0)

    mine = near(controls)
    inner, kept, coef = pl.pallas_call(
        inner_kernel,
        out_shape=(half, pltpu.VMEM((slots, 6, *row), f32), pltpu.VMEM((17, *row), f32)),
        in_specs=[VMEM, VMEM, VMEM, VMEM],
        out_specs=(VMEM, VMEM, VMEM),
        scratch_shapes=[pltpu.VMEM((3 * SWEEPS, *row), f32)] * 4
        + [pltpu.VMEM((SWEEPS - 1, slots, 3 * SWEEPS, *row), f32)],
        compiler_params=PARAMS,
        cost_estimate=cost(4_000_000, 1_000_000),
        name="inner_rows",
    )(mine, near(within), near(my_within), near(by_level))

    def shift(value):
        return [
            lax.ppermute(value, "tm", [(i, (i + step) % count) for i in range(count)])
            for step in range(1, count)
        ]

    inner_arrived = shift(inner)
    outer = pl.pallas_call(
        outer_kernel,
        out_shape=half,
        in_specs=[VMEM, VMEM, VMEM, VMEM, VMEM],
        out_specs=VMEM,
        scratch_shapes=[pltpu.VMEM((SWEEPS + 1, *row), f32)] * 4
        + [pltpu.VMEM((SWEEPS - 1, slots, 2 * SWEEPS, *row), f32)],
        compiler_params=PARAMS,
        cost_estimate=cost(2_000_000, 1_000_000),
        name="outer_rows",
    )(mine, near(across), near(kept), near(coef), near(by_level))
    outer_arrived = shift(outer)

    arrivals = count - 1
    result = jax.ShapeDtypeStruct((variables, height, *row), f32)
    part = pltpu.VMEM((variables, SWEEPS, *row), f32)
    others = max(arrivals, 1) * slots
    out, partial, chosen = pl.pallas_call(
        lambda *refs: early_kernel(arrivals, factor, *refs),
        out_shape=(result, part, pltpu.VMEM((others, variables, SWEEPS, *row), bf16)),
        in_specs=[VMEM, SMEM, VMEM, VMEM] + [VMEM] * arrivals,
        out_specs=(ANY, VMEM, VMEM),
        scratch_shapes=[pltpu.VMEM(part.shape, f32), dma((others,)), dma((variables,))],
        compiler_params=PARAMS,
        cost_estimate=cost(4_000_000, 2_000_000),
        name="early_products",
    )(near(perturbations[0]), owner, near(inner), near(outer), *map(near, inner_arrived))
    out = pl.pallas_call(
        lambda *refs: late_kernel(arrivals, factor, *refs),
        out_shape=result,
        in_specs=[VMEM, VMEM] + [VMEM] * arrivals + [ANY],
        out_specs=ANY,
        scratch_shapes=[pltpu.VMEM(part.shape, f32), dma((variables,))],
        input_output_aliases={2 + arrivals: 0},
        compiler_params=PARAMS,
        cost_estimate=cost(1_000_000, 1_000_000),
        name="late_products",
    )(near(partial), near(chosen), *map(near, outer_arrived), out)
    return out[None]


def solution(mesh):
    return jax.shard_map(
        on_device,
        mesh=mesh,
        in_specs=(
            P("tm", "tile", None, None),
            P("tm", None, None, "tile", None, None),
            P(),
            P("tile", None),
            P(),
        ),
        out_specs=P("tm", None, "tile", None, None),
        check_vma=False,
    )
```

```python
import math

import jax
import jax.numpy as jnp
from jax import lax
from jax.experimental import pallas as pl
from jax.experimental.pallas import tpu as pltpu
from jax.sharding import PartitionSpec as P

SWEEPS = 4
VMEM = pl.BlockSpec(memory_space=pltpu.VMEM)
SMEM = pl.BlockSpec(memory_space=pltpu.SMEM)
ANY = pl.BlockSpec(memory_space=pl.ANY)
PARAMS = pltpu.CompilerParams(vmem_limit_bytes=16 * 1024 * 1024)


def parity():
    return lax.rem(lax.axis_index("tile"), 2)


def own_row(odd, j):
    return j + odd * (2 * SWEEPS - 1 - 2 * j)


def half_row(odd, j):
    return j % SWEEPS + odd * (SWEEPS - 1 - 2 * (j % SWEEPS))


def outer_start(odd):
    return SWEEPS * odd


def inner_start(odd):
    return SWEEPS * (1 - odd)


def swap_within(value):
    pairs = [(i, i + 1) for i in range(0, lax.axis_size("tile"), 2)]
    return lax.ppermute(value, "tile", pairs + [(b, a) for a, b in pairs])


def swap_across(value):
    tiles, times = lax.axis_size("tile"), lax.axis_size("tm")
    pairs = [((i, t), (i + 1, t)) for i in range(1, tiles - 1, 2) for t in range(times)]
    pairs += [((i, t), (i, t + 1)) for i in (0, tiles - 1) for t in range(0, times, 2)]
    flat = [(a * times + t, b * times + u) for (a, t), (b, u) in pairs]
    return lax.ppermute(value, ("tile", "tm"), flat + [(b, a) for a, b in flat])


def half_codes(odd, code):
    half = code.shape[1] // 2
    left, right = code[:, :half], code[:, half:]
    top = lax.broadcasted_iota(jnp.int32, left.shape, 0) < SWEEPS
    even = jnp.where(top, left, pltpu.roll(right, SWEEPS, 0))
    return jnp.where(odd == 1, jnp.where(top, pltpu.roll(left, SWEEPS, 0), right), even)


def pack_kernel(controls, mask, diffusivity, across, codes, table, rows, sems):
    odd = parity()
    slots, columns = controls.shape[0], controls.shape[3]
    half, count = columns // 2, slots * SWEEPS
    copies = [
        pltpu.make_async_copy(mask, rows, sems.at[0]),
        pltpu.make_async_copy(diffusivity, table, sems.at[1]),
    ]
    for slot in range(slots):
        for side in range(2):
            copies.append(
                pltpu.make_async_copy(
                    controls.at[slot, pl.ds(outer_start(odd), SWEEPS), :, pl.ds(side * half, half)],
                    across.at[pl.ds(side * count + slot * SWEEPS, SWEEPS)],
                    sems.at[len(copies)],
                )
            )
    for copy in copies[2:] + copies[:2]:
        copy.start()
    copies[0].wait()
    code = rows[...].astype(jnp.float32) + 1.0
    codes[...] = code
    across[2 * count] = half_codes(odd, code)
    for copy in copies[1:]:
        copy.wait()


def within_kernel(controls, codes, first, second):
    odd = parity()
    for slot, piece in enumerate((first, second)):
        for row in range(SWEEPS):
            piece[row] = controls[slot, inner_start(odd) + row]
    second[SWEEPS] = codes[...]


def by_level(table, kind, shape):
    level = lax.broadcasted_iota(jnp.int32, shape, 0)
    value = jnp.broadcast_to(table[kind : kind + 1, 0:1], shape)
    for index in range(1, shape[0]):
        value = jnp.where(level == index, table[kind : kind + 1, index : index + 1], value)
    return value


def kappa_of(code, sea, land):
    return jnp.where(jnp.broadcast_to(code, sea.shape) == 2.0, land, sea)


def along_row(kappa):
    columns = kappa.shape[1]
    lane = lax.broadcasted_iota(jnp.int32, kappa.shape, 1)
    last = lane == columns - 1
    loss = kappa + jnp.where(last, 0.0, pltpu.roll(kappa, columns - 1, 1))
    east = jnp.where(last, 0.0, loss)
    west = pltpu.roll(east, 1, 1)
    return east, west, loss + jnp.where(lane == 0, kappa, west)


def sideways(centre, east, west, here):
    columns = here.shape[1]
    return centre * here + east * pltpu.roll(here, columns - 1, 1) + west * pltpu.roll(here, 1, 1)


FACE, EAST, WEST, CENTRE, KAPPA, COEFS = 0, 4, 8, 12, 16, 17
PART, VALUE, KEPT = 0, SWEEPS, 2 * SWEEPS - 1
OUTER, INNER = 0, 1


def row_of(side, odd, k):
    return own_row(odd, k if side == OUTER else 2 * SWEEPS - 1 - k)


def middle_kernel(controls, codes, table, kept, coef, halves, face, centre, east, west, field):
    odd = parity()
    slots, _, levels, columns = controls.shape
    shape = (levels, columns)
    total = 2 * SWEEPS
    for kind in range(2):
        halves[kind] = 0.5 * by_level(table, kind, shape)
    sea, land = halves[0], halves[1]

    previous = lost = None
    for j in range(total):
        kappa = kappa_of(codes[pl.ds(own_row(odd, j), 1), :], sea, land)
        e, w, loss = along_row(kappa)
        east[j], west[j] = e, w
        if j:
            face[j] = previous + kappa
            centre[j - 1] = 1.0 - (lost + face[j])
            lost = loss + face[j]
        else:
            lost = loss
        previous = kappa
        for side, k in ((OUTER, j), (INNER, total - 1 - j)):
            if k == 0:
                coef[side, KAPPA] = kappa
            if k < SWEEPS:
                coef[side, EAST + k], coef[side, WEST + k] = e, w
    centre[total - 1] = 1.0 - lost
    for k in range(SWEEPS):
        coef[OUTER, CENTRE + k], coef[INNER, CENTRE + k] = centre[k], centre[total - 1 - k]
        if k:
            coef[OUTER, FACE + k], coef[INNER, FACE + k] = face[k], face[total - k]

    def value(slot, sweep, j):
        return field[sweep - 1, slot, j] if sweep else controls[slot, own_row(odd, j)]

    for sweep in range(1, SWEEPS + 1):
        low, high = sweep - 1, total - sweep
        before = [None] * slots
        here = [value(slot, sweep - 1, low) for slot in range(slots)]
        for j in range(low, high + 1):
            c, e, w = centre[j], east[j], west[j]
            below = face[j] if j > low else None
            above = face[j + 1] if j < high else None
            for slot in range(slots):
                after = None
                result = sideways(c, e, w, here[slot])
                if above is not None:
                    after = value(slot, sweep - 1, j + 1)
                    result = result + above * after
                if below is not None:
                    result = result + below * before[slot]
                if j == low:
                    kept[OUTER, slot, PART + sweep - 1] = result
                elif j == high:
                    kept[INNER, slot, PART + sweep - 1] = result
                else:
                    field[sweep - 1, slot, j] = result
                    if j == low + 1:
                        kept[OUTER, slot, VALUE + sweep - 1] = result
                    if j == high - 1:
                        kept[INNER, slot, VALUE + sweep - 1] = result
                before[slot], here[slot] = here[slot], after


def side_rows(side, odd, controls, far, far_kappa, inside, kept, coef, weights, face, centre, east, west, field):
    slots = controls.shape[0]

    def masked(value):
        return value if inside is None else value * inside

    previous = masked(far_kappa(-SWEEPS))
    lost = None
    for k in range(1 - SWEEPS, 1):
        i = k + SWEEPS
        kappa = masked(far_kappa(k)) if k else coef[side, KAPPA]
        step = previous + kappa
        face[i] = step
        if lost is not None:
            centre[i - 1] = 1.0 - (lost + step)
        if k:
            e, w, loss = along_row(kappa)
            east[i], west[i] = e, w
            lost = loss + step
        else:
            centre[i] = coef[side, CENTRE] - step
        previous = kappa
    first = face[SWEEPS]
    first_inside = masked(first)

    def value(slot, sweep, k):
        if sweep == 0:
            return masked(far(slot, k)) if k < 0 else controls[slot, row_of(side, odd, k)]
        if k == sweep:
            return kept[side, slot, VALUE + sweep - 1]
        return field[sweep - 1, slot, k + SWEEPS]

    for sweep in range(1, SWEEPS + 1):
        low = sweep - SWEEPS
        before = [value(slot, sweep - 1, low - 1) for slot in range(slots)]
        here = [value(slot, sweep - 1, low) for slot in range(slots)]
        for k in range(low, sweep):
            i = k + SWEEPS
            below = face[i] if k < 0 else first if k == 0 else coef[side, FACE + k]
            if k < sweep - 1:
                above = face[i + 1] if k < -1 else first_inside if k == -1 else coef[side, FACE + k + 1]
                c = centre[i] if k <= 0 else coef[side, CENTRE + k]
                e, w = (east[i], west[i]) if k < 0 else (coef[side, EAST + k], coef[side, WEST + k])
            for slot in range(slots):
                after = None
                if k < sweep - 1:
                    after = value(slot, sweep - 1, k + 1)
                    result = sideways(c, e, w, here[slot]) + above * after + below * before[slot]
                elif k == 0:
                    result = kept[side, slot, PART] + below * (before[slot] - here[slot])
                else:
                    result = kept[side, slot, PART + sweep - 1] + below * before[slot]
                if sweep == SWEEPS:
                    place = half_row(odd, k if side == OUTER else 2 * SWEEPS - 1 - k)
                    weights[slot, place] = result.astype(weights.dtype)
                else:
                    field[sweep - 1, slot, i] = result
                before[slot], here[slot] = here[slot], after


def inner_kernel(controls, first, second, kept, coef, halves, weights, *scratch):
    odd = parity()

    def place(k):
        return -1 - k + odd * (SWEEPS + 1 + 2 * k)

    def far(slot, k):
        return (first, second)[slot][place(k)]

    def far_kappa(k):
        return kappa_of(second[SWEEPS, pl.ds(place(k) + SWEEPS * odd, 1), :], halves[0], halves[1])

    side_rows(INNER, odd, controls, far, far_kappa, None, kept, coef, weights, *scratch)


def outer_kernel(controls, packet, kept, coef, halves, weights, *scratch):
    odd = parity()
    tile, tiles = lax.axis_index("tile"), lax.axis_size("tile")
    count = controls.shape[0] * SWEEPS
    edge = jnp.where(odd == 1, tile == tiles - 1, tile == 0)
    inside = jnp.where(edge, 0.0, 1.0).astype(jnp.float32)

    def place(k):
        return SWEEPS + k - odd * (2 * k + SWEEPS + 1)

    def far(slot, k):
        at = SWEEPS * slot + place(k)
        return jnp.concatenate([packet[at], packet[count + at]], axis=1)

    def far_kappa(k):
        left = packet[2 * count, pl.ds(place(k), 1), :]
        right = packet[2 * count, pl.ds(place(k) + SWEEPS, 1), :]
        return kappa_of(jnp.concatenate([left, right], axis=1), halves[0], halves[1])

    side_rows(OUTER, odd, controls, far, far_kappa, inside, kept, coef, weights, *scratch)


def products(pert, weight, total):
    return [
        term if old is None else old + term
        for old, term in zip(total, [p.astype(jnp.float32) * weight for p in pert])
    ]


def own_kernel(factor, pert, owner, inner, outer, near_part, far_part, near_others, far_others, sems):
    odd = parity()
    count, here = lax.axis_size("tm"), lax.axis_index("tm")
    slots, variables = inner.shape[0], pert.shape[1]

    def member(step, slot):
        return owner[lax.rem(here - step + count, count) * slots + slot]

    copies = []
    for step in range(1, count):
        for slot in range(slots):
            place = (step - 1) * slots + slot
            for side, (start, others) in enumerate(
                ((inner_start(odd), near_others), (outer_start(odd), far_others))
            ):
                copies.append(
                    pltpu.make_async_copy(
                        pert.at[member(step, slot), :, pl.ds(start, SWEEPS)],
                        others.at[place],
                        sems.at[2 * place + side],
                    )
                )
    for copy in copies:
        copy.start()
    for start, weights, part in (
        (inner_start(odd), inner, near_part),
        (outer_start(odd), outer, far_part),
    ):
        for row in range(SWEEPS):
            total = [None] * variables
            for slot in range(slots):
                weight = weights[slot, row].astype(jnp.float32) * factor
                who = member(0, slot)
                total = products([pert[who, v, start + row] for v in range(variables)], weight, total)
            for v in range(variables):
                part[v, row] = total[v]
    for copy in copies:
        copy.wait()


def add_others(factor, part, others, arrived, row):
    variables = part.shape[0]
    total = [part[v, row] for v in range(variables)]
    for index, weights in enumerate(arrived):
        slots = weights.shape[0]
        for slot in range(slots):
            weight = weights[slot, row].astype(jnp.float32) * factor
            place = index * slots + slot
            total = products([others[place, v, row] for v in range(variables)], weight, total)
    return total


def add_and_write(factor, start, part, others, arrived, out, ready, sems):
    for row in range(SWEEPS):
        for v, total in enumerate(add_others(factor, part, others, arrived, row)):
            ready[v, row] = total
    writes = [
        pltpu.make_async_copy(ready.at[v], out.at[v, pl.ds(start, SWEEPS)], sems.at[v])
        for v in range(part.shape[0])
    ]
    for copy in writes:
        copy.start()
    for copy in writes:
        copy.wait()


def near_kernel(factor, part, others, *refs):
    *arrived, out, ready, sems = refs
    add_and_write(factor, inner_start(parity()), part, others, arrived, out, ready, sems)


def far_kernel(factor, part, others, *refs):
    *arrived, _, out, ready, sems = refs
    add_and_write(factor, outer_start(parity()), part, others, arrived, out, ready, sems)


def cost(flops, moved):
    return pl.CostEstimate(flops=flops, bytes_accessed=moved, transcendentals=0)


def near(value):
    return pltpu.with_memory_space_constraint(value, pltpu.VMEM)


def far(value):
    return pltpu.with_memory_space_constraint(value, pltpu.HBM)


def on_device(controls, perturbations, owner, land_mask, diffusivity):
    slots, height, levels, columns = controls.shape
    members, variables = perturbations.shape[1:3]
    count = lax.axis_size("tm")
    factor = 1.0 / math.sqrt(owner.shape[0] - 1)
    row = (levels, columns)
    f32, bf16 = jnp.float32, jnp.bfloat16
    dma = pltpu.SemaphoreType.DMA

    packet = pltpu.VMEM((2 * slots * SWEEPS + 1, levels, columns // 2), f32)
    mine = near(controls)
    my_across, codes, table = pl.pallas_call(
        pack_kernel,
        out_shape=(packet, pltpu.VMEM((height, columns), f32), pltpu.VMEM((2, levels), f32)),
        in_specs=[ANY, ANY, ANY],
        out_specs=(VMEM, VMEM, VMEM),
        scratch_shapes=[pltpu.VMEM((height, columns), land_mask.dtype), dma((2 * slots + 2,))],
        compiler_params=PARAMS,
        name="pack",
    )(far(controls), far(land_mask), far(diffusivity))
    across = swap_across(my_across)
    my_within = pl.pallas_call(
        within_kernel,
        out_shape=(pltpu.VMEM((SWEEPS, *row), f32), pltpu.VMEM((SWEEPS + 1, *row), f32)),
        in_specs=[VMEM, VMEM],
        out_specs=(VMEM, VMEM),
        compiler_params=PARAMS,
        cost_estimate=cost(1, 1),
        name="pack_within",
    )(mine, near(codes))
    within = [swap_within(value) for value in my_within]

    kept, coef, halves = pl.pallas_call(
        middle_kernel,
        out_shape=(
            pltpu.VMEM((2, slots, KEPT, *row), f32),
            pltpu.VMEM((2, COEFS, *row), f32),
            pltpu.VMEM((2, *row), f32),
        ),
        in_specs=[VMEM] * 3,
        out_specs=(VMEM,) * 3,
        scratch_shapes=[pltpu.VMEM((height, *row), f32)] * 4
        + [pltpu.VMEM((SWEEPS - 1, slots, height, *row), f32)],
        compiler_params=PARAMS,
        cost_estimate=cost(1, 1),
        name="middle",
    )(mine, near(codes), near(table))
    shared = (near(kept), near(coef), near(halves))

    def side(kernel, arrived, name):
        return pl.pallas_call(
            kernel,
            out_shape=pltpu.VMEM((slots, SWEEPS, *row), bf16),
            in_specs=[VMEM] * (4 + len(arrived)),
            out_specs=VMEM,
            scratch_shapes=[pltpu.VMEM((SWEEPS + 1, *row), f32)] * 4
            + [pltpu.VMEM((SWEEPS - 1, slots, 2 * SWEEPS, *row), f32)],
            compiler_params=PARAMS,
            cost_estimate=cost(1, 1),
            name=name,
        )(mine, *map(near, arrived), *shared)

    inner = side(inner_kernel, within, "inner_rows")

    def shift(value):
        return [
            near(lax.ppermute(value, "tm", [(i, (i + step) % count) for i in range(count)]))
            for step in range(1, count)
        ]

    inner_arrived = shift(inner)
    outer = side(outer_kernel, [across], "outer_rows")
    outer_arrived = shift(outer)

    arrivals = count - 1
    part = pltpu.VMEM((variables, SWEEPS, *row), f32)
    others = pltpu.VMEM((max(arrivals, 1) * slots, variables, SWEEPS, *row), bf16)
    near_part, far_part, near_others, far_others = pl.pallas_call(
        lambda *refs: own_kernel(factor, *refs),
        out_shape=(part, part, others, others),
        in_specs=[VMEM, SMEM, VMEM, VMEM],
        out_specs=(VMEM,) * 4,
        scratch_shapes=[dma((2 * max(arrivals, 1) * slots,))],
        compiler_params=PARAMS,
        cost_estimate=cost(4_000_000, 2_000_000),
        name="own_products",
    )(near(perturbations[0]), owner, near(inner), near(outer))
    result = jax.ShapeDtypeStruct((variables, height, *row), f32)
    scratch = [pltpu.VMEM((variables, SWEEPS, *row), f32), dma((variables,))]
    out = pl.pallas_call(
        lambda *refs: near_kernel(factor, *refs),
        out_shape=result,
        in_specs=[VMEM] * (2 + arrivals),
        out_specs=ANY,
        scratch_shapes=scratch,
        compiler_params=PARAMS,
        cost_estimate=cost(1_000_000, 1_000_000),
        name="near_products",
    )(near(near_part), near(near_others), *inner_arrived)
    out = pl.pallas_call(
        lambda *refs: far_kernel(factor, *refs),
        out_shape=result,
        in_specs=[VMEM] * (2 + arrivals) + [ANY],
        out_specs=ANY,
        scratch_shapes=scratch,
        input_output_aliases={2 + arrivals: 0},
        compiler_params=PARAMS,
        cost_estimate=cost(1_000_000, 1_000_000),
        name="far_products",
    )(near(far_part), near(far_others), *outer_arrived, out)
    return out[None]


def solution(mesh):
    return jax.shard_map(
        on_device,
        mesh=mesh,
        in_specs=(
            P("tm", "tile", None, None),
            P("tm", None, None, "tile", None, None),
            P(),
            P("tile", None),
            P(),
        ),
        out_specs=P("tm", None, "tile", None, None),
        check_vma=False,
    )
```

```python
import functools
import math

import jax
import jax.numpy as jnp
from jax import lax
from jax.experimental import pallas as pl
from jax.experimental.pallas import tpu as pltpu
from jax.sharding import PartitionSpec as P

SWEEPS = 4
VMEM = pl.BlockSpec(memory_space=pltpu.VMEM)
SMEM = pl.BlockSpec(memory_space=pltpu.SMEM)
ANY = pl.BlockSpec(memory_space=pl.ANY)
PARAMS = pltpu.CompilerParams(vmem_limit_bytes=16 * 1024 * 1024)


def parity():
    return lax.rem(lax.axis_index("tile"), 2)


def own_row(odd, j):
    return j + odd * (2 * SWEEPS - 1 - 2 * j)


OUTER, INNER = 0, 1


def row_of(side, odd, k):
    return own_row(odd, k if side == OUTER else 2 * SWEEPS - 1 - k)


def half_row(odd, j):
    return j % SWEEPS + odd * (SWEEPS - 1 - 2 * (j % SWEEPS))


def outer_start(odd):
    return SWEEPS * odd


def inner_start(odd):
    return SWEEPS * (1 - odd)


def swap_within(value):
    pairs = [(i, i + 1) for i in range(0, lax.axis_size("tile"), 2)]
    return lax.ppermute(value, "tile", pairs + [(b, a) for a, b in pairs])


def swap_across(value):
    tiles, times = lax.axis_size("tile"), lax.axis_size("tm")
    pairs = [((i, t), (i + 1, t)) for i in range(1, tiles - 1, 2) for t in range(times)]
    pairs += [((i, t), (i, t + 1)) for i in (0, tiles - 1) for t in range(0, times, 2)]
    flat = [(a * times + t, b * times + u) for (a, t), (b, u) in pairs]
    return lax.ppermute(value, ("tile", "tm"), flat + [(b, a) for a, b in flat])


FRACTION = (20, 18, 14, 12)


def to_fixed(value, bits):
    return jnp.round(value * float(2**bits)).astype(jnp.int32) + (8 << bits)


def from_fixed(value, bits):
    return (value - (8 << bits)).astype(jnp.float32) * float(0.5**bits)


def word_count(slots):
    return 2 * slots + (slots + 1) // 2


def encode(slots, read, code, packet):
    words, last = [], []
    for slot in range(slots):
        one, two, three, four = (to_fixed(read(slot, k), FRACTION[k]) for k in range(SWEEPS))
        words += [one | (two << 24), (two >> 8) | (three << 14)]
        last.append(four)
    words += [sum(value << (16 * i) for i, value in enumerate(last[at : at + 2])) for at in range(0, slots, 2)]
    width = packet.shape[2]
    parts = words[0].shape[1] // width
    for index, word in enumerate(words):
        for part in range(parts):
            packet[index * parts + part] = word[:, part * width : (part + 1) * width]
    for k in range(SWEEPS):
        value = code(k)
        for part in range(parts // 2):
            low = value[:, part * width : (part + 1) * width]
            high = value[:, (part + parts // 2) * width : (part + parts // 2 + 1) * width]
            packet[len(words) * parts, pl.ds(k * (parts // 2) + part, 1), :] = low | (high << 16)


def decode(packet, slots, slot, k):
    count = word_count(slots)
    parts = (packet.shape[0] - 1) // count

    def word(index):
        return jnp.concatenate([packet[index * parts + part] for part in range(parts)], axis=1)

    def right(value, bits):
        return lax.shift_right_logical(value, jnp.int32(bits))

    if k == 0:
        value = word(2 * slot) & 0xFFFFFF
    elif k == 1:
        value = right(word(2 * slot), 24) | ((word(2 * slot + 1) & 0x3FFF) << 8)
    elif k == 2:
        value = right(word(2 * slot + 1), 14)
    else:
        value = word(2 * slots + slot // 2)
        value = right(value, 16) if slot % 2 else value & 0xFFFF
    return from_fixed(value, FRACTION[k])


def decode_codes(packet, slots, k):
    count = word_count(slots)
    half = (packet.shape[0] - 1) // count // 2
    words = [packet[packet.shape[0] - 1, pl.ds(k * half + part, 1), :] for part in range(half)]
    return jnp.concatenate([word & 0xFFFF for word in words] + [word >> 16 for word in words], axis=1)


def pack_kernel(controls, mask, diffusivity, packet, codes, table, rows, sems):
    odd = parity()
    slots = controls.shape[0]
    copies = [
        pltpu.make_async_copy(mask, codes, sems.at[0]),
        pltpu.make_async_copy(diffusivity, table, sems.at[1]),
    ]
    for slot in range(slots):
        for part in range(2):
            at = SWEEPS // 2 * part
            copies.append(
                pltpu.make_async_copy(
                    controls.at[slot, pl.ds(outer_start(odd) + at, SWEEPS // 2)],
                    rows.at[slot, pl.ds(at, SWEEPS // 2)],
                    sems.at[len(copies)],
                )
            )
    for copy in copies[2:] + copies[:2]:
        copy.start()
    for copy in copies:
        copy.wait()
    encode(
        slots,
        lambda slot, k: rows[slot, half_row(odd, k)],
        lambda k: codes[pl.ds(row_of(OUTER, odd, k), 1), :] + 1,
        packet,
    )


def within_kernel(controls, codes, packet):
    odd = parity()
    encode(
        controls.shape[0],
        lambda slot, k: controls[slot, row_of(INNER, odd, k)],
        lambda k: codes[pl.ds(row_of(INNER, odd, k), 1), :] + 1,
        packet,
    )


def by_level(table, kind, shape):
    level = lax.broadcasted_iota(jnp.int32, shape, 0)
    value = jnp.broadcast_to(table[kind : kind + 1, 0:1], shape)
    for index in range(1, shape[0]):
        value = jnp.where(level == index, table[kind : kind + 1, index : index + 1], value)
    return value


def kappa_of(code, sea, land):
    return jnp.where(jnp.broadcast_to(code, sea.shape) == 2, land, sea)


def along_row(kappa):
    columns = kappa.shape[1]
    lane = lax.broadcasted_iota(jnp.int32, kappa.shape, 1)
    last = lane == columns - 1
    loss = kappa + jnp.where(last, 0.0, pltpu.roll(kappa, columns - 1, 1))
    east = jnp.where(last, 0.0, loss)
    west = pltpu.roll(east, 1, 1)
    return east, west, loss + jnp.where(lane == 0, kappa, west)


def sideways(centre, east, west, here):
    columns = here.shape[1]
    return centre * here + east * pltpu.roll(here, columns - 1, 1) + west * pltpu.roll(here, 1, 1)


FACE, EAST, WEST, CENTRE, KAPPA, COEFS = 0, 4, 8, 12, 16, 17
PART, VALUE, KEPT = 0, SWEEPS, 2 * SWEEPS - 1


def middle_kernel(controls, codes, table, kept, coef, halves, face, centre, east, west, field):
    odd = parity()
    slots, _, levels, columns = controls.shape
    shape = (levels, columns)
    total = 2 * SWEEPS
    for kind in range(2):
        halves[kind] = 0.5 * by_level(table, kind, shape)
    sea, land = halves[0], halves[1]

    previous = lost = None
    for j in range(total):
        kappa = kappa_of(codes[pl.ds(own_row(odd, j), 1), :] + 1, sea, land)
        e, w, loss = along_row(kappa)
        east[j], west[j] = e, w
        if j:
            face[j] = previous + kappa
            centre[j - 1] = 1.0 - (lost + face[j])
            lost = loss + face[j]
        else:
            lost = loss
        previous = kappa
        for side, k in ((OUTER, j), (INNER, total - 1 - j)):
            if k == 0:
                coef[side, KAPPA] = kappa
            if k < SWEEPS:
                coef[side, EAST + k], coef[side, WEST + k] = e, w
    centre[total - 1] = 1.0 - lost
    for k in range(SWEEPS):
        coef[OUTER, CENTRE + k], coef[INNER, CENTRE + k] = centre[k], centre[total - 1 - k]
        if k:
            coef[OUTER, FACE + k], coef[INNER, FACE + k] = face[k], face[total - k]

    def value(slot, sweep, j):
        return field[sweep - 1, slot, j] if sweep else controls[slot, own_row(odd, j)]

    for sweep in range(1, SWEEPS + 1):
        low, high = sweep - 1, total - sweep
        before = [None] * slots
        here = [value(slot, sweep - 1, low) for slot in range(slots)]
        for j in range(low, high + 1):
            c, e, w = centre[j], east[j], west[j]
            below = face[j] if j > low else None
            above = face[j + 1] if j < high else None
            for slot in range(slots):
                after = None
                result = sideways(c, e, w, here[slot])
                if above is not None:
                    after = value(slot, sweep - 1, j + 1)
                    result = result + above * after
                if below is not None:
                    result = result + below * before[slot]
                if j == low:
                    kept[OUTER, slot, PART + sweep - 1] = result
                elif j == high:
                    kept[INNER, slot, PART + sweep - 1] = result
                else:
                    field[sweep - 1, slot, j] = result
                    if j == low + 1:
                        kept[OUTER, slot, VALUE + sweep - 1] = result
                    if j == high - 1:
                        kept[INNER, slot, VALUE + sweep - 1] = result
                before[slot], here[slot] = here[slot], after


def side_rows(side, odd, controls, far, far_kappa, inside, kept, coef, weights, face, centre, east, west, field):
    slots = controls.shape[0]

    def masked(value):
        return value if inside is None else value * inside

    previous = masked(far_kappa(-SWEEPS))
    lost = None
    for k in range(1 - SWEEPS, 1):
        i = k + SWEEPS
        kappa = masked(far_kappa(k)) if k else coef[side, KAPPA]
        step = previous + kappa
        face[i] = step
        if lost is not None:
            centre[i - 1] = 1.0 - (lost + step)
        if k:
            e, w, loss = along_row(kappa)
            east[i], west[i] = e, w
            lost = loss + step
        else:
            centre[i] = coef[side, CENTRE] - step
        previous = kappa
    first = face[SWEEPS]
    first_inside = masked(first)

    def value(slot, sweep, k):
        if sweep == 0:
            return masked(far(slot, k)) if k < 0 else controls[slot, row_of(side, odd, k)]
        if k == sweep:
            return kept[side, slot, VALUE + sweep - 1]
        return field[sweep - 1, slot, k + SWEEPS]

    for sweep in range(1, SWEEPS + 1):
        low = sweep - SWEEPS
        before = [value(slot, sweep - 1, low - 1) for slot in range(slots)]
        here = [value(slot, sweep - 1, low) for slot in range(slots)]
        for k in range(low, sweep):
            i = k + SWEEPS
            below = face[i] if k < 0 else first if k == 0 else coef[side, FACE + k]
            if k < sweep - 1:
                above = face[i + 1] if k < -1 else first_inside if k == -1 else coef[side, FACE + k + 1]
                c = centre[i] if k <= 0 else coef[side, CENTRE + k]
                e, w = (east[i], west[i]) if k < 0 else (coef[side, EAST + k], coef[side, WEST + k])
            for slot in range(slots):
                after = None
                if k < sweep - 1:
                    after = value(slot, sweep - 1, k + 1)
                    result = sideways(c, e, w, here[slot]) + above * after + below * before[slot]
                elif k == 0:
                    result = kept[side, slot, PART] + below * (before[slot] - here[slot])
                else:
                    result = kept[side, slot, PART + sweep - 1] + below * before[slot]
                if sweep == SWEEPS:
                    place = half_row(odd, k if side == OUTER else 2 * SWEEPS - 1 - k)
                    weights[slot, place] = result.astype(weights.dtype)
                else:
                    field[sweep - 1, slot, i] = result
                before[slot], here[slot] = here[slot], after


def side_kernel(side, controls, packet, kept, coef, halves, *refs):
    odd = parity()
    slots = controls.shape[0]
    inside = None
    if side == OUTER:
        tile, tiles = lax.axis_index("tile"), lax.axis_size("tile")
        edge = jnp.where(odd == 1, tile == tiles - 1, tile == 0)
        inside = jnp.where(edge, 0.0, 1.0).astype(jnp.float32)
    side_rows(
        side,
        odd,
        controls,
        lambda slot, k: decode(packet, slots, slot, -1 - k),
        lambda k: kappa_of(decode_codes(packet, slots, -1 - k), halves[0], halves[1]),
        inside,
        kept,
        coef,
        *refs,
    )


def products(pert, weight, total):
    return [
        term if old is None else old + term
        for old, term in zip(total, [p.astype(jnp.float32) * weight for p in pert])
    ]


def own_kernel(factor, pert, owner, inner, outer, near_part, far_part, near_others, far_others, sems):
    odd = parity()
    count, here = lax.axis_size("tm"), lax.axis_index("tm")
    slots, variables = inner.shape[0], pert.shape[1]

    def member(step, slot):
        return owner[lax.rem(here - step + count, count) * slots + slot]

    copies = []
    for step in range(1, count):
        for slot in range(slots):
            place = (step - 1) * slots + slot
            for side, (start, others) in enumerate(
                ((inner_start(odd), near_others), (outer_start(odd), far_others))
            ):
                copies.append(
                    pltpu.make_async_copy(
                        pert.at[member(step, slot), :, pl.ds(start, SWEEPS)],
                        others.at[place],
                        sems.at[2 * place + side],
                    )
                )
    for copy in copies:
        copy.start()
    for start, weights, part in (
        (inner_start(odd), inner, near_part),
        (outer_start(odd), outer, far_part),
    ):
        for row in range(SWEEPS):
            total = [None] * variables
            for slot in range(slots):
                weight = weights[slot, row].astype(jnp.float32) * factor
                who = member(0, slot)
                total = products([pert[who, v, start + row] for v in range(variables)], weight, total)
            for v in range(variables):
                part[v, row] = total[v]
    for copy in copies:
        copy.wait()


def add_others(factor, part, others, arrived, row):
    variables = part.shape[0]
    total = [part[v, row] for v in range(variables)]
    for index, weights in enumerate(arrived):
        slots = weights.shape[0]
        for slot in range(slots):
            weight = weights[slot, row].astype(jnp.float32) * factor
            place = index * slots + slot
            total = products([others[place, v, row] for v in range(variables)], weight, total)
    return total


def add_and_write(factor, start, part, others, arrived, out, ready, sems):
    for row in range(SWEEPS):
        for v, total in enumerate(add_others(factor, part, others, arrived, row)):
            ready[v, row] = total
    writes = [
        pltpu.make_async_copy(ready.at[v], out.at[v, pl.ds(start, SWEEPS)], sems.at[v])
        for v in range(part.shape[0])
    ]
    for copy in writes:
        copy.start()
    for copy in writes:
        copy.wait()


def near_kernel(factor, part, others, *refs):
    *arrived, out, ready, sems = refs
    add_and_write(factor, inner_start(parity()), part, others, arrived, out, ready, sems)


def far_kernel(factor, part, others, *refs):
    *arrived, _, out, ready, sems = refs
    add_and_write(factor, outer_start(parity()), part, others, arrived, out, ready, sems)


def cost(flops, moved):
    return pl.CostEstimate(flops=flops, bytes_accessed=moved, transcendentals=0)


def near(value):
    return pltpu.with_memory_space_constraint(value, pltpu.VMEM)


def far(value):
    return pltpu.with_memory_space_constraint(value, pltpu.HBM)


def on_device(controls, perturbations, owner, land_mask, diffusivity):
    slots, height, levels, columns = controls.shape
    members, variables = perturbations.shape[1:3]
    count = lax.axis_size("tm")
    factor = 1.0 / math.sqrt(owner.shape[0] - 1)
    row = (levels, columns)
    f32, bf16 = jnp.float32, jnp.bfloat16
    dma = pltpu.SemaphoreType.DMA

    packet = pltpu.VMEM((4 * word_count(slots) + 1, levels, columns // 4), jnp.int32)
    mine = near(controls)
    my_across, codes, table = pl.pallas_call(
        pack_kernel,
        out_shape=(packet, pltpu.VMEM((height, columns), jnp.int32), pltpu.VMEM((2, levels), f32)),
        in_specs=[ANY, ANY, ANY],
        out_specs=(VMEM, VMEM, VMEM),
        scratch_shapes=[pltpu.VMEM((slots, SWEEPS, *row), f32), dma((2 * slots + 2,))],
        compiler_params=PARAMS,
        name="pack",
    )(far(controls), far(land_mask), far(diffusivity))
    across = swap_across(my_across)
    my_within = pl.pallas_call(
        within_kernel,
        out_shape=packet,
        in_specs=[VMEM, VMEM],
        out_specs=VMEM,
        compiler_params=PARAMS,
        cost_estimate=cost(1, 1),
        name="pack_within",
    )(mine, near(codes))
    within = swap_within(my_within)

    kept, coef, halves = pl.pallas_call(
        middle_kernel,
        out_shape=(
            pltpu.VMEM((2, slots, KEPT, *row), f32),
            pltpu.VMEM((2, COEFS, *row), f32),
            pltpu.VMEM((2, *row), f32),
        ),
        in_specs=[VMEM] * 3,
        out_specs=(VMEM,) * 3,
        scratch_shapes=[pltpu.VMEM((height, *row), f32)] * 4
        + [pltpu.VMEM((SWEEPS - 1, slots, height, *row), f32)],
        compiler_params=PARAMS,
        cost_estimate=cost(1, 1),
        name="middle",
    )(mine, near(codes), near(table))
    shared = (near(kept), near(coef), near(halves))

    def side(which, arrived, name):
        return pl.pallas_call(
            functools.partial(side_kernel, which),
            out_shape=pltpu.VMEM((slots, SWEEPS, *row), bf16),
            in_specs=[VMEM] * 5,
            out_specs=VMEM,
            scratch_shapes=[pltpu.VMEM((SWEEPS + 1, *row), f32)] * 4
            + [pltpu.VMEM((SWEEPS - 1, slots, 2 * SWEEPS, *row), f32)],
            compiler_params=PARAMS,
            cost_estimate=cost(1, 1),
            name=name,
        )(mine, near(arrived), *shared)

    inner = side(INNER, within, "inner_rows")

    def shift(value):
        return [
            near(lax.ppermute(value, "tm", [(i, (i + step) % count) for i in range(count)]))
            for step in range(1, count)
        ]

    inner_arrived = shift(inner)
    outer = side(OUTER, across, "outer_rows")
    outer_arrived = shift(outer)

    arrivals = count - 1
    part = pltpu.VMEM((variables, SWEEPS, *row), f32)
    others = pltpu.VMEM((max(arrivals, 1) * slots, variables, SWEEPS, *row), bf16)
    near_part, far_part, near_others, far_others = pl.pallas_call(
        lambda *refs: own_kernel(factor, *refs),
        out_shape=(part, part, others, others),
        in_specs=[VMEM, SMEM, VMEM, VMEM],
        out_specs=(VMEM,) * 4,
        scratch_shapes=[dma((2 * max(arrivals, 1) * slots,))],
        compiler_params=PARAMS,
        cost_estimate=cost(4_000_000, 2_000_000),
        name="own_products",
    )(near(perturbations[0]), owner, near(inner), near(outer))
    result = jax.ShapeDtypeStruct((variables, height, *row), f32)
    scratch = [pltpu.VMEM((variables, SWEEPS, *row), f32), dma((variables,))]
    out = pl.pallas_call(
        lambda *refs: near_kernel(factor, *refs),
        out_shape=result,
        in_specs=[VMEM] * (2 + arrivals),
        out_specs=ANY,
        scratch_shapes=scratch,
        compiler_params=PARAMS,
        cost_estimate=cost(1_000_000, 1_000_000),
        name="near_products",
    )(near(near_part), near(near_others), *inner_arrived)
    out = pl.pallas_call(
        lambda *refs: far_kernel(factor, *refs),
        out_shape=result,
        in_specs=[VMEM] * (2 + arrivals) + [ANY],
        out_specs=ANY,
        scratch_shapes=scratch,
        input_output_aliases={2 + arrivals: 0},
        compiler_params=PARAMS,
        cost_estimate=cost(1_000_000, 1_000_000),
        name="far_products",
    )(near(far_part), near(far_others), *outer_arrived, out)
    return out[None]


def solution(mesh):
    return jax.shard_map(
        on_device,
        mesh=mesh,
        in_specs=(
            P("tm", "tile", None, None),
            P("tm", None, None, "tile", None, None),
            P(),
            P("tile", None),
            P(),
        ),
        out_specs=P("tm", None, "tile", None, None),
        check_vma=False,
    )
```

```python
import functools
import math

import jax
import jax.numpy as jnp
from jax import lax
from jax.experimental import pallas as pl
from jax.experimental.pallas import tpu as pltpu
from jax.sharding import PartitionSpec as P

SWEEPS = 4
VMEM = pl.BlockSpec(memory_space=pltpu.VMEM)
SMEM = pl.BlockSpec(memory_space=pltpu.SMEM)
ANY = pl.BlockSpec(memory_space=pl.ANY)
PARAMS = pltpu.CompilerParams(vmem_limit_bytes=16 * 1024 * 1024)


def parity():
    return lax.rem(lax.axis_index("tile"), 2)


def own_row(odd, j):
    return j + odd * (2 * SWEEPS - 1 - 2 * j)


OUTER, INNER = 0, 1


def row_of(side, odd, k):
    return own_row(odd, k if side == OUTER else 2 * SWEEPS - 1 - k)


def half_row(odd, j):
    return j % SWEEPS + odd * (SWEEPS - 1 - 2 * (j % SWEEPS))


def outer_start(odd):
    return SWEEPS * odd


def inner_start(odd):
    return SWEEPS * (1 - odd)


def swap_within(value):
    pairs = [(i, i + 1) for i in range(0, lax.axis_size("tile"), 2)]
    return lax.ppermute(value, "tile", pairs + [(b, a) for a, b in pairs])


def swap_across(value):
    tiles, times = lax.axis_size("tile"), lax.axis_size("tm")
    pairs = [((i, t), (i + 1, t)) for i in range(1, tiles - 1, 2) for t in range(times)]
    pairs += [((i, t), (i, t + 1)) for i in (0, tiles - 1) for t in range(0, times, 2)]
    flat = [(a * times + t, b * times + u) for (a, t), (b, u) in pairs]
    return lax.ppermute(value, ("tile", "tm"), flat + [(b, a) for a, b in flat])


FRACTION = (20, 18, 14, 12)


def to_fixed(value, bits):
    return jnp.round(value * float(2**bits)).astype(jnp.int32) + (8 << bits)


def from_fixed(value, bits):
    return (value - (8 << bits)).astype(jnp.float32) * float(0.5**bits)


def word_count(slots):
    return 2 * slots + (slots + 1) // 2


def encode(slots, read, code, packet):
    words, last = [], []
    for slot in range(slots):
        one, two, three, four = (to_fixed(read(slot, k), FRACTION[k]) for k in range(SWEEPS))
        words += [one | (two << 24), (two >> 8) | (three << 14)]
        last.append(four)
    words += [sum(value << (16 * i) for i, value in enumerate(last[at : at + 2])) for at in range(0, slots, 2)]
    width = packet.shape[2]
    parts = words[0].shape[1] // width
    for index, word in enumerate(words):
        for part in range(parts):
            packet[index * parts + part] = word[:, part * width : (part + 1) * width]
    for k in range(SWEEPS):
        value = code(k)
        for part in range(parts // 2):
            low = value[:, part * width : (part + 1) * width]
            high = value[:, (part + parts // 2) * width : (part + parts // 2 + 1) * width]
            packet[len(words) * parts, pl.ds(k * (parts // 2) + part, 1), :] = low | (high << 16)


def decode(packet, slots, slot, k):
    count = word_count(slots)
    parts = (packet.shape[0] - 1) // count

    def word(index):
        return jnp.concatenate([packet[index * parts + part] for part in range(parts)], axis=1)

    def right(value, bits):
        return lax.shift_right_logical(value, jnp.int32(bits))

    if k == 0:
        value = word(2 * slot) & 0xFFFFFF
    elif k == 1:
        value = right(word(2 * slot), 24) | ((word(2 * slot + 1) & 0x3FFF) << 8)
    elif k == 2:
        value = right(word(2 * slot + 1), 14)
    else:
        value = word(2 * slots + slot // 2)
        value = right(value, 16) if slot % 2 else value & 0xFFFF
    return from_fixed(value, FRACTION[k])


def decode_codes(packet, slots, k):
    count = word_count(slots)
    half = (packet.shape[0] - 1) // count // 2
    words = [packet[packet.shape[0] - 1, pl.ds(k * half + part, 1), :] for part in range(half)]
    return jnp.concatenate([word & 0xFFFF for word in words] + [word >> 16 for word in words], axis=1)


def pack_kernel(controls, mask, diffusivity, across, within, mine, codes, table, sems):
    odd = parity()
    slots = controls.shape[0]
    copies = [
        pltpu.make_async_copy(mask, codes, sems.at[0]),
        pltpu.make_async_copy(diffusivity, table, sems.at[1]),
    ]
    for start in (outer_start(odd), inner_start(odd)):
        for slot in range(slots):
            for part in range(2):
                rows = pl.ds(start + SWEEPS // 2 * part, SWEEPS // 2)
                copies.append(
                    pltpu.make_async_copy(controls.at[slot, rows], mine.at[slot, rows], sems.at[len(copies)])
                )
    own, outer, inner = copies[:2], copies[2 : 2 + 2 * slots], copies[2 + 2 * slots :]
    for copy in outer + own + inner:
        copy.start()
    for side, packet, arriving in ((OUTER, across, outer + own), (INNER, within, inner)):
        for copy in arriving:
            copy.wait()
        encode(
            slots,
            lambda slot, k, side=side: mine[slot, row_of(side, odd, k)],
            lambda k, side=side: codes[pl.ds(row_of(side, odd, k), 1), :] + 1,
            packet,
        )


def by_level(table, kind, shape):
    level = lax.broadcasted_iota(jnp.int32, shape, 0)
    value = jnp.broadcast_to(table[kind : kind + 1, 0:1], shape)
    for index in range(1, shape[0]):
        value = jnp.where(level == index, table[kind : kind + 1, index : index + 1], value)
    return value


def kappa_of(code, sea, land):
    return jnp.where(jnp.broadcast_to(code, sea.shape) == 2, land, sea)


def along_row(kappa):
    columns = kappa.shape[1]
    lane = lax.broadcasted_iota(jnp.int32, kappa.shape, 1)
    last = lane == columns - 1
    loss = kappa + jnp.where(last, 0.0, pltpu.roll(kappa, columns - 1, 1))
    east = jnp.where(last, 0.0, loss)
    west = pltpu.roll(east, 1, 1)
    return east, west, loss + jnp.where(lane == 0, kappa, west)


def sideways(centre, east, west, here):
    columns = here.shape[1]
    return centre * here + east * pltpu.roll(here, columns - 1, 1) + west * pltpu.roll(here, 1, 1)


FACE, EAST, WEST, CENTRE, KAPPA, COEFS = 0, 4, 8, 12, 16, 17
PART, VALUE, KEPT = 0, SWEEPS, 2 * SWEEPS - 1


def middle_kernel(controls, codes, table, kept, coef, halves, face, centre, east, west, field):
    odd = parity()
    slots, _, levels, columns = controls.shape
    shape = (levels, columns)
    total = 2 * SWEEPS
    for kind in range(2):
        halves[kind] = 0.5 * by_level(table, kind, shape)
    sea, land = halves[0], halves[1]

    previous = lost = None
    for j in range(total):
        kappa = kappa_of(codes[pl.ds(own_row(odd, j), 1), :] + 1, sea, land)
        e, w, loss = along_row(kappa)
        east[j], west[j] = e, w
        if j:
            face[j] = previous + kappa
            centre[j - 1] = 1.0 - (lost + face[j])
            lost = loss + face[j]
        else:
            lost = loss
        previous = kappa
        for side, k in ((OUTER, j), (INNER, total - 1 - j)):
            if k == 0:
                coef[side, KAPPA] = kappa
            if k < SWEEPS:
                coef[side, EAST + k], coef[side, WEST + k] = e, w
    centre[total - 1] = 1.0 - lost
    for k in range(SWEEPS):
        coef[OUTER, CENTRE + k], coef[INNER, CENTRE + k] = centre[k], centre[total - 1 - k]
        if k:
            coef[OUTER, FACE + k], coef[INNER, FACE + k] = face[k], face[total - k]

    def value(slot, sweep, j):
        return field[sweep - 1, slot, j] if sweep else controls[slot, own_row(odd, j)]

    for sweep in range(1, SWEEPS + 1):
        low, high = sweep - 1, total - sweep
        before = [None] * slots
        here = [value(slot, sweep - 1, low) for slot in range(slots)]
        for j in range(low, high + 1):
            c, e, w = centre[j], east[j], west[j]
            below = face[j] if j > low else None
            above = face[j + 1] if j < high else None
            for slot in range(slots):
                after = None
                result = sideways(c, e, w, here[slot])
                if above is not None:
                    after = value(slot, sweep - 1, j + 1)
                    result = result + above * after
                if below is not None:
                    result = result + below * before[slot]
                if j == low:
                    kept[OUTER, slot, PART + sweep - 1] = result
                elif j == high:
                    kept[INNER, slot, PART + sweep - 1] = result
                else:
                    field[sweep - 1, slot, j] = result
                    if j == low + 1:
                        kept[OUTER, slot, VALUE + sweep - 1] = result
                    if j == high - 1:
                        kept[INNER, slot, VALUE + sweep - 1] = result
                before[slot], here[slot] = here[slot], after


def side_rows(side, odd, controls, far, far_kappa, inside, kept, coef, weights, face, centre, east, west, field):
    slots = controls.shape[0]

    def masked(value):
        return value if inside is None else value * inside

    previous = masked(far_kappa(-SWEEPS))
    lost = None
    for k in range(1 - SWEEPS, 1):
        i = k + SWEEPS
        kappa = masked(far_kappa(k)) if k else coef[side, KAPPA]
        step = previous + kappa
        face[i] = step
        if lost is not None:
            centre[i - 1] = 1.0 - (lost + step)
        if k:
            e, w, loss = along_row(kappa)
            east[i], west[i] = e, w
            lost = loss + step
        else:
            centre[i] = coef[side, CENTRE] - step
        previous = kappa
    first = face[SWEEPS]
    first_inside = masked(first)

    def value(slot, sweep, k):
        if sweep == 0:
            return masked(far(slot, k)) if k < 0 else controls[slot, row_of(side, odd, k)]
        if k == sweep:
            return kept[side, slot, VALUE + sweep - 1]
        return field[sweep - 1, slot, k + SWEEPS]

    for sweep in range(1, SWEEPS + 1):
        low = sweep - SWEEPS
        before = [value(slot, sweep - 1, low - 1) for slot in range(slots)]
        here = [value(slot, sweep - 1, low) for slot in range(slots)]
        for k in range(low, sweep):
            i = k + SWEEPS
            below = face[i] if k < 0 else first if k == 0 else coef[side, FACE + k]
            if k < sweep - 1:
                above = face[i + 1] if k < -1 else first_inside if k == -1 else coef[side, FACE + k + 1]
                c = centre[i] if k <= 0 else coef[side, CENTRE + k]
                e, w = (east[i], west[i]) if k < 0 else (coef[side, EAST + k], coef[side, WEST + k])
            for slot in range(slots):
                after = None
                if k < sweep - 1:
                    after = value(slot, sweep - 1, k + 1)
                    result = sideways(c, e, w, here[slot]) + above * after + below * before[slot]
                elif k == 0:
                    result = kept[side, slot, PART] + below * (before[slot] - here[slot])
                else:
                    result = kept[side, slot, PART + sweep - 1] + below * before[slot]
                if sweep == SWEEPS:
                    place = half_row(odd, k if side == OUTER else 2 * SWEEPS - 1 - k)
                    weights[slot, place] = result.astype(weights.dtype)
                else:
                    field[sweep - 1, slot, i] = result
                before[slot], here[slot] = here[slot], after


def side_kernel(side, controls, packet, kept, coef, halves, *refs):
    odd = parity()
    slots = controls.shape[0]
    inside = None
    if side == OUTER:
        tile, tiles = lax.axis_index("tile"), lax.axis_size("tile")
        edge = jnp.where(odd == 1, tile == tiles - 1, tile == 0)
        inside = jnp.where(edge, 0.0, 1.0).astype(jnp.float32)
    side_rows(
        side,
        odd,
        controls,
        lambda slot, k: decode(packet, slots, slot, -1 - k),
        lambda k: kappa_of(decode_codes(packet, slots, -1 - k), halves[0], halves[1]),
        inside,
        kept,
        coef,
        *refs,
    )


def products(pert, weight, total):
    return [
        term if old is None else old + term
        for old, term in zip(total, [p.astype(jnp.float32) * weight for p in pert])
    ]


def own_kernel(factor, pert, owner, inner, outer, near_part, far_part, near_others, far_others, sems):
    odd = parity()
    count, here = lax.axis_size("tm"), lax.axis_index("tm")
    slots, variables = inner.shape[0], pert.shape[1]

    def member(step, slot):
        return owner[lax.rem(here - step + count, count) * slots + slot]

    copies = []
    for step in range(1, count):
        for slot in range(slots):
            place = (step - 1) * slots + slot
            for side, (start, others) in enumerate(
                ((inner_start(odd), near_others), (outer_start(odd), far_others))
            ):
                copies.append(
                    pltpu.make_async_copy(
                        pert.at[member(step, slot), :, pl.ds(start, SWEEPS)],
                        others.at[place],
                        sems.at[2 * place + side],
                    )
                )
    for copy in copies:
        copy.start()
    for start, weights, part in (
        (inner_start(odd), inner, near_part),
        (outer_start(odd), outer, far_part),
    ):
        for row in range(SWEEPS):
            total = [None] * variables
            for slot in range(slots):
                weight = weights[slot, row].astype(jnp.float32) * factor
                who = member(0, slot)
                total = products([pert[who, v, start + row] for v in range(variables)], weight, total)
            for v in range(variables):
                part[v, row] = total[v]
    for copy in copies:
        copy.wait()


def add_others(factor, part, others, arrived, row):
    variables = part.shape[0]
    total = [part[v, row] for v in range(variables)]
    for index, weights in enumerate(arrived):
        slots = weights.shape[0]
        for slot in range(slots):
            weight = weights[slot, row].astype(jnp.float32) * factor
            place = index * slots + slot
            total = products([others[place, v, row] for v in range(variables)], weight, total)
    return total


def add_and_write(factor, start, part, others, arrived, out, ready, sems):
    for row in range(SWEEPS):
        for v, total in enumerate(add_others(factor, part, others, arrived, row)):
            ready[v, row] = total
    writes = [
        pltpu.make_async_copy(ready.at[v], out.at[v, pl.ds(start, SWEEPS)], sems.at[v])
        for v in range(part.shape[0])
    ]
    for copy in writes:
        copy.start()
    for copy in writes:
        copy.wait()


def near_kernel(factor, part, others, *refs):
    *arrived, out, ready, sems = refs
    add_and_write(factor, inner_start(parity()), part, others, arrived, out, ready, sems)


def far_kernel(factor, part, others, *refs):
    *arrived, _, out, ready, sems = refs
    add_and_write(factor, outer_start(parity()), part, others, arrived, out, ready, sems)


def cost(flops, moved):
    return pl.CostEstimate(flops=flops, bytes_accessed=moved, transcendentals=0)


def near(value):
    return pltpu.with_memory_space_constraint(value, pltpu.VMEM)


def far(value):
    return pltpu.with_memory_space_constraint(value, pltpu.HBM)


def on_device(controls, perturbations, owner, land_mask, diffusivity):
    slots, height, levels, columns = controls.shape
    members, variables = perturbations.shape[1:3]
    count = lax.axis_size("tm")
    factor = 1.0 / math.sqrt(owner.shape[0] - 1)
    row = (levels, columns)
    f32, bf16 = jnp.float32, jnp.bfloat16
    dma = pltpu.SemaphoreType.DMA

    packet = pltpu.VMEM((4 * word_count(slots) + 1, levels, columns // 4), jnp.int32)
    my_across, my_within, mine, codes, table = pl.pallas_call(
        pack_kernel,
        out_shape=(
            packet,
            packet,
            pltpu.VMEM(controls.shape, f32),
            pltpu.VMEM((height, columns), jnp.int32),
            pltpu.VMEM((2, levels), f32),
        ),
        in_specs=[ANY, ANY, ANY],
        out_specs=(VMEM,) * 5,
        scratch_shapes=[dma((2 * 2 * slots + 2,))],
        compiler_params=PARAMS,
        name="pack",
    )(far(controls), far(land_mask), far(diffusivity))
    across = swap_across(my_across)
    within = swap_within(my_within)
    mine = near(mine)

    kept, coef, halves = pl.pallas_call(
        middle_kernel,
        out_shape=(
            pltpu.VMEM((2, slots, KEPT, *row), f32),
            pltpu.VMEM((2, COEFS, *row), f32),
            pltpu.VMEM((2, *row), f32),
        ),
        in_specs=[VMEM] * 3,
        out_specs=(VMEM,) * 3,
        scratch_shapes=[pltpu.VMEM((height, *row), f32)] * 4
        + [pltpu.VMEM((SWEEPS - 1, slots, height, *row), f32)],
        compiler_params=PARAMS,
        cost_estimate=cost(1, 1),
        name="middle",
    )(mine, near(codes), near(table))
    shared = (near(kept), near(coef), near(halves))

    def side(which, arrived, name):
        return pl.pallas_call(
            functools.partial(side_kernel, which),
            out_shape=pltpu.VMEM((slots, SWEEPS, *row), bf16),
            in_specs=[VMEM] * 5,
            out_specs=VMEM,
            scratch_shapes=[pltpu.VMEM((SWEEPS + 1, *row), f32)] * 4
            + [pltpu.VMEM((SWEEPS - 1, slots, 2 * SWEEPS, *row), f32)],
            compiler_params=PARAMS,
            cost_estimate=cost(1, 1),
            name=name,
        )(mine, near(arrived), *shared)

    inner = side(INNER, within, "inner_rows")

    def shift(value):
        return [
            near(lax.ppermute(value, "tm", [(i, (i + step) % count) for i in range(count)]))
            for step in range(1, count)
        ]

    inner_arrived = shift(inner)
    outer = side(OUTER, across, "outer_rows")
    outer_arrived = shift(outer)

    arrivals = count - 1
    part = pltpu.VMEM((variables, SWEEPS, *row), f32)
    others = pltpu.VMEM((max(arrivals, 1) * slots, variables, SWEEPS, *row), bf16)
    near_part, far_part, near_others, far_others = pl.pallas_call(
        lambda *refs: own_kernel(factor, *refs),
        out_shape=(part, part, others, others),
        in_specs=[VMEM, SMEM, VMEM, VMEM],
        out_specs=(VMEM,) * 4,
        scratch_shapes=[dma((2 * max(arrivals, 1) * slots,))],
        compiler_params=PARAMS,
        cost_estimate=cost(4_000_000, 2_000_000),
        name="own_products",
    )(near(perturbations[0]), owner, near(inner), near(outer))
    result = jax.ShapeDtypeStruct((variables, height, *row), f32)
    scratch = [pltpu.VMEM((variables, SWEEPS, *row), f32), dma((variables,))]
    out = pl.pallas_call(
        lambda *refs: near_kernel(factor, *refs),
        out_shape=result,
        in_specs=[VMEM] * (2 + arrivals),
        out_specs=ANY,
        scratch_shapes=scratch,
        compiler_params=PARAMS,
        cost_estimate=cost(1_000_000, 1_000_000),
        name="near_products",
    )(near(near_part), near(near_others), *inner_arrived)
    out = pl.pallas_call(
        lambda *refs: far_kernel(factor, *refs),
        out_shape=result,
        in_specs=[VMEM] * (2 + arrivals) + [ANY],
        out_specs=ANY,
        scratch_shapes=scratch,
        input_output_aliases={2 + arrivals: 0},
        compiler_params=PARAMS,
        cost_estimate=cost(1_000_000, 1_000_000),
        name="far_products",
    )(near(far_part), near(far_others), *outer_arrived, out)
    return out[None]


def solution(mesh):
    return jax.shard_map(
        on_device,
        mesh=mesh,
        in_specs=(
            P("tm", "tile", None, None),
            P("tm", None, None, "tile", None, None),
            P(),
            P("tile", None),
            P(),
        ),
        out_specs=P("tm", None, "tile", None, None),
        check_vma=False,
    )
```

```python
import functools
import math

import jax
import jax.numpy as jnp
from jax import lax
from jax.experimental import pallas as pl
from jax.experimental.pallas import tpu as pltpu
from jax.sharding import PartitionSpec as P

SWEEPS = 4
VMEM = pl.BlockSpec(memory_space=pltpu.VMEM)
SMEM = pl.BlockSpec(memory_space=pltpu.SMEM)
ANY = pl.BlockSpec(memory_space=pl.ANY)
PARAMS = pltpu.CompilerParams(vmem_limit_bytes=16 * 1024 * 1024)


def parity():
    return lax.rem(lax.axis_index("tile"), 2)


def own_row(odd, j):
    return j + odd * (2 * SWEEPS - 1 - 2 * j)


OUTER, INNER = 0, 1


def row_of(side, odd, k):
    return own_row(odd, k if side == OUTER else 2 * SWEEPS - 1 - k)


def half_row(odd, j):
    return j % SWEEPS + odd * (SWEEPS - 1 - 2 * (j % SWEEPS))


def outer_start(odd):
    return SWEEPS * odd


def inner_start(odd):
    return SWEEPS * (1 - odd)


def swap_within(value):
    pairs = [(i, i + 1) for i in range(0, lax.axis_size("tile"), 2)]
    return lax.ppermute(value, "tile", pairs + [(b, a) for a, b in pairs])


def swap_across(value):
    tiles, times = lax.axis_size("tile"), lax.axis_size("tm")
    pairs = [((i, t), (i + 1, t)) for i in range(1, tiles - 1, 2) for t in range(times)]
    pairs += [((i, t), (i, t + 1)) for i in (0, tiles - 1) for t in range(0, times, 2)]
    flat = [(a * times + t, b * times + u) for (a, t), (b, u) in pairs]
    return lax.ppermute(value, ("tile", "tm"), flat + [(b, a) for a, b in flat])


FRACTION = (16, 16, 12, 12)


def to_fixed(value, bits):
    return jnp.round(value * float(2**bits)).astype(jnp.int32) + (8 << bits)


def from_fixed(value, bits):
    return (value - (8 << bits)).astype(jnp.float32) * float(0.5**bits)


QUARTERS = 4
PAIR_UNITS = 2 * QUARTERS + QUARTERS // 2


def unit_count(slots):
    return QUARTERS * slots + PAIR_UNITS * ((slots + 1) // 2) + 1


def encode(slots, read, code, packet):
    width = packet.shape[2]

    def quarters(value):
        return [value[:, part * width : (part + 1) * width] for part in range(QUARTERS)]

    def halves_together(value):
        parts = quarters(value)
        return [low | (high << 16) for low, high in zip(parts[: QUARTERS // 2], parts[QUARTERS // 2 :])]

    units, pairs = [], []
    for slot in range(slots):
        one, two, three, four = (to_fixed(read(slot, k), FRACTION[k]) for k in range(SWEEPS))
        units += quarters(one | (two << 20))
        rest = two >> 12
        if slot % 2:
            before = pairs.pop()
            pairs.append((before[0] | (three << 16), before[1] | (four << 16), before[2] | (rest << 8)))
        else:
            pairs.append((three, four, rest))
    for three, four, rest in pairs:
        units += quarters(three) + quarters(four) + halves_together(rest)
    for index, unit in enumerate(units):
        packet[index] = unit
    for k in range(SWEEPS):
        for part, unit in enumerate(halves_together(code(k))):
            packet[len(units), pl.ds(k * (QUARTERS // 2) + part, 1), :] = unit


def decode(packet, slots, slot, k):
    base = QUARTERS * slots + PAIR_UNITS * (slot // 2)

    def words(start, count=QUARTERS):
        return jnp.concatenate([packet[start + part] for part in range(count)], axis=1)

    def right(value, bits):
        return lax.shift_right_logical(value, jnp.int32(bits))

    if k == 0:
        value = words(QUARTERS * slot) & 0xFFFFF
    elif k == 1:
        folded = words(base + 2 * QUARTERS, QUARTERS // 2)
        rest = jnp.concatenate([folded, right(folded, 16)], axis=1)
        rest = right(rest, 8) & 0xFF if slot % 2 else rest & 0xFF
        value = right(words(QUARTERS * slot), 20) | (rest << 12)
    else:
        value = words(base + QUARTERS * (k - 2))
        value = right(value, 16) if slot % 2 else value & 0xFFFF
    return from_fixed(value, FRACTION[k])


def decode_codes(packet, slots, k):
    half = QUARTERS // 2
    words = [packet[unit_count(slots) - 1, pl.ds(k * half + part, 1), :] for part in range(half)]
    return jnp.concatenate([word & 0xFFFF for word in words] + [word >> 16 for word in words], axis=1)


def pack_kernel(controls, mask, diffusivity, across, within, mine, codes, table, sems):
    odd = parity()
    slots = controls.shape[0]
    copies = [
        pltpu.make_async_copy(mask, codes, sems.at[0]),
        pltpu.make_async_copy(diffusivity, table, sems.at[1]),
    ]
    for start in (outer_start(odd), inner_start(odd)):
        for slot in range(slots):
            for part in range(2):
                rows = pl.ds(start + SWEEPS // 2 * part, SWEEPS // 2)
                copies.append(
                    pltpu.make_async_copy(controls.at[slot, rows], mine.at[slot, rows], sems.at[len(copies)])
                )
    own, outer, inner = copies[:2], copies[2 : 2 + 2 * slots], copies[2 + 2 * slots :]
    for copy in outer + own + inner:
        copy.start()
    for side, packet, arriving in ((OUTER, across, outer + own), (INNER, within, inner)):
        for copy in arriving:
            copy.wait()
        encode(
            slots,
            lambda slot, k, side=side: mine[slot, row_of(side, odd, k)],
            lambda k, side=side: codes[pl.ds(row_of(side, odd, k), 1), :] + 1,
            packet,
        )


def by_level(table, kind, shape):
    level = lax.broadcasted_iota(jnp.int32, shape, 0)
    value = jnp.broadcast_to(table[kind : kind + 1, 0:1], shape)
    for index in range(1, shape[0]):
        value = jnp.where(level == index, table[kind : kind + 1, index : index + 1], value)
    return value


def kappa_of(code, sea, land):
    return jnp.where(jnp.broadcast_to(code, sea.shape) == 2, land, sea)


def along_row(kappa):
    columns = kappa.shape[1]
    lane = lax.broadcasted_iota(jnp.int32, kappa.shape, 1)
    last = lane == columns - 1
    loss = kappa + jnp.where(last, 0.0, pltpu.roll(kappa, columns - 1, 1))
    east = jnp.where(last, 0.0, loss)
    west = pltpu.roll(east, 1, 1)
    return east, west, loss + jnp.where(lane == 0, kappa, west)


def sideways(centre, east, west, here):
    columns = here.shape[1]
    return centre * here + east * pltpu.roll(here, columns - 1, 1) + west * pltpu.roll(here, 1, 1)


FACE, EAST, WEST, CENTRE, KAPPA, COEFS = 0, 4, 8, 12, 16, 17
PART, VALUE, KEPT = 0, SWEEPS, 2 * SWEEPS - 1


def middle_kernel(controls, codes, table, kept, coef, halves, face, centre, east, west, field):
    odd = parity()
    slots, _, levels, columns = controls.shape
    shape = (levels, columns)
    total = 2 * SWEEPS
    for kind in range(2):
        halves[kind] = 0.5 * by_level(table, kind, shape)
    sea, land = halves[0], halves[1]

    previous = lost = None
    for j in range(total):
        kappa = kappa_of(codes[pl.ds(own_row(odd, j), 1), :] + 1, sea, land)
        e, w, loss = along_row(kappa)
        east[j], west[j] = e, w
        if j:
            face[j] = previous + kappa
            centre[j - 1] = 1.0 - (lost + face[j])
            lost = loss + face[j]
        else:
            lost = loss
        previous = kappa
        for side, k in ((OUTER, j), (INNER, total - 1 - j)):
            if k == 0:
                coef[side, KAPPA] = kappa
            if k < SWEEPS:
                coef[side, EAST + k], coef[side, WEST + k] = e, w
    centre[total - 1] = 1.0 - lost
    for k in range(SWEEPS):
        coef[OUTER, CENTRE + k], coef[INNER, CENTRE + k] = centre[k], centre[total - 1 - k]
        if k:
            coef[OUTER, FACE + k], coef[INNER, FACE + k] = face[k], face[total - k]

    def value(slot, sweep, j):
        return field[sweep - 1, slot, j] if sweep else controls[slot, own_row(odd, j)]

    for sweep in range(1, SWEEPS + 1):
        low, high = sweep - 1, total - sweep
        before = [None] * slots
        here = [value(slot, sweep - 1, low) for slot in range(slots)]
        for j in range(low, high + 1):
            c, e, w = centre[j], east[j], west[j]
            below = face[j] if j > low else None
            above = face[j + 1] if j < high else None
            for slot in range(slots):
                after = None
                result = sideways(c, e, w, here[slot])
                if above is not None:
                    after = value(slot, sweep - 1, j + 1)
                    result = result + above * after
                if below is not None:
                    result = result + below * before[slot]
                if j == low:
                    kept[OUTER, slot, PART + sweep - 1] = result
                elif j == high:
                    kept[INNER, slot, PART + sweep - 1] = result
                else:
                    field[sweep - 1, slot, j] = result
                    if j == low + 1:
                        kept[OUTER, slot, VALUE + sweep - 1] = result
                    if j == high - 1:
                        kept[INNER, slot, VALUE + sweep - 1] = result
                before[slot], here[slot] = here[slot], after


def side_rows(side, odd, controls, far, far_kappa, inside, kept, coef, weights, face, centre, east, west, field):
    slots = controls.shape[0]

    def masked(value):
        return value if inside is None else value * inside

    previous = masked(far_kappa(-SWEEPS))
    lost = None
    for k in range(1 - SWEEPS, 1):
        i = k + SWEEPS
        kappa = masked(far_kappa(k)) if k else coef[side, KAPPA]
        step = previous + kappa
        face[i] = step
        if lost is not None:
            centre[i - 1] = 1.0 - (lost + step)
        if k:
            e, w, loss = along_row(kappa)
            east[i], west[i] = e, w
            lost = loss + step
        else:
            centre[i] = coef[side, CENTRE] - step
        previous = kappa
    first = face[SWEEPS]
    first_inside = masked(first)

    def value(slot, sweep, k):
        if sweep == 0:
            return masked(far(slot, k)) if k < 0 else controls[slot, row_of(side, odd, k)]
        if k == sweep:
            return kept[side, slot, VALUE + sweep - 1]
        return field[sweep - 1, slot, k + SWEEPS]

    for sweep in range(1, SWEEPS + 1):
        low = sweep - SWEEPS
        before = [value(slot, sweep - 1, low - 1) for slot in range(slots)]
        here = [value(slot, sweep - 1, low) for slot in range(slots)]
        for k in range(low, sweep):
            i = k + SWEEPS
            below = face[i] if k < 0 else first if k == 0 else coef[side, FACE + k]
            if k < sweep - 1:
                above = face[i + 1] if k < -1 else first_inside if k == -1 else coef[side, FACE + k + 1]
                c = centre[i] if k <= 0 else coef[side, CENTRE + k]
                e, w = (east[i], west[i]) if k < 0 else (coef[side, EAST + k], coef[side, WEST + k])
            for slot in range(slots):
                after = None
                if k < sweep - 1:
                    after = value(slot, sweep - 1, k + 1)
                    result = sideways(c, e, w, here[slot]) + above * after + below * before[slot]
                elif k == 0:
                    result = kept[side, slot, PART] + below * (before[slot] - here[slot])
                else:
                    result = kept[side, slot, PART + sweep - 1] + below * before[slot]
                if sweep == SWEEPS:
                    place = half_row(odd, k if side == OUTER else 2 * SWEEPS - 1 - k)
                    weights[slot, place] = result.astype(weights.dtype)
                else:
                    field[sweep - 1, slot, i] = result
                before[slot], here[slot] = here[slot], after


def side_kernel(side, controls, packet, kept, coef, halves, *refs):
    odd = parity()
    slots = controls.shape[0]
    inside = None
    if side == OUTER:
        tile, tiles = lax.axis_index("tile"), lax.axis_size("tile")
        edge = jnp.where(odd == 1, tile == tiles - 1, tile == 0)
        inside = jnp.where(edge, 0.0, 1.0).astype(jnp.float32)
    side_rows(
        side,
        odd,
        controls,
        lambda slot, k: decode(packet, slots, slot, -1 - k),
        lambda k: kappa_of(decode_codes(packet, slots, -1 - k), halves[0], halves[1]),
        inside,
        kept,
        coef,
        *refs,
    )


def products(pert, weight, total):
    return [
        term if old is None else old + term
        for old, term in zip(total, [p.astype(jnp.float32) * weight for p in pert])
    ]


def own_kernel(factor, pert, owner, inner, outer, near_part, far_part, near_others, far_others, sems):
    odd = parity()
    count, here = lax.axis_size("tm"), lax.axis_index("tm")
    slots, variables = inner.shape[0], pert.shape[1]

    def member(step, slot):
        return owner[lax.rem(here - step + count, count) * slots + slot]

    copies = []
    for step in range(1, count):
        for slot in range(slots):
            place = (step - 1) * slots + slot
            for side, (start, others) in enumerate(
                ((inner_start(odd), near_others), (outer_start(odd), far_others))
            ):
                copies.append(
                    pltpu.make_async_copy(
                        pert.at[member(step, slot), :, pl.ds(start, SWEEPS)],
                        others.at[place],
                        sems.at[2 * place + side],
                    )
                )
    for copy in copies:
        copy.start()
    for start, weights, part in (
        (inner_start(odd), inner, near_part),
        (outer_start(odd), outer, far_part),
    ):
        for row in range(SWEEPS):
            total = [None] * variables
            for slot in range(slots):
                weight = weights[slot, row].astype(jnp.float32) * factor
                who = member(0, slot)
                total = products([pert[who, v, start + row] for v in range(variables)], weight, total)
            for v in range(variables):
                part[v, row] = total[v]
    for copy in copies:
        copy.wait()


def add_others(factor, part, others, arrived, row):
    variables = part.shape[0]
    total = [part[v, row] for v in range(variables)]
    for index, weights in enumerate(arrived):
        slots = weights.shape[0]
        for slot in range(slots):
            weight = weights[slot, row].astype(jnp.float32) * factor
            place = index * slots + slot
            total = products([others[place, v, row] for v in range(variables)], weight, total)
    return total


def add_and_write(factor, start, part, others, arrived, out, ready, sems):
    for row in range(SWEEPS):
        for v, total in enumerate(add_others(factor, part, others, arrived, row)):
            ready[v, row] = total
    writes = [
        pltpu.make_async_copy(ready.at[v], out.at[v, pl.ds(start, SWEEPS)], sems.at[v])
        for v in range(part.shape[0])
    ]
    for copy in writes:
        copy.start()
    for copy in writes:
        copy.wait()


def near_kernel(factor, part, others, *refs):
    *arrived, out, ready, sems = refs
    add_and_write(factor, inner_start(parity()), part, others, arrived, out, ready, sems)


def far_kernel(factor, part, others, *refs):
    *arrived, _, out, ready, sems = refs
    add_and_write(factor, outer_start(parity()), part, others, arrived, out, ready, sems)


def cost(flops, moved):
    return pl.CostEstimate(flops=flops, bytes_accessed=moved, transcendentals=0)


def near(value):
    return pltpu.with_memory_space_constraint(value, pltpu.VMEM)


def far(value):
    return pltpu.with_memory_space_constraint(value, pltpu.HBM)


def on_device(controls, perturbations, owner, land_mask, diffusivity):
    slots, height, levels, columns = controls.shape
    members, variables = perturbations.shape[1:3]
    count = lax.axis_size("tm")
    factor = 1.0 / math.sqrt(owner.shape[0] - 1)
    row = (levels, columns)
    f32, bf16 = jnp.float32, jnp.bfloat16
    dma = pltpu.SemaphoreType.DMA

    packet = pltpu.VMEM((unit_count(slots), levels, columns // QUARTERS), jnp.int32)
    my_across, my_within, mine, codes, table = pl.pallas_call(
        pack_kernel,
        out_shape=(
            packet,
            packet,
            pltpu.VMEM(controls.shape, f32),
            pltpu.VMEM((height, columns), jnp.int32),
            pltpu.VMEM((2, levels), f32),
        ),
        in_specs=[ANY, ANY, ANY],
        out_specs=(VMEM,) * 5,
        scratch_shapes=[dma((2 * 2 * slots + 2,))],
        compiler_params=PARAMS,
        name="pack",
    )(far(controls), far(land_mask), far(diffusivity))
    across = swap_across(my_across)
    within = swap_within(my_within)
    mine = near(mine)

    kept, coef, halves = pl.pallas_call(
        middle_kernel,
        out_shape=(
            pltpu.VMEM((2, slots, KEPT, *row), f32),
            pltpu.VMEM((2, COEFS, *row), f32),
            pltpu.VMEM((2, *row), f32),
        ),
        in_specs=[VMEM] * 3,
        out_specs=(VMEM,) * 3,
        scratch_shapes=[pltpu.VMEM((height, *row), f32)] * 4
        + [pltpu.VMEM((SWEEPS - 1, slots, height, *row), f32)],
        compiler_params=PARAMS,
        cost_estimate=cost(1, 1),
        name="middle",
    )(mine, near(codes), near(table))
    shared = (near(kept), near(coef), near(halves))

    def side(which, arrived, name):
        return pl.pallas_call(
            functools.partial(side_kernel, which),
            out_shape=pltpu.VMEM((slots, SWEEPS, *row), bf16),
            in_specs=[VMEM] * 5,
            out_specs=VMEM,
            scratch_shapes=[pltpu.VMEM((SWEEPS + 1, *row), f32)] * 4
            + [pltpu.VMEM((SWEEPS - 1, slots, 2 * SWEEPS, *row), f32)],
            compiler_params=PARAMS,
            cost_estimate=cost(1, 1),
            name=name,
        )(mine, near(arrived), *shared)

    inner = side(INNER, within, "inner_rows")

    def shift(value):
        return [
            near(lax.ppermute(value, "tm", [(i, (i + step) % count) for i in range(count)]))
            for step in range(1, count)
        ]

    inner_arrived = shift(inner)
    outer = side(OUTER, across, "outer_rows")
    outer_arrived = shift(outer)

    arrivals = count - 1
    part = pltpu.VMEM((variables, SWEEPS, *row), f32)
    others = pltpu.VMEM((max(arrivals, 1) * slots, variables, SWEEPS, *row), bf16)
    near_part, far_part, near_others, far_others = pl.pallas_call(
        lambda *refs: own_kernel(factor, *refs),
        out_shape=(part, part, others, others),
        in_specs=[VMEM, SMEM, VMEM, VMEM],
        out_specs=(VMEM,) * 4,
        scratch_shapes=[dma((2 * max(arrivals, 1) * slots,))],
        compiler_params=PARAMS,
        cost_estimate=cost(4_000_000, 2_000_000),
        name="own_products",
    )(near(perturbations[0]), owner, near(inner), near(outer))
    result = jax.ShapeDtypeStruct((variables, height, *row), f32)
    scratch = [pltpu.VMEM((variables, SWEEPS, *row), f32), dma((variables,))]
    out = pl.pallas_call(
        lambda *refs: near_kernel(factor, *refs),
        out_shape=result,
        in_specs=[VMEM] * (2 + arrivals),
        out_specs=ANY,
        scratch_shapes=scratch,
        compiler_params=PARAMS,
        cost_estimate=cost(1_000_000, 1_000_000),
        name="near_products",
    )(near(near_part), near(near_others), *inner_arrived)
    out = pl.pallas_call(
        lambda *refs: far_kernel(factor, *refs),
        out_shape=result,
        in_specs=[VMEM] * (2 + arrivals) + [ANY],
        out_specs=ANY,
        scratch_shapes=scratch,
        input_output_aliases={2 + arrivals: 0},
        compiler_params=PARAMS,
        cost_estimate=cost(1_000_000, 1_000_000),
        name="far_products",
    )(near(far_part), near(far_others), *outer_arrived, out)
    return out[None]


def solution(mesh):
    return jax.shard_map(
        on_device,
        mesh=mesh,
        in_specs=(
            P("tm", "tile", None, None),
            P("tm", None, None, "tile", None, None),
            P(),
            P("tile", None),
            P(),
        ),
        out_specs=P("tm", None, "tile", None, None),
        check_vma=False,
    )
```

```python
import functools
import math

import jax
import jax.numpy as jnp
from jax import lax
from jax.experimental import pallas as pl
from jax.experimental.pallas import tpu as pltpu
from jax.sharding import PartitionSpec as P

SWEEPS = 4
VMEM = pl.BlockSpec(memory_space=pltpu.VMEM)
SMEM = pl.BlockSpec(memory_space=pltpu.SMEM)
ANY = pl.BlockSpec(memory_space=pl.ANY)
PARAMS = pltpu.CompilerParams(vmem_limit_bytes=16 * 1024 * 1024)


def parity():
    return lax.rem(lax.axis_index("tile"), 2)


def own_row(odd, j):
    return j + odd * (2 * SWEEPS - 1 - 2 * j)


OUTER, INNER = 0, 1


def row_of(side, odd, k):
    return own_row(odd, k if side == OUTER else 2 * SWEEPS - 1 - k)


def half_row(odd, j):
    return j % SWEEPS + odd * (SWEEPS - 1 - 2 * (j % SWEEPS))


def outer_start(odd):
    return SWEEPS * odd


def inner_start(odd):
    return SWEEPS * (1 - odd)


def swap_within(value):
    pairs = [(i, i + 1) for i in range(0, lax.axis_size("tile"), 2)]
    return lax.ppermute(value, "tile", pairs + [(b, a) for a, b in pairs])


def swap_across(value):
    tiles, times = lax.axis_size("tile"), lax.axis_size("tm")
    pairs = [((i, t), (i + 1, t)) for i in range(1, tiles - 1, 2) for t in range(times)]
    pairs += [((i, t), (i, t + 1)) for i in (0, tiles - 1) for t in range(0, times, 2)]
    flat = [(a * times + t, b * times + u) for (a, t), (b, u) in pairs]
    return lax.ppermute(value, ("tile", "tm"), flat + [(b, a) for a, b in flat])


FRACTION = (16, 16, 12, 12)


def to_fixed(value, bits):
    return jnp.round(value * float(2**bits)).astype(jnp.int32) + (8 << bits)


def from_fixed(value, bits):
    return (value - (8 << bits)).astype(jnp.float32) * float(0.5**bits)


QUARTERS = 4
PAIR_UNITS = 2 * QUARTERS + QUARTERS // 2


def unit_count(slots):
    return QUARTERS * slots + PAIR_UNITS * ((slots + 1) // 2) + 1


def encode(slots, read, code, packet):
    width = packet.shape[2]

    def quarters(value):
        return [value[:, part * width : (part + 1) * width] for part in range(QUARTERS)]

    def halves_together(value):
        parts = quarters(value)
        return [low | (high << 16) for low, high in zip(parts[: QUARTERS // 2], parts[QUARTERS // 2 :])]

    units, pairs = [], []
    for slot in range(slots):
        one, two, three, four = (to_fixed(read(slot, k), FRACTION[k]) for k in range(SWEEPS))
        units += quarters(one | (two << 20))
        rest = two >> 12
        if slot % 2:
            before = pairs.pop()
            pairs.append((before[0] | (three << 16), before[1] | (four << 16), before[2] | (rest << 8)))
        else:
            pairs.append((three, four, rest))
    for three, four, rest in pairs:
        units += quarters(three) + quarters(four) + halves_together(rest)
    for index, unit in enumerate(units):
        packet[index] = unit
    for k in range(SWEEPS):
        for part, unit in enumerate(halves_together(code(k))):
            packet[len(units), pl.ds(k * (QUARTERS // 2) + part, 1), :] = unit


def decode(packet, slots, slot, k):
    base = QUARTERS * slots + PAIR_UNITS * (slot // 2)

    def words(start, count=QUARTERS):
        return jnp.concatenate([packet[start + part] for part in range(count)], axis=1)

    def right(value, bits):
        return lax.shift_right_logical(value, jnp.int32(bits))

    if k == 0:
        value = words(QUARTERS * slot) & 0xFFFFF
    elif k == 1:
        folded = words(base + 2 * QUARTERS, QUARTERS // 2)
        rest = jnp.concatenate([folded, right(folded, 16)], axis=1)
        rest = right(rest, 8) & 0xFF if slot % 2 else rest & 0xFF
        value = right(words(QUARTERS * slot), 20) | (rest << 12)
    else:
        value = words(base + QUARTERS * (k - 2))
        value = right(value, 16) if slot % 2 else value & 0xFFFF
    return from_fixed(value, FRACTION[k])


def decode_codes(packet, slots, k):
    half = QUARTERS // 2
    words = [packet[unit_count(slots) - 1, pl.ds(k * half + part, 1), :] for part in range(half)]
    return jnp.concatenate([word & 0xFFFF for word in words] + [word >> 16 for word in words], axis=1)


def pack_kernel(controls, mask, diffusivity, across, within, mine, codes, table, sems):
    odd = parity()
    slots = controls.shape[0]
    copies = [
        pltpu.make_async_copy(mask, codes, sems.at[0]),
        pltpu.make_async_copy(diffusivity, table, sems.at[1]),
    ]
    for start in (outer_start(odd), inner_start(odd)):
        for slot in range(slots):
            for part in range(2):
                rows = pl.ds(start + SWEEPS // 2 * part, SWEEPS // 2)
                copies.append(
                    pltpu.make_async_copy(controls.at[slot, rows], mine.at[slot, rows], sems.at[len(copies)])
                )
    own, outer, inner = copies[:2], copies[2 : 2 + 2 * slots], copies[2 + 2 * slots :]
    for copy in outer + own + inner:
        copy.start()

    def read(side, arriving, slot, k):
        if k == 0:
            for copy in arriving[2 * slot : 2 * slot + 2]:
                copy.wait()
        return mine[slot, row_of(side, odd, k)]

    def code(side, k):
        if side == OUTER and k == 0:
            for copy in own:
                copy.wait()
        return codes[pl.ds(row_of(side, odd, k), 1), :] + 1

    for side, packet, arriving in ((OUTER, across, outer), (INNER, within, inner)):
        encode(slots, functools.partial(read, side, arriving), functools.partial(code, side), packet)


def by_level(table, kind, shape):
    levels = shape[0]
    square = jnp.broadcast_to(table[kind : kind + 1, :], (levels, levels))
    diagonal = lax.broadcasted_iota(jnp.int32, square.shape, 0) == lax.broadcasted_iota(jnp.int32, square.shape, 1)
    return jnp.broadcast_to(jnp.sum(jnp.where(diagonal, square, 0.0), axis=1, keepdims=True), shape)


def kappa_of(code, sea, land):
    return jnp.where(jnp.broadcast_to(code, sea.shape) == 2, land, sea)


def along_row(kappa):
    columns = kappa.shape[1]
    lane = lax.broadcasted_iota(jnp.int32, kappa.shape, 1)
    last = lane == columns - 1
    loss = kappa + jnp.where(last, 0.0, pltpu.roll(kappa, columns - 1, 1))
    east = jnp.where(last, 0.0, loss)
    west = pltpu.roll(east, 1, 1)
    return east, west, loss + jnp.where(lane == 0, kappa, west)


def sideways(centre, east, west, here):
    columns = here.shape[1]
    return centre * here + east * pltpu.roll(here, columns - 1, 1) + west * pltpu.roll(here, 1, 1)


FACE, EAST, WEST, CENTRE, KAPPA, COEFS = 0, 4, 8, 12, 16, 17
PART, VALUE, KEPT = 0, SWEEPS, 2 * SWEEPS - 1


def middle_kernel(controls, codes, table, kept, coef, halves, shifted, face, centre, east, west, field):
    odd = parity()
    slots, _, levels, columns = controls.shape
    shape = (levels, columns)
    total = 2 * SWEEPS
    for kind in range(2):
        halves[kind] = 0.5 * by_level(table, kind, shape)
    sea, land = halves[0], halves[1]

    lane = lax.broadcasted_iota(jnp.int32, shape, 1)
    first_lane, last_lane = lane == 0, lane == columns - 1
    shifted[0] = pltpu.roll(codes[...], columns - 1, 1)
    shifted[1] = pltpu.roll(codes[...], 1, 1)
    previous = lost = None
    for j in range(total):
        place = pl.ds(own_row(odd, j), 1)
        kappa = kappa_of(codes[place, :] + 1, sea, land)
        to_east = kappa + jnp.where(last_lane, 0.0, kappa_of(shifted[0, place, :] + 1, sea, land))
        to_west = kappa + jnp.where(first_lane, 0.0, kappa_of(shifted[1, place, :] + 1, sea, land))
        loss = to_east + to_west
        e, w = jnp.where(last_lane, 0.0, to_east), jnp.where(first_lane, 0.0, to_west)
        east[j], west[j] = e, w
        if j:
            face[j] = previous + kappa
            centre[j - 1] = 1.0 - (lost + face[j])
            lost = loss + face[j]
        else:
            lost = loss
        previous = kappa
        for side, k in ((OUTER, j), (INNER, total - 1 - j)):
            if k == 0:
                coef[side, KAPPA] = kappa
            if k < SWEEPS:
                coef[side, EAST + k], coef[side, WEST + k] = e, w
    centre[total - 1] = 1.0 - lost
    for k in range(SWEEPS):
        coef[OUTER, CENTRE + k], coef[INNER, CENTRE + k] = centre[k], centre[total - 1 - k]
        if k:
            coef[OUTER, FACE + k], coef[INNER, FACE + k] = face[k], face[total - k]

    def value(slot, sweep, j):
        return field[sweep - 1, slot, j] if sweep else controls[slot, own_row(odd, j)]

    for sweep in range(1, SWEEPS + 1):
        low, high = sweep - 1, total - sweep
        before = [None] * slots
        here = [value(slot, sweep - 1, low) for slot in range(slots)]
        for j in range(low, high + 1):
            c, e, w = centre[j], east[j], west[j]
            below = face[j] if j > low else None
            above = face[j + 1] if j < high else None
            for slot in range(slots):
                after = None
                result = sideways(c, e, w, here[slot])
                if above is not None:
                    after = value(slot, sweep - 1, j + 1)
                    result = result + above * after
                if below is not None:
                    result = result + below * before[slot]
                if j == low:
                    kept[OUTER, slot, PART + sweep - 1] = result
                elif j == high:
                    kept[INNER, slot, PART + sweep - 1] = result
                else:
                    field[sweep - 1, slot, j] = result
                    if j == low + 1:
                        kept[OUTER, slot, VALUE + sweep - 1] = result
                    if j == high - 1:
                        kept[INNER, slot, VALUE + sweep - 1] = result
                before[slot], here[slot] = here[slot], after


def side_rows(side, odd, controls, far, far_kappa, inside, kept, coef, weights, face, centre, east, west, field):
    slots = controls.shape[0]

    def masked(value):
        return value if inside is None else value * inside

    previous = masked(far_kappa(-SWEEPS))
    lost = None
    for k in range(1 - SWEEPS, 1):
        i = k + SWEEPS
        kappa = masked(far_kappa(k)) if k else coef[side, KAPPA]
        step = previous + kappa
        face[i] = step
        if lost is not None:
            centre[i - 1] = 1.0 - (lost + step)
        if k:
            e, w, loss = along_row(kappa)
            east[i], west[i] = e, w
            lost = loss + step
        else:
            centre[i] = coef[side, CENTRE] - step
        previous = kappa
    first = face[SWEEPS]
    first_inside = masked(first)

    def value(slot, sweep, k):
        if sweep == 0:
            return masked(far(slot, k)) if k < 0 else controls[slot, row_of(side, odd, k)]
        if k == sweep:
            return kept[side, slot, VALUE + sweep - 1]
        return field[sweep - 1, slot, k + SWEEPS]

    for sweep in range(1, SWEEPS + 1):
        low = sweep - SWEEPS
        before = [value(slot, sweep - 1, low - 1) for slot in range(slots)]
        here = [value(slot, sweep - 1, low) for slot in range(slots)]
        for k in range(low, sweep):
            i = k + SWEEPS
            below = face[i] if k < 0 else first if k == 0 else coef[side, FACE + k]
            if k < sweep - 1:
                above = face[i + 1] if k < -1 else first_inside if k == -1 else coef[side, FACE + k + 1]
                c = centre[i] if k <= 0 else coef[side, CENTRE + k]
                e, w = (east[i], west[i]) if k < 0 else (coef[side, EAST + k], coef[side, WEST + k])
            for slot in range(slots):
                after = None
                if k < sweep - 1:
                    after = value(slot, sweep - 1, k + 1)
                    result = sideways(c, e, w, here[slot]) + above * after + below * before[slot]
                elif k == 0:
                    result = kept[side, slot, PART] + below * (before[slot] - here[slot])
                else:
                    result = kept[side, slot, PART + sweep - 1] + below * before[slot]
                if sweep == SWEEPS:
                    place = half_row(odd, k if side == OUTER else 2 * SWEEPS - 1 - k)
                    weights[slot, place] = result.astype(weights.dtype)
                else:
                    field[sweep - 1, slot, i] = result
                before[slot], here[slot] = here[slot], after


def side_kernel(side, controls, packet, kept, coef, halves, *refs):
    odd = parity()
    slots = controls.shape[0]
    inside = None
    if side == OUTER:
        tile, tiles = lax.axis_index("tile"), lax.axis_size("tile")
        edge = jnp.where(odd == 1, tile == tiles - 1, tile == 0)
        inside = jnp.where(edge, 0.0, 1.0).astype(jnp.float32)
    side_rows(
        side,
        odd,
        controls,
        lambda slot, k: decode(packet, slots, slot, -1 - k),
        lambda k: kappa_of(decode_codes(packet, slots, -1 - k), halves[0], halves[1]),
        inside,
        kept,
        coef,
        *refs,
    )


def products(pert, weight, total):
    return [
        term if old is None else old + term
        for old, term in zip(total, [p.astype(jnp.float32) * weight for p in pert])
    ]


def own_kernel(factor, pert, owner, inner, outer, near_part, far_part, near_others, far_others, sems):
    odd = parity()
    count, here = lax.axis_size("tm"), lax.axis_index("tm")
    slots, variables = inner.shape[0], pert.shape[1]

    def member(step, slot):
        return owner[lax.rem(here - step + count, count) * slots + slot]

    copies = []
    for step in range(1, count):
        for slot in range(slots):
            place = (step - 1) * slots + slot
            for side, (start, others) in enumerate(
                ((inner_start(odd), near_others), (outer_start(odd), far_others))
            ):
                copies.append(
                    pltpu.make_async_copy(
                        pert.at[member(step, slot), :, pl.ds(start, SWEEPS)],
                        others.at[place],
                        sems.at[2 * place + side],
                    )
                )
    for copy in copies:
        copy.start()
    for start, weights, part in (
        (inner_start(odd), inner, near_part),
        (outer_start(odd), outer, far_part),
    ):
        for row in range(SWEEPS):
            total = [None] * variables
            for slot in range(slots):
                weight = weights[slot, row].astype(jnp.float32) * factor
                who = member(0, slot)
                total = products([pert[who, v, start + row] for v in range(variables)], weight, total)
            for v in range(variables):
                part[v, row] = total[v]
    for copy in copies:
        copy.wait()


def add_others(factor, part, others, arrived, row, variables):
    total = [part[v, row] for v in variables]
    for index, weights in enumerate(arrived):
        slots = weights.shape[0]
        for slot in range(slots):
            weight = weights[slot, row].astype(jnp.float32) * factor
            place = index * slots + slot
            total = products([others[place, v, row] for v in variables], weight, total)
    return total


def add_and_write(factor, start, part, others, arrived, out, ready, sems):
    count = part.shape[0]
    half = (count + 1) // 2
    writes = []
    for first in range(0, count, half):
        variables = range(first, min(first + half, count))
        for row in range(SWEEPS):
            for v, total in zip(variables, add_others(factor, part, others, arrived, row, variables)):
                ready[v, row] = total
        for v in variables:
            writes.append(pltpu.make_async_copy(ready.at[v], out.at[v, pl.ds(start, SWEEPS)], sems.at[v]))
            writes[-1].start()
    for copy in writes:
        copy.wait()


def near_kernel(factor, part, others, *refs):
    *arrived, out, ready, sems = refs
    add_and_write(factor, inner_start(parity()), part, others, arrived, out, ready, sems)


def far_kernel(factor, part, others, *refs):
    *arrived, _, out, ready, sems = refs
    add_and_write(factor, outer_start(parity()), part, others, arrived, out, ready, sems)


def cost(flops, moved):
    return pl.CostEstimate(flops=flops, bytes_accessed=moved, transcendentals=0)


def near(value):
    return pltpu.with_memory_space_constraint(value, pltpu.VMEM)


def far(value):
    return pltpu.with_memory_space_constraint(value, pltpu.HBM)


def on_device(controls, perturbations, owner, land_mask, diffusivity):
    slots, height, levels, columns = controls.shape
    members, variables = perturbations.shape[1:3]
    count = lax.axis_size("tm")
    factor = 1.0 / math.sqrt(owner.shape[0] - 1)
    row = (levels, columns)
    f32, bf16 = jnp.float32, jnp.bfloat16
    dma = pltpu.SemaphoreType.DMA

    packet = pltpu.VMEM((unit_count(slots), levels, columns // QUARTERS), jnp.int32)
    my_across, my_within, mine, codes, table = pl.pallas_call(
        pack_kernel,
        out_shape=(
            packet,
            packet,
            pltpu.VMEM(controls.shape, f32),
            pltpu.VMEM((height, columns), jnp.int32),
            pltpu.VMEM((2, levels), f32),
        ),
        in_specs=[ANY, ANY, ANY],
        out_specs=(VMEM,) * 5,
        scratch_shapes=[dma((2 * 2 * slots + 2,))],
        compiler_params=PARAMS,
        name="pack",
    )(far(controls), far(land_mask), far(diffusivity))
    across = swap_across(my_across)
    within = swap_within(my_within)
    mine = near(mine)

    kept, coef, halves = pl.pallas_call(
        middle_kernel,
        out_shape=(
            pltpu.VMEM((2, slots, KEPT, *row), f32),
            pltpu.VMEM((2, COEFS, *row), f32),
            pltpu.VMEM((2, *row), f32),
        ),
        in_specs=[VMEM] * 3,
        out_specs=(VMEM,) * 3,
        scratch_shapes=[pltpu.VMEM((2, height, columns), jnp.int32)]
        + [pltpu.VMEM((height, *row), f32)] * 4
        + [pltpu.VMEM((SWEEPS - 1, slots, height, *row), f32)],
        compiler_params=PARAMS,
        cost_estimate=cost(1, 1),
        name="middle",
    )(mine, near(codes), near(table))
    shared = (near(kept), near(coef), near(halves))

    def side(which, arrived, name):
        return pl.pallas_call(
            functools.partial(side_kernel, which),
            out_shape=pltpu.VMEM((slots, SWEEPS, *row), bf16),
            in_specs=[VMEM] * 5,
            out_specs=VMEM,
            scratch_shapes=[pltpu.VMEM((SWEEPS + 1, *row), f32)] * 4
            + [pltpu.VMEM((SWEEPS - 1, slots, 2 * SWEEPS, *row), f32)],
            compiler_params=PARAMS,
            cost_estimate=cost(1, 1),
            name=name,
        )(mine, near(arrived), *shared)

    inner = side(INNER, within, "inner_rows")

    def shift(value):
        return [
            near(lax.ppermute(value, "tm", [(i, (i + step) % count) for i in range(count)]))
            for step in range(1, count)
        ]

    inner_arrived = shift(inner)
    outer = side(OUTER, across, "outer_rows")
    outer_arrived = shift(outer)

    arrivals = count - 1
    part = pltpu.VMEM((variables, SWEEPS, *row), f32)
    others = pltpu.VMEM((max(arrivals, 1) * slots, variables, SWEEPS, *row), bf16)
    near_part, far_part, near_others, far_others = pl.pallas_call(
        lambda *refs: own_kernel(factor, *refs),
        out_shape=(part, part, others, others),
        in_specs=[VMEM, SMEM, VMEM, VMEM],
        out_specs=(VMEM,) * 4,
        scratch_shapes=[dma((2 * max(arrivals, 1) * slots,))],
        compiler_params=PARAMS,
        cost_estimate=cost(4_000_000, 2_000_000),
        name="own_products",
    )(near(perturbations[0]), owner, near(inner), near(outer))
    result = jax.ShapeDtypeStruct((variables, height, *row), f32)
    scratch = [pltpu.VMEM((variables, SWEEPS, *row), f32), dma((variables,))]
    out = pl.pallas_call(
        lambda *refs: near_kernel(factor, *refs),
        out_shape=result,
        in_specs=[VMEM] * (2 + arrivals),
        out_specs=ANY,
        scratch_shapes=scratch,
        compiler_params=PARAMS,
        cost_estimate=cost(1_000_000, 1_000_000),
        name="near_products",
    )(near(near_part), near(near_others), *inner_arrived)
    out = pl.pallas_call(
        lambda *refs: far_kernel(factor, *refs),
        out_shape=result,
        in_specs=[VMEM] * (2 + arrivals) + [ANY],
        out_specs=ANY,
        scratch_shapes=scratch,
        input_output_aliases={2 + arrivals: 0},
        compiler_params=PARAMS,
        cost_estimate=cost(1_000_000, 1_000_000),
        name="far_products",
    )(near(far_part), near(far_others), *outer_arrived, out)
    return out[None]


def solution(mesh):
    return jax.shard_map(
        on_device,
        mesh=mesh,
        in_specs=(
            P("tm", "tile", None, None),
            P("tm", None, None, "tile", None, None),
            P(),
            P("tile", None),
            P(),
        ),
        out_specs=P("tm", None, "tile", None, None),
        check_vma=False,
    )
```

```python
import functools
import math

import jax
import jax.numpy as jnp
from jax import lax
from jax.experimental import pallas as pl
from jax.experimental.pallas import tpu as pltpu
from jax.sharding import PartitionSpec as P

SWEEPS = 4
VMEM = pl.BlockSpec(memory_space=pltpu.VMEM)
SMEM = pl.BlockSpec(memory_space=pltpu.SMEM)
ANY = pl.BlockSpec(memory_space=pl.ANY)
PARAMS = pltpu.CompilerParams(vmem_limit_bytes=16 * 1024 * 1024)


def parity():
    return lax.rem(lax.axis_index("tile"), 2)


def own_row(odd, j):
    return j + odd * (2 * SWEEPS - 1 - 2 * j)


OUTER, INNER = 0, 1


def row_of(side, odd, k):
    return own_row(odd, k if side == OUTER else 2 * SWEEPS - 1 - k)


def half_row(odd, j):
    return j % SWEEPS + odd * (SWEEPS - 1 - 2 * (j % SWEEPS))


def outer_start(odd):
    return SWEEPS * odd


def inner_start(odd):
    return SWEEPS * (1 - odd)


def swap_within(value):
    pairs = [(i, i + 1) for i in range(0, lax.axis_size("tile"), 2)]
    return lax.ppermute(value, "tile", pairs + [(b, a) for a, b in pairs])


def swap_across(value):
    tiles, times = lax.axis_size("tile"), lax.axis_size("tm")
    pairs = [((i, t), (i + 1, t)) for i in range(1, tiles - 1, 2) for t in range(times)]
    pairs += [((i, t), (i, t + 1)) for i in (0, tiles - 1) for t in range(0, times, 2)]
    flat = [(a * times + t, b * times + u) for (a, t), (b, u) in pairs]
    return lax.ppermute(value, ("tile", "tm"), flat + [(b, a) for a, b in flat])


FRACTION = (16, 16, 12, 12)


def to_fixed(value, bits):
    return jnp.round(value * float(2**bits)).astype(jnp.int32) + (8 << bits)


def from_fixed(value, bits):
    return (value - (8 << bits)).astype(jnp.float32) * float(0.5**bits)


QUARTERS = 4
PAIR_UNITS = 2 * QUARTERS + QUARTERS // 2


def unit_count(slots):
    return QUARTERS * slots + PAIR_UNITS * ((slots + 1) // 2) + 1


def encode(slots, read, code, packet):
    width = packet.shape[2]

    def quarters(value):
        return [value[:, part * width : (part + 1) * width] for part in range(QUARTERS)]

    def halves_together(value):
        parts = quarters(value)
        return [low | (high << 16) for low, high in zip(parts[: QUARTERS // 2], parts[QUARTERS // 2 :])]

    units, pairs = [], []
    for slot in range(slots):
        one, two, three, four = (to_fixed(read(slot, k), FRACTION[k]) for k in range(SWEEPS))
        units += quarters(one | (two << 20))
        rest = two >> 12
        if slot % 2:
            before = pairs.pop()
            pairs.append((before[0] | (three << 16), before[1] | (four << 16), before[2] | (rest << 8)))
        else:
            pairs.append((three, four, rest))
    for three, four, rest in pairs:
        units += quarters(three) + quarters(four) + halves_together(rest)
    for index, unit in enumerate(units):
        packet[index] = unit
    for k in range(SWEEPS):
        for part, unit in enumerate(halves_together(code(k))):
            packet[len(units), pl.ds(k * (QUARTERS // 2) + part, 1), :] = unit


def decode(packet, slots, slot, k):
    base = QUARTERS * slots + PAIR_UNITS * (slot // 2)

    def words(start, count=QUARTERS):
        return jnp.concatenate([packet[start + part] for part in range(count)], axis=1)

    def right(value, bits):
        return lax.shift_right_logical(value, jnp.int32(bits))

    if k == 0:
        value = words(QUARTERS * slot) & 0xFFFFF
    elif k == 1:
        folded = words(base + 2 * QUARTERS, QUARTERS // 2)
        rest = jnp.concatenate([folded, right(folded, 16)], axis=1)
        rest = right(rest, 8) & 0xFF if slot % 2 else rest & 0xFF
        value = right(words(QUARTERS * slot), 20) | (rest << 12)
    else:
        value = words(base + QUARTERS * (k - 2))
        value = right(value, 16) if slot % 2 else value & 0xFFFF
    return from_fixed(value, FRACTION[k])


def decode_codes(packet, slots, k):
    half = QUARTERS // 2
    words = [packet[unit_count(slots) - 1, pl.ds(k * half + part, 1), :] for part in range(half)]
    return jnp.concatenate([word & 0xFFFF for word in words] + [word >> 16 for word in words], axis=1)


def pack_kernel(controls, mask, diffusivity, across, within, mine, codes, table, sems):
    odd = parity()
    slots = controls.shape[0]
    copies = [
        pltpu.make_async_copy(mask, codes, sems.at[0]),
        pltpu.make_async_copy(diffusivity, table, sems.at[1]),
    ]
    for start in (outer_start(odd), inner_start(odd)):
        for slot in range(slots):
            for part in range(2):
                rows = pl.ds(start + SWEEPS // 2 * part, SWEEPS // 2)
                copies.append(
                    pltpu.make_async_copy(controls.at[slot, rows], mine.at[slot, rows], sems.at[len(copies)])
                )
    own, outer, inner = copies[:2], copies[2 : 2 + 2 * slots], copies[2 + 2 * slots :]
    for copy in outer + own + inner:
        copy.start()

    def read(side, arriving, slot, k):
        if k == 0:
            for copy in arriving[2 * slot : 2 * slot + 2]:
                copy.wait()
        return mine[slot, row_of(side, odd, k)]

    def code(side, k):
        if side == OUTER and k == 0:
            for copy in own:
                copy.wait()
        return codes[pl.ds(row_of(side, odd, k), 1), :] + 1

    for side, packet, arriving in ((OUTER, across, outer), (INNER, within, inner)):
        encode(slots, functools.partial(read, side, arriving), functools.partial(code, side), packet)


def by_level(table, kind, shape):
    levels = shape[0]
    square = jnp.broadcast_to(table[kind : kind + 1, :], (levels, levels))
    diagonal = lax.broadcasted_iota(jnp.int32, square.shape, 0) == lax.broadcasted_iota(jnp.int32, square.shape, 1)
    return jnp.broadcast_to(jnp.sum(jnp.where(diagonal, square, 0.0), axis=1, keepdims=True), shape)


def kappa_of(code, sea, land):
    return jnp.where(jnp.broadcast_to(code, sea.shape) == 2, land, sea)


def along_row(kappa):
    columns = kappa.shape[1]
    lane = lax.broadcasted_iota(jnp.int32, kappa.shape, 1)
    last = lane == columns - 1
    loss = kappa + jnp.where(last, 0.0, pltpu.roll(kappa, columns - 1, 1))
    east = jnp.where(last, 0.0, loss)
    west = pltpu.roll(east, 1, 1)
    return east, west, loss + jnp.where(lane == 0, kappa, west)


def sideways(centre, east, west, here):
    columns = here.shape[1]
    return centre * here + east * pltpu.roll(here, columns - 1, 1) + west * pltpu.roll(here, 1, 1)


FACE, EAST, WEST, CENTRE, KAPPA, COEFS = 0, 4, 8, 12, 16, 17
PART, VALUE, KEPT = 0, SWEEPS, 2 * SWEEPS - 1


def middle_kernel(controls, codes, table, kept, coef, halves, shifted, face, centre, east, west, field):
    odd = parity()
    slots, _, levels, columns = controls.shape
    shape = (levels, columns)
    total = 2 * SWEEPS
    for kind in range(2):
        halves[kind] = 0.5 * by_level(table, kind, shape)
    sea, land = halves[0], halves[1]

    lane = lax.broadcasted_iota(jnp.int32, shape, 1)
    first_lane, last_lane = lane == 0, lane == columns - 1
    shifted[0] = pltpu.roll(codes[...], columns - 1, 1)
    shifted[1] = pltpu.roll(codes[...], 1, 1)
    previous = lost = None
    for j in range(total):
        place = pl.ds(own_row(odd, j), 1)
        kappa = kappa_of(codes[place, :] + 1, sea, land)
        to_east = kappa + jnp.where(last_lane, 0.0, kappa_of(shifted[0, place, :] + 1, sea, land))
        to_west = kappa + jnp.where(first_lane, 0.0, kappa_of(shifted[1, place, :] + 1, sea, land))
        loss = to_east + to_west
        e, w = jnp.where(last_lane, 0.0, to_east), jnp.where(first_lane, 0.0, to_west)
        east[j], west[j] = e, w
        if j:
            face[j] = previous + kappa
            centre[j - 1] = 1.0 - (lost + face[j])
            lost = loss + face[j]
        else:
            lost = loss
        previous = kappa
        for side, k in ((OUTER, j), (INNER, total - 1 - j)):
            if k == 0:
                coef[side, KAPPA] = kappa
            if k < SWEEPS:
                coef[side, EAST + k], coef[side, WEST + k] = e, w
    centre[total - 1] = 1.0 - lost
    for k in range(SWEEPS):
        coef[OUTER, CENTRE + k], coef[INNER, CENTRE + k] = centre[k], centre[total - 1 - k]
        if k:
            coef[OUTER, FACE + k], coef[INNER, FACE + k] = face[k], face[total - k]

    def value(slot, sweep, j):
        return field[sweep - 1, slot, j] if sweep else controls[slot, own_row(odd, j)]

    for sweep in range(1, SWEEPS + 1):
        low, high = sweep - 1, total - sweep
        before = [None] * slots
        here = [value(slot, sweep - 1, low) for slot in range(slots)]
        for j in range(low, high + 1):
            c, e, w = centre[j], east[j], west[j]
            below = face[j] if j > low else None
            above = face[j + 1] if j < high else None
            for slot in range(slots):
                after = None
                result = sideways(c, e, w, here[slot])
                if above is not None:
                    after = value(slot, sweep - 1, j + 1)
                    result = result + above * after
                if below is not None:
                    result = result + below * before[slot]
                if j == low:
                    kept[OUTER, slot, PART + sweep - 1] = result
                elif j == high:
                    kept[INNER, slot, PART + sweep - 1] = result
                else:
                    field[sweep - 1, slot, j] = result
                    if j == low + 1:
                        kept[OUTER, slot, VALUE + sweep - 1] = result
                    if j == high - 1:
                        kept[INNER, slot, VALUE + sweep - 1] = result
                before[slot], here[slot] = here[slot], after


def edge_here(odd):
    tile, tiles = lax.axis_index("tile"), lax.axis_size("tile")
    return jnp.where(odd == 1, tile == tiles - 1, tile == 0)


def side_rows(side, odd, controls, neighbour, kept, coef, weights, face, centre, east, west, field):
    slots = controls.shape[0]
    if neighbour is None:
        face[SWEEPS] = coef[side, KAPPA]
    else:
        far, far_kappa = neighbour
        previous = far_kappa(-SWEEPS)
        lost = None
        for k in range(1 - SWEEPS, 1):
            i = k + SWEEPS
            kappa = far_kappa(k) if k else coef[side, KAPPA]
            step = previous + kappa
            face[i] = step
            if lost is not None:
                centre[i - 1] = 1.0 - (lost + step)
            if k:
                e, w, loss = along_row(kappa)
                east[i], west[i] = e, w
                lost = loss + step
            previous = kappa
    centre[SWEEPS] = coef[side, CENTRE] - face[SWEEPS]

    def value(slot, sweep, k):
        if sweep == 0:
            return far(slot, k) if k < 0 else controls[slot, row_of(side, odd, k)]
        if k == sweep:
            return kept[side, slot, VALUE + sweep - 1]
        return field[sweep - 1, slot, k + SWEEPS]

    for sweep in range(1, SWEEPS + 1):
        low = 0 if neighbour is None else sweep - SWEEPS
        before = [None if neighbour is None else value(slot, sweep - 1, low - 1) for slot in range(slots)]
        here = [value(slot, sweep - 1, low) for slot in range(slots)]
        for k in range(low, sweep):
            i = k + SWEEPS
            below = face[i] if k <= 0 else coef[side, FACE + k]
            if k < sweep - 1:
                above = face[i + 1] if k < 0 else coef[side, FACE + k + 1]
                c = centre[i] if k <= 0 else coef[side, CENTRE + k]
                e, w = (east[i], west[i]) if k < 0 else (coef[side, EAST + k], coef[side, WEST + k])
            for slot in range(slots):
                after = None
                if k < sweep - 1:
                    after = value(slot, sweep - 1, k + 1)
                    result = sideways(c, e, w, here[slot]) + above * after
                    if before[slot] is not None:
                        result = result + below * before[slot]
                else:
                    result = kept[side, slot, PART + sweep - 1]
                    if before[slot] is not None:
                        result = result + below * before[slot]
                    if k == 0:
                        result = result - below * here[slot]
                if sweep == SWEEPS:
                    place = half_row(odd, k if side == OUTER else 2 * SWEEPS - 1 - k)
                    weights[slot, place] = result.astype(weights.dtype)
                else:
                    field[sweep - 1, slot, i] = result
                before[slot], here[slot] = here[slot], after


def neighbour_of(packet, slots, halves):
    return (
        lambda slot, k: decode(packet, slots, slot, -1 - k),
        lambda k: kappa_of(decode_codes(packet, slots, -1 - k), halves[0], halves[1]),
    )


def inner_kernel(controls, packet, kept, coef, halves, weights, *scratch):
    neighbour = neighbour_of(packet, controls.shape[0], halves)
    side_rows(INNER, parity(), controls, neighbour, kept, coef, weights, *scratch)


def outer_kernel(controls, packet, kept, coef, halves, weights, *scratch):
    odd = parity()
    edge = edge_here(odd)

    @pl.when(edge)
    def _():
        side_rows(OUTER, odd, controls, None, kept, coef, weights, *scratch)

    @pl.when(jnp.logical_not(edge))
    def _():
        neighbour = neighbour_of(packet, controls.shape[0], halves)
        side_rows(OUTER, odd, controls, neighbour, kept, coef, weights, *scratch)


def products(pert, weight, total):
    return [
        term if old is None else old + term
        for old, term in zip(total, [p.astype(jnp.float32) * weight for p in pert])
    ]


def own_kernel(factor, pert, owner, inner, outer, near_part, far_part, near_others, far_others, sems):
    odd = parity()
    count, here = lax.axis_size("tm"), lax.axis_index("tm")
    slots, variables = inner.shape[0], pert.shape[1]

    def member(step, slot):
        return owner[lax.rem(here - step + count, count) * slots + slot]

    copies = []
    for step in range(1, count):
        for slot in range(slots):
            place = (step - 1) * slots + slot
            for side, (start, others) in enumerate(
                ((inner_start(odd), near_others), (outer_start(odd), far_others))
            ):
                copies.append(
                    pltpu.make_async_copy(
                        pert.at[member(step, slot), :, pl.ds(start, SWEEPS)],
                        others.at[place],
                        sems.at[2 * place + side],
                    )
                )
    for copy in copies:
        copy.start()
    for start, weights, part in (
        (inner_start(odd), inner, near_part),
        (outer_start(odd), outer, far_part),
    ):
        for row in range(SWEEPS):
            total = [None] * variables
            for slot in range(slots):
                weight = weights[slot, row].astype(jnp.float32) * factor
                who = member(0, slot)
                total = products([pert[who, v, start + row] for v in range(variables)], weight, total)
            for v in range(variables):
                part[v, row] = total[v]
    for copy in copies:
        copy.wait()


def add_others(factor, part, others, arrived, row, variables):
    total = [part[v, row] for v in variables]
    for index, weights in enumerate(arrived):
        slots = weights.shape[0]
        for slot in range(slots):
            weight = weights[slot, row].astype(jnp.float32) * factor
            place = index * slots + slot
            total = products([others[place, v, row] for v in variables], weight, total)
    return total


def add_and_write(factor, start, part, others, arrived, out, ready, sems):
    count = part.shape[0]
    half = (count + 1) // 2
    writes = []
    for first in range(0, count, half):
        variables = range(first, min(first + half, count))
        for row in range(SWEEPS):
            for v, total in zip(variables, add_others(factor, part, others, arrived, row, variables)):
                ready[v, row] = total
        for v in variables:
            writes.append(pltpu.make_async_copy(ready.at[v], out.at[v, pl.ds(start, SWEEPS)], sems.at[v]))
            writes[-1].start()
    for copy in writes:
        copy.wait()


def near_kernel(factor, part, others, *refs):
    *arrived, out, ready, sems = refs
    add_and_write(factor, inner_start(parity()), part, others, arrived, out, ready, sems)


def far_kernel(factor, part, others, *refs):
    *arrived, _, out, ready, sems = refs
    add_and_write(factor, outer_start(parity()), part, others, arrived, out, ready, sems)


def cost(flops, moved):
    return pl.CostEstimate(flops=flops, bytes_accessed=moved, transcendentals=0)


def near(value):
    return pltpu.with_memory_space_constraint(value, pltpu.VMEM)


def far(value):
    return pltpu.with_memory_space_constraint(value, pltpu.HBM)


def on_device(controls, perturbations, owner, land_mask, diffusivity):
    slots, height, levels, columns = controls.shape
    members, variables = perturbations.shape[1:3]
    count = lax.axis_size("tm")
    factor = 1.0 / math.sqrt(owner.shape[0] - 1)
    row = (levels, columns)
    f32, bf16 = jnp.float32, jnp.bfloat16
    dma = pltpu.SemaphoreType.DMA

    packet = pltpu.VMEM((unit_count(slots), levels, columns // QUARTERS), jnp.int32)
    my_across, my_within, mine, codes, table = pl.pallas_call(
        pack_kernel,
        out_shape=(
            packet,
            packet,
            pltpu.VMEM(controls.shape, f32),
            pltpu.VMEM((height, columns), jnp.int32),
            pltpu.VMEM((2, levels), f32),
        ),
        in_specs=[ANY, ANY, ANY],
        out_specs=(VMEM,) * 5,
        scratch_shapes=[dma((2 * 2 * slots + 2,))],
        compiler_params=PARAMS,
        name="pack",
    )(far(controls), far(land_mask), far(diffusivity))
    across = swap_across(my_across)
    within = swap_within(my_within)
    mine = near(mine)

    half = pltpu.VMEM((slots, SWEEPS, *row), bf16)
    middle_scratch = [pltpu.VMEM((2, height, columns), jnp.int32)]
    middle_scratch += [pltpu.VMEM((height, *row), f32)] * 4
    middle_scratch += [pltpu.VMEM((SWEEPS - 1, slots, height, *row), f32)]
    kept, coef, halves = pl.pallas_call(
        middle_kernel,
        out_shape=(
            pltpu.VMEM((2, slots, KEPT, *row), f32),
            pltpu.VMEM((2, COEFS, *row), f32),
            pltpu.VMEM((2, *row), f32),
        ),
        in_specs=[VMEM] * 3,
        out_specs=(VMEM,) * 3,
        scratch_shapes=middle_scratch,
        compiler_params=PARAMS,
        cost_estimate=cost(1, 1),
        name="middle",
    )(mine, near(codes), near(table))
    shared = (near(kept), near(coef), near(halves))

    def side(kernel, name, *operands):
        return pl.pallas_call(
            kernel,
            out_shape=half,
            in_specs=[VMEM] * len(operands),
            out_specs=VMEM,
            scratch_shapes=[pltpu.VMEM((SWEEPS + 1, *row), f32)] * 4
            + [pltpu.VMEM((SWEEPS - 1, slots, 2 * SWEEPS, *row), f32)],
            compiler_params=PARAMS,
            cost_estimate=cost(1, 1),
            name=name,
        )(*operands)

    inner = side(inner_kernel, "inner_rows", mine, near(within), *shared)

    def shift(value):
        return [
            near(lax.ppermute(value, "tm", [(i, (i + step) % count) for i in range(count)]))
            for step in range(1, count)
        ]

    inner_arrived = shift(inner)
    outer = side(outer_kernel, "outer_rows", mine, near(across), *shared)
    outer_arrived = shift(outer)

    arrivals = count - 1
    part = pltpu.VMEM((variables, SWEEPS, *row), f32)
    others = pltpu.VMEM((max(arrivals, 1) * slots, variables, SWEEPS, *row), bf16)
    near_part, far_part, near_others, far_others = pl.pallas_call(
        lambda *refs: own_kernel(factor, *refs),
        out_shape=(part, part, others, others),
        in_specs=[VMEM, SMEM, VMEM, VMEM],
        out_specs=(VMEM,) * 4,
        scratch_shapes=[dma((2 * max(arrivals, 1) * slots,))],
        compiler_params=PARAMS,
        cost_estimate=cost(4_000_000, 2_000_000),
        name="own_products",
    )(near(perturbations[0]), owner, near(inner), near(outer))
    result = jax.ShapeDtypeStruct((variables, height, *row), f32)
    scratch = [pltpu.VMEM((variables, SWEEPS, *row), f32), dma((variables,))]
    out = pl.pallas_call(
        lambda *refs: near_kernel(factor, *refs),
        out_shape=result,
        in_specs=[VMEM] * (2 + arrivals),
        out_specs=ANY,
        scratch_shapes=scratch,
        compiler_params=PARAMS,
        cost_estimate=cost(1_000_000, 1_000_000),
        name="near_products",
    )(near(near_part), near(near_others), *inner_arrived)
    out = pl.pallas_call(
        lambda *refs: far_kernel(factor, *refs),
        out_shape=result,
        in_specs=[VMEM] * (2 + arrivals) + [ANY],
        out_specs=ANY,
        scratch_shapes=scratch,
        input_output_aliases={2 + arrivals: 0},
        compiler_params=PARAMS,
        cost_estimate=cost(1_000_000, 1_000_000),
        name="far_products",
    )(near(far_part), near(far_others), *outer_arrived, out)
    return out[None]


def solution(mesh):
    return jax.shard_map(
        on_device,
        mesh=mesh,
        in_specs=(
            P("tm", "tile", None, None),
            P("tm", None, None, "tile", None, None),
            P(),
            P("tile", None),
            P(),
        ),
        out_specs=P("tm", None, "tile", None, None),
        check_vma=False,
    )
```

```python
import functools
import math

import jax
import jax.numpy as jnp
from jax import lax
from jax.experimental import pallas as pl
from jax.experimental.pallas import tpu as pltpu
from jax.sharding import PartitionSpec as P

SWEEPS = 4
VMEM = pl.BlockSpec(memory_space=pltpu.VMEM)
SMEM = pl.BlockSpec(memory_space=pltpu.SMEM)
ANY = pl.BlockSpec(memory_space=pl.ANY)
PARAMS = pltpu.CompilerParams(vmem_limit_bytes=16 * 1024 * 1024)


def parity():
    return lax.rem(lax.axis_index("tile"), 2)


def own_row(odd, j):
    return j + odd * (2 * SWEEPS - 1 - 2 * j)


OUTER, INNER = 0, 1


def row_of(side, odd, k):
    return own_row(odd, k if side == OUTER else 2 * SWEEPS - 1 - k)


def half_row(odd, j):
    return j % SWEEPS + odd * (SWEEPS - 1 - 2 * (j % SWEEPS))


def outer_start(odd):
    return SWEEPS * odd


def inner_start(odd):
    return SWEEPS * (1 - odd)


def swap_within(value):
    pairs = [(i, i + 1) for i in range(0, lax.axis_size("tile"), 2)]
    return lax.ppermute(value, "tile", pairs + [(b, a) for a, b in pairs])


def swap_across(value):
    tiles, times = lax.axis_size("tile"), lax.axis_size("tm")
    pairs = [((i, t), (i + 1, t)) for i in range(1, tiles - 1, 2) for t in range(times)]
    pairs += [((i, t), (i, t + 1)) for i in (0, tiles - 1) for t in range(0, times, 2)]
    flat = [(a * times + t, b * times + u) for (a, t), (b, u) in pairs]
    return lax.ppermute(value, ("tile", "tm"), flat + [(b, a) for a, b in flat])


FRACTION = (16, 16, 12, 12)


def to_fixed(value, bits):
    return jnp.round(value * float(2**bits)).astype(jnp.int32) + (8 << bits)


def from_fixed(value, bits):
    return (value - (8 << bits)).astype(jnp.float32) * float(0.5**bits)


QUARTERS = 4
PAIR_UNITS = 2 * QUARTERS + QUARTERS // 2


def unit_count(slots):
    return QUARTERS * slots + PAIR_UNITS * ((slots + 1) // 2) + 1


def encode(slots, read, code, packet):
    width = packet.shape[2]

    def quarters(value):
        return [value[:, part * width : (part + 1) * width] for part in range(QUARTERS)]

    def halves_together(value):
        parts = quarters(value)
        return [low | (high << 16) for low, high in zip(parts[: QUARTERS // 2], parts[QUARTERS // 2 :])]

    units, pairs = [], []
    for slot in range(slots):
        one, two, three, four = (to_fixed(read(slot, k), FRACTION[k]) for k in range(SWEEPS))
        units += quarters(one | (two << 20))
        rest = two >> 12
        if slot % 2:
            before = pairs.pop()
            pairs.append((before[0] | (three << 16), before[1] | (four << 16), before[2] | (rest << 8)))
        else:
            pairs.append((three, four, rest))
    for three, four, rest in pairs:
        units += quarters(three) + quarters(four) + halves_together(rest)
    for index, unit in enumerate(units):
        packet[index] = unit
    for k in range(SWEEPS):
        for part, unit in enumerate(halves_together(code(k))):
            packet[len(units), pl.ds(k * (QUARTERS // 2) + part, 1), :] = unit


def decode(packet, slots, slot, k):
    base = QUARTERS * slots + PAIR_UNITS * (slot // 2)

    def words(start, count=QUARTERS):
        return jnp.concatenate([packet[start + part] for part in range(count)], axis=1)

    def right(value, bits):
        return lax.shift_right_logical(value, jnp.int32(bits))

    if k == 0:
        value = words(QUARTERS * slot) & 0xFFFFF
    elif k == 1:
        folded = words(base + 2 * QUARTERS, QUARTERS // 2)
        rest = jnp.concatenate([folded, right(folded, 16)], axis=1)
        rest = right(rest, 8) & 0xFF if slot % 2 else rest & 0xFF
        value = right(words(QUARTERS * slot), 20) | (rest << 12)
    else:
        value = words(base + QUARTERS * (k - 2))
        value = right(value, 16) if slot % 2 else value & 0xFFFF
    return from_fixed(value, FRACTION[k])


def decode_codes(packet, slots, k):
    half = QUARTERS // 2
    words = [packet[unit_count(slots) - 1, pl.ds(k * half + part, 1), :] for part in range(half)]
    return jnp.concatenate([word & 0xFFFF for word in words] + [word >> 16 for word in words], axis=1)


def pack_kernel(
    controls, mask, diffusivity, across, within, mine, codes, table, kept, coef, halves, sems, *scratch
):
    odd = parity()
    slots = controls.shape[0]
    copies = [
        pltpu.make_async_copy(mask, codes, sems.at[0]),
        pltpu.make_async_copy(diffusivity, table, sems.at[1]),
    ]
    for start in (outer_start(odd), inner_start(odd)):
        for slot in range(slots):
            for part in range(2):
                rows = pl.ds(start + SWEEPS // 2 * part, SWEEPS // 2)
                copies.append(
                    pltpu.make_async_copy(controls.at[slot, rows], mine.at[slot, rows], sems.at[len(copies)])
                )
    own, outer, inner = copies[:2], copies[2 : 2 + 2 * slots], copies[2 + 2 * slots :]
    for copy in outer + own + inner:
        copy.start()

    def read(side, arriving, slot, k):
        if k == 0:
            for copy in arriving[2 * slot : 2 * slot + 2]:
                copy.wait()
        return mine[slot, row_of(side, odd, k)]

    def code(side, k):
        if side == OUTER and k == 0:
            for copy in own:
                copy.wait()
        return codes[pl.ds(row_of(side, odd, k), 1), :] + 1

    for side, packet, arriving in ((OUTER, across, outer), (INNER, within, inner)):
        encode(slots, functools.partial(read, side, arriving), functools.partial(code, side), packet)

    @pl.when(starts_first())
    def _():
        own_rows(mine, codes, table, kept, coef, halves, *scratch)


def by_level(table, kind, shape):
    levels = shape[0]
    square = jnp.broadcast_to(table[kind : kind + 1, :], (levels, levels))
    diagonal = lax.broadcasted_iota(jnp.int32, square.shape, 0) == lax.broadcasted_iota(jnp.int32, square.shape, 1)
    return jnp.broadcast_to(jnp.sum(jnp.where(diagonal, square, 0.0), axis=1, keepdims=True), shape)


def kappa_of(code, sea, land):
    return jnp.where(jnp.broadcast_to(code, sea.shape) == 2, land, sea)


def along_row(kappa):
    columns = kappa.shape[1]
    lane = lax.broadcasted_iota(jnp.int32, kappa.shape, 1)
    last = lane == columns - 1
    loss = kappa + jnp.where(last, 0.0, pltpu.roll(kappa, columns - 1, 1))
    east = jnp.where(last, 0.0, loss)
    west = pltpu.roll(east, 1, 1)
    return east, west, loss + jnp.where(lane == 0, kappa, west)


def sideways(centre, east, west, here):
    columns = here.shape[1]
    return centre * here + east * pltpu.roll(here, columns - 1, 1) + west * pltpu.roll(here, 1, 1)


FACE, EAST, WEST, CENTRE, KAPPA, COEFS = 0, 4, 8, 12, 16, 17
PART, VALUE, KEPT = 0, SWEEPS, 2 * SWEEPS - 1


def starts_first():
    return jnp.logical_and(lax.axis_index("tile") == 0, lax.axis_index("tm") == 0)


def middle_kernel(controls, codes, table, *refs):
    kept, coef, halves = refs[3:6]

    @pl.when(jnp.logical_not(starts_first()))
    def _():
        own_rows(controls, codes, table, kept, coef, halves, *refs[6:])


def own_rows(controls, codes, table, kept, coef, halves, shifted, face, centre, east, west, field):
    odd = parity()
    slots, _, levels, columns = controls.shape
    shape = (levels, columns)
    total = 2 * SWEEPS
    for kind in range(2):
        halves[kind] = 0.5 * by_level(table, kind, shape)
    sea, land = halves[0], halves[1]

    lane = lax.broadcasted_iota(jnp.int32, shape, 1)
    first_lane, last_lane = lane == 0, lane == columns - 1
    shifted[0] = pltpu.roll(codes[...], columns - 1, 1)
    shifted[1] = pltpu.roll(codes[...], 1, 1)
    previous = lost = None
    for j in range(total):
        place = pl.ds(own_row(odd, j), 1)
        kappa = kappa_of(codes[place, :] + 1, sea, land)
        to_east = kappa + jnp.where(last_lane, 0.0, kappa_of(shifted[0, place, :] + 1, sea, land))
        to_west = kappa + jnp.where(first_lane, 0.0, kappa_of(shifted[1, place, :] + 1, sea, land))
        loss = to_east + to_west
        e, w = jnp.where(last_lane, 0.0, to_east), jnp.where(first_lane, 0.0, to_west)
        east[j], west[j] = e, w
        if j:
            face[j] = previous + kappa
            centre[j - 1] = 1.0 - (lost + face[j])
            lost = loss + face[j]
        else:
            lost = loss
        previous = kappa
        for side, k in ((OUTER, j), (INNER, total - 1 - j)):
            if k == 0:
                coef[side, KAPPA] = kappa
            if k < SWEEPS:
                coef[side, EAST + k], coef[side, WEST + k] = e, w
    centre[total - 1] = 1.0 - lost
    for k in range(SWEEPS):
        coef[OUTER, CENTRE + k], coef[INNER, CENTRE + k] = centre[k], centre[total - 1 - k]
        if k:
            coef[OUTER, FACE + k], coef[INNER, FACE + k] = face[k], face[total - k]

    def value(slot, sweep, j):
        return field[sweep - 1, slot, j] if sweep else controls[slot, own_row(odd, j)]

    for sweep in range(1, SWEEPS + 1):
        low, high = sweep - 1, total - sweep
        before = [None] * slots
        here = [value(slot, sweep - 1, low) for slot in range(slots)]
        for j in range(low, high + 1):
            c, e, w = centre[j], east[j], west[j]
            below = face[j] if j > low else None
            above = face[j + 1] if j < high else None
            for slot in range(slots):
                after = None
                result = sideways(c, e, w, here[slot])
                if above is not None:
                    after = value(slot, sweep - 1, j + 1)
                    result = result + above * after
                if below is not None:
                    result = result + below * before[slot]
                if j == low:
                    kept[OUTER, slot, PART + sweep - 1] = result
                elif j == high:
                    kept[INNER, slot, PART + sweep - 1] = result
                else:
                    field[sweep - 1, slot, j] = result
                    if j == low + 1:
                        kept[OUTER, slot, VALUE + sweep - 1] = result
                    if j == high - 1:
                        kept[INNER, slot, VALUE + sweep - 1] = result
                before[slot], here[slot] = here[slot], after


def edge_here(odd):
    tile, tiles = lax.axis_index("tile"), lax.axis_size("tile")
    return jnp.where(odd == 1, tile == tiles - 1, tile == 0)


def side_rows(side, odd, controls, neighbour, kept, coef, weights, face, centre, east, west, field):
    slots = controls.shape[0]
    if neighbour is None:
        face[SWEEPS] = coef[side, KAPPA]
    else:
        far, far_kappa = neighbour
        previous = far_kappa(-SWEEPS)
        lost = None
        for k in range(1 - SWEEPS, 1):
            i = k + SWEEPS
            kappa = far_kappa(k) if k else coef[side, KAPPA]
            step = previous + kappa
            face[i] = step
            if lost is not None:
                centre[i - 1] = 1.0 - (lost + step)
            if k:
                e, w, loss = along_row(kappa)
                east[i], west[i] = e, w
                lost = loss + step
            previous = kappa
    centre[SWEEPS] = coef[side, CENTRE] - face[SWEEPS]

    def value(slot, sweep, k):
        if sweep == 0:
            return far(slot, k) if k < 0 else controls[slot, row_of(side, odd, k)]
        if k == sweep:
            return kept[side, slot, VALUE + sweep - 1]
        return field[sweep - 1, slot, k + SWEEPS]

    for sweep in range(1, SWEEPS + 1):
        low = 0 if neighbour is None else sweep - SWEEPS
        before = [None if neighbour is None else value(slot, sweep - 1, low - 1) for slot in range(slots)]
        here = [value(slot, sweep - 1, low) for slot in range(slots)]
        for k in range(low, sweep):
            i = k + SWEEPS
            below = face[i] if k <= 0 else coef[side, FACE + k]
            if k < sweep - 1:
                above = face[i + 1] if k < 0 else coef[side, FACE + k + 1]
                c = centre[i] if k <= 0 else coef[side, CENTRE + k]
                e, w = (east[i], west[i]) if k < 0 else (coef[side, EAST + k], coef[side, WEST + k])
            for slot in range(slots):
                after = None
                if k < sweep - 1:
                    after = value(slot, sweep - 1, k + 1)
                    result = sideways(c, e, w, here[slot]) + above * after
                    if before[slot] is not None:
                        result = result + below * before[slot]
                else:
                    result = kept[side, slot, PART + sweep - 1]
                    if before[slot] is not None:
                        result = result + below * before[slot]
                    if k == 0:
                        result = result - below * here[slot]
                if sweep == SWEEPS:
                    place = half_row(odd, k if side == OUTER else 2 * SWEEPS - 1 - k)
                    weights[slot, place] = result.astype(weights.dtype)
                else:
                    field[sweep - 1, slot, i] = result
                before[slot], here[slot] = here[slot], after


def neighbour_of(packet, slots, halves):
    return (
        lambda slot, k: decode(packet, slots, slot, -1 - k),
        lambda k: kappa_of(decode_codes(packet, slots, -1 - k), halves[0], halves[1]),
    )


def inner_kernel(controls, packet, kept, coef, halves, weights, *scratch):
    neighbour = neighbour_of(packet, controls.shape[0], halves)
    side_rows(INNER, parity(), controls, neighbour, kept, coef, weights, *scratch)


def outer_kernel(controls, packet, kept, coef, halves, weights, *scratch):
    odd = parity()
    edge = edge_here(odd)

    @pl.when(edge)
    def _():
        side_rows(OUTER, odd, controls, None, kept, coef, weights, *scratch)

    @pl.when(jnp.logical_not(edge))
    def _():
        neighbour = neighbour_of(packet, controls.shape[0], halves)
        side_rows(OUTER, odd, controls, neighbour, kept, coef, weights, *scratch)


def products(pert, weight, total):
    return [
        term if old is None else old + term
        for old, term in zip(total, [p.astype(jnp.float32) * weight for p in pert])
    ]


def own_kernel(factor, pert, owner, inner, outer, near_part, far_part, near_others, far_others, sems):
    odd = parity()
    count, here = lax.axis_size("tm"), lax.axis_index("tm")
    slots, variables = inner.shape[0], pert.shape[1]

    def member(step, slot):
        return owner[lax.rem(here - step + count, count) * slots + slot]

    copies = []
    for step in range(1, count):
        for slot in range(slots):
            place = (step - 1) * slots + slot
            for side, (start, others) in enumerate(
                ((inner_start(odd), near_others), (outer_start(odd), far_others))
            ):
                copies.append(
                    pltpu.make_async_copy(
                        pert.at[member(step, slot), :, pl.ds(start, SWEEPS)],
                        others.at[place],
                        sems.at[2 * place + side],
                    )
                )
    for copy in copies:
        copy.start()
    for start, weights, part in (
        (inner_start(odd), inner, near_part),
        (outer_start(odd), outer, far_part),
    ):
        for row in range(SWEEPS):
            total = [None] * variables
            for slot in range(slots):
                weight = weights[slot, row].astype(jnp.float32) * factor
                who = member(0, slot)
                total = products([pert[who, v, start + row] for v in range(variables)], weight, total)
            for v in range(variables):
                part[v, row] = total[v]
    for copy in copies:
        copy.wait()


def add_others(factor, part, others, arrived, row, variables):
    total = [part[v, row] for v in variables]
    for index, weights in enumerate(arrived):
        slots = weights.shape[0]
        for slot in range(slots):
            weight = weights[slot, row].astype(jnp.float32) * factor
            place = index * slots + slot
            total = products([others[place, v, row] for v in variables], weight, total)
    return total


def add_and_write(factor, start, part, others, arrived, out, ready, sems):
    count = part.shape[0]
    half = (count + 1) // 2
    writes = []
    for first in range(0, count, half):
        variables = range(first, min(first + half, count))
        for row in range(SWEEPS):
            for v, total in zip(variables, add_others(factor, part, others, arrived, row, variables)):
                ready[v, row] = total
        for v in variables:
            writes.append(pltpu.make_async_copy(ready.at[v], out.at[v, pl.ds(start, SWEEPS)], sems.at[v]))
            writes[-1].start()
    for copy in writes:
        copy.wait()


def near_kernel(factor, part, others, *refs):
    *arrived, out, ready, sems = refs
    add_and_write(factor, inner_start(parity()), part, others, arrived, out, ready, sems)


def far_kernel(factor, part, others, *refs):
    *arrived, _, out, ready, sems = refs
    add_and_write(factor, outer_start(parity()), part, others, arrived, out, ready, sems)


def cost(flops, moved):
    return pl.CostEstimate(flops=flops, bytes_accessed=moved, transcendentals=0)


def near(value):
    return pltpu.with_memory_space_constraint(value, pltpu.VMEM)


def far(value):
    return pltpu.with_memory_space_constraint(value, pltpu.HBM)


def on_device(controls, perturbations, owner, land_mask, diffusivity):
    slots, height, levels, columns = controls.shape
    members, variables = perturbations.shape[1:3]
    count = lax.axis_size("tm")
    factor = 1.0 / math.sqrt(owner.shape[0] - 1)
    row = (levels, columns)
    f32, bf16 = jnp.float32, jnp.bfloat16
    dma = pltpu.SemaphoreType.DMA

    packet = pltpu.VMEM((unit_count(slots), levels, columns // QUARTERS), jnp.int32)
    middle_scratch = [pltpu.VMEM((2, height, columns), jnp.int32)]
    middle_scratch += [pltpu.VMEM((height, *row), f32)] * 4
    middle_scratch += [pltpu.VMEM((SWEEPS - 1, slots, height, *row), f32)]
    middle_out = (
        pltpu.VMEM((2, slots, KEPT, *row), f32),
        pltpu.VMEM((2, COEFS, *row), f32),
        pltpu.VMEM((2, *row), f32),
    )
    my_across, my_within, mine, codes, table, *middle = pl.pallas_call(
        pack_kernel,
        out_shape=(
            packet,
            packet,
            pltpu.VMEM(controls.shape, f32),
            pltpu.VMEM((height, columns), jnp.int32),
            pltpu.VMEM((2, levels), f32),
            *middle_out,
        ),
        in_specs=[ANY, ANY, ANY],
        out_specs=(VMEM,) * 8,
        scratch_shapes=[dma((4 * slots + 2,)), *middle_scratch],
        compiler_params=PARAMS,
        name="pack",
    )(far(controls), far(land_mask), far(diffusivity))
    across = swap_across(my_across)
    within = swap_within(my_within)
    mine = near(mine)

    half = pltpu.VMEM((slots, SWEEPS, *row), bf16)
    kept, coef, halves = pl.pallas_call(
        middle_kernel,
        out_shape=middle_out,
        in_specs=[VMEM] * 6,
        out_specs=(VMEM,) * 3,
        scratch_shapes=middle_scratch,
        input_output_aliases={3: 0, 4: 1, 5: 2},
        compiler_params=PARAMS,
        cost_estimate=cost(1, 1),
        name="middle",
    )(mine, near(codes), near(table), *map(near, middle))
    shared = (near(kept), near(coef), near(halves))

    def side(kernel, name, *operands):
        return pl.pallas_call(
            kernel,
            out_shape=half,
            in_specs=[VMEM] * len(operands),
            out_specs=VMEM,
            scratch_shapes=[pltpu.VMEM((SWEEPS + 1, *row), f32)] * 4
            + [pltpu.VMEM((SWEEPS - 1, slots, 2 * SWEEPS, *row), f32)],
            compiler_params=PARAMS,
            cost_estimate=cost(1, 1),
            name=name,
        )(*operands)

    inner = side(inner_kernel, "inner_rows", mine, near(within), *shared)

    def shift(value):
        return [
            near(lax.ppermute(value, "tm", [(i, (i + step) % count) for i in range(count)]))
            for step in range(1, count)
        ]

    inner_arrived = shift(inner)
    outer = side(outer_kernel, "outer_rows", mine, near(across), *shared)
    outer_arrived = shift(outer)

    arrivals = count - 1
    part = pltpu.VMEM((variables, SWEEPS, *row), f32)
    others = pltpu.VMEM((max(arrivals, 1) * slots, variables, SWEEPS, *row), bf16)
    near_part, far_part, near_others, far_others = pl.pallas_call(
        lambda *refs: own_kernel(factor, *refs),
        out_shape=(part, part, others, others),
        in_specs=[VMEM, SMEM, VMEM, VMEM],
        out_specs=(VMEM,) * 4,
        scratch_shapes=[dma((2 * max(arrivals, 1) * slots,))],
        compiler_params=PARAMS,
        cost_estimate=cost(4_000_000, 2_000_000),
        name="own_products",
    )(near(perturbations[0]), owner, near(inner), near(outer))
    result = jax.ShapeDtypeStruct((variables, height, *row), f32)
    scratch = [pltpu.VMEM((variables, SWEEPS, *row), f32), dma((variables,))]
    out = pl.pallas_call(
        lambda *refs: near_kernel(factor, *refs),
        out_shape=result,
        in_specs=[VMEM] * (2 + arrivals),
        out_specs=ANY,
        scratch_shapes=scratch,
        compiler_params=PARAMS,
        cost_estimate=cost(1_000_000, 1_000_000),
        name="near_products",
    )(near(near_part), near(near_others), *inner_arrived)
    out = pl.pallas_call(
        lambda *refs: far_kernel(factor, *refs),
        out_shape=result,
        in_specs=[VMEM] * (2 + arrivals) + [ANY],
        out_specs=ANY,
        scratch_shapes=scratch,
        input_output_aliases={2 + arrivals: 0},
        compiler_params=PARAMS,
        cost_estimate=cost(1_000_000, 1_000_000),
        name="far_products",
    )(near(far_part), near(far_others), *outer_arrived, out)
    return out[None]


def solution(mesh):
    return jax.shard_map(
        on_device,
        mesh=mesh,
        in_specs=(
            P("tm", "tile", None, None),
            P("tm", None, None, "tile", None, None),
            P(),
            P("tile", None),
            P(),
        ),
        out_specs=P("tm", None, "tile", None, None),
        check_vma=False,
    )
```

```python
import functools
import math

import jax
import jax.numpy as jnp
from jax import lax
from jax.experimental import pallas as pl
from jax.experimental.pallas import tpu as pltpu
from jax.sharding import PartitionSpec as P

SWEEPS = 4
VMEM = pl.BlockSpec(memory_space=pltpu.VMEM)
SMEM = pl.BlockSpec(memory_space=pltpu.SMEM)
ANY = pl.BlockSpec(memory_space=pl.ANY)
PARAMS = pltpu.CompilerParams(vmem_limit_bytes=16 * 1024 * 1024)


def parity():
    return lax.rem(lax.axis_index("tile"), 2)


def own_row(odd, j):
    return j + odd * (2 * SWEEPS - 1 - 2 * j)


OUTER, INNER = 0, 1


def row_of(side, odd, k):
    return own_row(odd, k if side == OUTER else 2 * SWEEPS - 1 - k)


def half_row(odd, j):
    return j % SWEEPS + odd * (SWEEPS - 1 - 2 * (j % SWEEPS))


def outer_start(odd):
    return SWEEPS * odd


def inner_start(odd):
    return SWEEPS * (1 - odd)


def swap_within(value):
    pairs = [(i, i + 1) for i in range(0, lax.axis_size("tile"), 2)]
    return lax.ppermute(value, "tile", pairs + [(b, a) for a, b in pairs])


def swap_across(value):
    tiles, times = lax.axis_size("tile"), lax.axis_size("tm")
    pairs = [((i, t), (i + 1, t)) for i in range(1, tiles - 1, 2) for t in range(times)]
    pairs += [((i, t), (i, t + 1)) for i in (0, tiles - 1) for t in range(0, times, 2)]
    flat = [(a * times + t, b * times + u) for (a, t), (b, u) in pairs]
    return lax.ppermute(value, ("tile", "tm"), flat + [(b, a) for a, b in flat])


FRACTION = (16, 16, 12, 12)


def to_fixed(value, bits):
    return jnp.round(value * float(2**bits)).astype(jnp.int32) + (8 << bits)


def from_fixed(value, bits):
    return (value - (8 << bits)).astype(jnp.float32) * float(0.5**bits)


QUARTERS = 4
PAIR_UNITS = 2 * QUARTERS + QUARTERS // 2


def unit_count(slots):
    return QUARTERS * slots + PAIR_UNITS * ((slots + 1) // 2) + 1


def encode(slots, read, code, packet):
    width = packet.shape[2]

    def quarters(value):
        return [value[:, part * width : (part + 1) * width] for part in range(QUARTERS)]

    def halves_together(value):
        parts = quarters(value)
        return [low | (high << 16) for low, high in zip(parts[: QUARTERS // 2], parts[QUARTERS // 2 :])]

    units, pairs = [], []
    for slot in range(slots):
        one, two, three, four = (to_fixed(read(slot, k), FRACTION[k]) for k in range(SWEEPS))
        units += quarters(one | (two << 20))
        rest = two >> 12
        if slot % 2:
            before = pairs.pop()
            pairs.append((before[0] | (three << 16), before[1] | (four << 16), before[2] | (rest << 8)))
        else:
            pairs.append((three, four, rest))
    for three, four, rest in pairs:
        units += quarters(three) + quarters(four) + halves_together(rest)
    for index, unit in enumerate(units):
        packet[index] = unit
    for k in range(SWEEPS):
        for part, unit in enumerate(halves_together(code(k))):
            packet[len(units), pl.ds(k * (QUARTERS // 2) + part, 1), :] = unit


def decode(packet, slots, slot, k):
    base = QUARTERS * slots + PAIR_UNITS * (slot // 2)

    def words(start, count=QUARTERS):
        return jnp.concatenate([packet[start + part] for part in range(count)], axis=1)

    def right(value, bits):
        return lax.shift_right_logical(value, jnp.int32(bits))

    if k == 0:
        value = words(QUARTERS * slot) & 0xFFFFF
    elif k == 1:
        folded = words(base + 2 * QUARTERS, QUARTERS // 2)
        rest = jnp.concatenate([folded, right(folded, 16)], axis=1)
        rest = right(rest, 8) & 0xFF if slot % 2 else rest & 0xFF
        value = right(words(QUARTERS * slot), 20) | (rest << 12)
    else:
        value = words(base + QUARTERS * (k - 2))
        value = right(value, 16) if slot % 2 else value & 0xFFFF
    return from_fixed(value, FRACTION[k])


def decode_codes(packet, slots, k):
    half = QUARTERS // 2
    words = [packet[unit_count(slots) - 1, pl.ds(k * half + part, 1), :] for part in range(half)]
    return jnp.concatenate([word & 0xFFFF for word in words] + [word >> 16 for word in words], axis=1)


def pack_kernel(controls, mask, diffusivity, across, within, mine, codes, table, sems):
    odd = parity()
    slots = controls.shape[0]
    copies = [
        pltpu.make_async_copy(mask, codes, sems.at[0]),
        pltpu.make_async_copy(diffusivity, table, sems.at[1]),
    ]
    for start in (outer_start(odd), inner_start(odd)):
        for slot in range(slots):
            for part in range(2):
                rows = pl.ds(start + SWEEPS // 2 * part, SWEEPS // 2)
                copies.append(
                    pltpu.make_async_copy(controls.at[slot, rows], mine.at[slot, rows], sems.at[len(copies)])
                )
    own, outer, inner = copies[:2], copies[2 : 2 + 2 * slots], copies[2 + 2 * slots :]
    for copy in own[:1] + outer + inner + own[1:]:
        copy.start()

    def read(side, arriving, slot, k):
        if k == 0:
            for copy in arriving[2 * slot : 2 * slot + 2]:
                copy.wait()
        return mine[slot, row_of(side, odd, k)]

    def code(side, k):
        if side == OUTER and k == 0:
            for copy in own:
                copy.wait()
        return codes[pl.ds(row_of(side, odd, k), 1), :] + 1

    for side, packet, arriving in ((OUTER, across, outer), (INNER, within, inner)):
        encode(slots, functools.partial(read, side, arriving), functools.partial(code, side), packet)


def by_level(table, kind, shape):
    levels = shape[0]
    square = jnp.broadcast_to(table[kind : kind + 1, :], (levels, levels))
    diagonal = lax.broadcasted_iota(jnp.int32, square.shape, 0) == lax.broadcasted_iota(jnp.int32, square.shape, 1)
    return jnp.broadcast_to(jnp.sum(jnp.where(diagonal, square, 0.0), axis=1, keepdims=True), shape)


def kappa_of(code, sea, land):
    return jnp.where(jnp.broadcast_to(code, sea.shape) == 2, land, sea)


def along_row(kappa):
    columns = kappa.shape[1]
    lane = lax.broadcasted_iota(jnp.int32, kappa.shape, 1)
    last = lane == columns - 1
    loss = kappa + jnp.where(last, 0.0, pltpu.roll(kappa, columns - 1, 1))
    east = jnp.where(last, 0.0, loss)
    west = pltpu.roll(east, 1, 1)
    return east, west, loss + jnp.where(lane == 0, kappa, west)


def sideways(centre, east, west, here):
    columns = here.shape[1]
    return centre * here + east * pltpu.roll(here, columns - 1, 1) + west * pltpu.roll(here, 1, 1)


FACE, EAST, WEST, CENTRE, KAPPA, COEFS = 0, 4, 8, 12, 16, 17
PART, VALUE, KEPT = 0, SWEEPS, 2 * SWEEPS - 1


def middle_kernel(controls, codes, table, kept, coef, halves, shifted, face, centre, east, west, field):
    odd = parity()
    slots, _, levels, columns = controls.shape
    shape = (levels, columns)
    total = 2 * SWEEPS
    for kind in range(2):
        halves[kind] = 0.5 * by_level(table, kind, shape)
    sea, land = halves[0], halves[1]

    lane = lax.broadcasted_iota(jnp.int32, shape, 1)
    first_lane, last_lane = lane == 0, lane == columns - 1
    shifted[0] = pltpu.roll(codes[...], columns - 1, 1)
    shifted[1] = pltpu.roll(codes[...], 1, 1)
    previous = lost = None
    for j in range(total):
        place = pl.ds(own_row(odd, j), 1)
        kappa = kappa_of(codes[place, :] + 1, sea, land)
        to_east = kappa + jnp.where(last_lane, 0.0, kappa_of(shifted[0, place, :] + 1, sea, land))
        to_west = kappa + jnp.where(first_lane, 0.0, kappa_of(shifted[1, place, :] + 1, sea, land))
        loss = to_east + to_west
        e, w = jnp.where(last_lane, 0.0, to_east), jnp.where(first_lane, 0.0, to_west)
        east[j], west[j] = e, w
        if j:
            face[j] = previous + kappa
            centre[j - 1] = 1.0 - (lost + face[j])
            lost = loss + face[j]
        else:
            lost = loss
        previous = kappa
        for side, k in ((OUTER, j), (INNER, total - 1 - j)):
            if k == 0:
                coef[side, KAPPA] = kappa
            if k < SWEEPS:
                coef[side, EAST + k], coef[side, WEST + k] = e, w
    centre[total - 1] = 1.0 - lost
    for k in range(SWEEPS):
        coef[OUTER, CENTRE + k], coef[INNER, CENTRE + k] = centre[k], centre[total - 1 - k]
        if k:
            coef[OUTER, FACE + k], coef[INNER, FACE + k] = face[k], face[total - k]

    def value(slot, sweep, j):
        return field[sweep - 1, slot, j] if sweep else controls[slot, own_row(odd, j)]

    for sweep in range(1, SWEEPS + 1):
        low, high = sweep - 1, total - sweep
        before = [None] * slots
        here = [value(slot, sweep - 1, low) for slot in range(slots)]
        for j in range(low, high + 1):
            c, e, w = centre[j], east[j], west[j]
            below = face[j] if j > low else None
            above = face[j + 1] if j < high else None
            for slot in range(slots):
                after = None
                result = sideways(c, e, w, here[slot])
                if above is not None:
                    after = value(slot, sweep - 1, j + 1)
                    result = result + above * after
                if below is not None:
                    result = result + below * before[slot]
                if j == low:
                    kept[OUTER, slot, PART + sweep - 1] = result
                elif j == high:
                    kept[INNER, slot, PART + sweep - 1] = result
                else:
                    field[sweep - 1, slot, j] = result
                    if j == low + 1:
                        kept[OUTER, slot, VALUE + sweep - 1] = result
                    if j == high - 1:
                        kept[INNER, slot, VALUE + sweep - 1] = result
                before[slot], here[slot] = here[slot], after


def edge_here(odd):
    tile, tiles = lax.axis_index("tile"), lax.axis_size("tile")
    return jnp.where(odd == 1, tile == tiles - 1, tile == 0)


def side_rows(side, odd, controls, neighbour, kept, coef, weights, face, centre, east, west, field):
    slots = controls.shape[0]
    if neighbour is None:
        face[SWEEPS] = coef[side, KAPPA]
    else:
        far, far_kappa = neighbour
        previous = far_kappa(-SWEEPS)
        lost = None
        for k in range(1 - SWEEPS, 1):
            i = k + SWEEPS
            kappa = far_kappa(k) if k else coef[side, KAPPA]
            step = previous + kappa
            face[i] = step
            if lost is not None:
                centre[i - 1] = 1.0 - (lost + step)
            if k:
                e, w, loss = along_row(kappa)
                east[i], west[i] = e, w
                lost = loss + step
            previous = kappa
    centre[SWEEPS] = coef[side, CENTRE] - face[SWEEPS]

    def value(slot, sweep, k):
        if sweep == 0:
            return far(slot, k) if k < 0 else controls[slot, row_of(side, odd, k)]
        if k == sweep:
            return kept[side, slot, VALUE + sweep - 1]
        return field[sweep - 1, slot, k + SWEEPS]

    for sweep in range(1, SWEEPS + 1):
        low = 0 if neighbour is None else sweep - SWEEPS
        before = [None if neighbour is None else value(slot, sweep - 1, low - 1) for slot in range(slots)]
        here = [value(slot, sweep - 1, low) for slot in range(slots)]
        for k in range(low, sweep):
            i = k + SWEEPS
            below = face[i] if k <= 0 else coef[side, FACE + k]
            if k < sweep - 1:
                above = face[i + 1] if k < 0 else coef[side, FACE + k + 1]
                c = centre[i] if k <= 0 else coef[side, CENTRE + k]
                e, w = (east[i], west[i]) if k < 0 else (coef[side, EAST + k], coef[side, WEST + k])
            for slot in range(slots):
                after = None
                if k < sweep - 1:
                    after = value(slot, sweep - 1, k + 1)
                    result = sideways(c, e, w, here[slot]) + above * after
                    if before[slot] is not None:
                        result = result + below * before[slot]
                else:
                    result = kept[side, slot, PART + sweep - 1]
                    if before[slot] is not None:
                        result = result + below * before[slot]
                    if k == 0:
                        result = result - below * here[slot]
                if sweep == SWEEPS:
                    place = half_row(odd, k if side == OUTER else 2 * SWEEPS - 1 - k)
                    weights[slot, place] = result.astype(weights.dtype)
                else:
                    field[sweep - 1, slot, i] = result
                before[slot], here[slot] = here[slot], after


def neighbour_of(packet, slots, halves):
    return (
        lambda slot, k: decode(packet, slots, slot, -1 - k),
        lambda k: kappa_of(decode_codes(packet, slots, -1 - k), halves[0], halves[1]),
    )


def inner_kernel(controls, packet, kept, coef, halves, weights, *scratch):
    neighbour = neighbour_of(packet, controls.shape[0], halves)
    side_rows(INNER, parity(), controls, neighbour, kept, coef, weights, *scratch)


def outer_kernel(controls, packet, kept, coef, halves, weights, *scratch):
    odd = parity()
    edge = edge_here(odd)

    @pl.when(edge)
    def _():
        side_rows(OUTER, odd, controls, None, kept, coef, weights, *scratch)

    @pl.when(jnp.logical_not(edge))
    def _():
        neighbour = neighbour_of(packet, controls.shape[0], halves)
        side_rows(OUTER, odd, controls, neighbour, kept, coef, weights, *scratch)


def products(pert, weight, total):
    return [
        term if old is None else old + term
        for old, term in zip(total, [p.astype(jnp.float32) * weight for p in pert])
    ]


def own_kernel(factor, pert, owner, inner, outer, near_part, far_part, near_others, far_others, sems):
    odd = parity()
    count, here = lax.axis_size("tm"), lax.axis_index("tm")
    slots, variables = inner.shape[0], pert.shape[1]

    def member(step, slot):
        return owner[lax.rem(here - step + count, count) * slots + slot]

    copies = []
    for step in range(1, count):
        for slot in range(slots):
            place = (step - 1) * slots + slot
            for side, (start, others) in enumerate(
                ((inner_start(odd), near_others), (outer_start(odd), far_others))
            ):
                copies.append(
                    pltpu.make_async_copy(
                        pert.at[member(step, slot), :, pl.ds(start, SWEEPS)],
                        others.at[place],
                        sems.at[2 * place + side],
                    )
                )
    for copy in copies:
        copy.start()
    for start, weights, part in (
        (inner_start(odd), inner, near_part),
        (outer_start(odd), outer, far_part),
    ):
        for row in range(SWEEPS):
            total = [None] * variables
            for slot in range(slots):
                weight = weights[slot, row].astype(jnp.float32) * factor
                who = member(0, slot)
                total = products([pert[who, v, start + row] for v in range(variables)], weight, total)
            for v in range(variables):
                part[v, row] = total[v]
    for copy in copies:
        copy.wait()


def add_others(factor, part, others, arrived, row, variables):
    total = [part[v, row] for v in variables]
    for index, weights in enumerate(arrived):
        slots = weights.shape[0]
        for slot in range(slots):
            weight = weights[slot, row].astype(jnp.float32) * factor
            place = index * slots + slot
            total = products([others[place, v, row] for v in variables], weight, total)
    return total


def add_and_write(factor, start, part, others, arrived, out, ready, sems):
    count = part.shape[0]
    half = (count + 1) // 2
    writes = []
    for first in range(0, count, half):
        variables = range(first, min(first + half, count))
        for row in range(SWEEPS):
            for v, total in zip(variables, add_others(factor, part, others, arrived, row, variables)):
                ready[v, row] = total
        for v in variables:
            writes.append(pltpu.make_async_copy(ready.at[v], out.at[v, pl.ds(start, SWEEPS)], sems.at[v]))
            writes[-1].start()
    for copy in writes:
        copy.wait()


def near_kernel(factor, part, others, *refs):
    *arrived, out, ready, sems = refs
    add_and_write(factor, inner_start(parity()), part, others, arrived, out, ready, sems)


def far_kernel(factor, part, others, *refs):
    *arrived, _, out, ready, sems = refs
    add_and_write(factor, outer_start(parity()), part, others, arrived, out, ready, sems)


def cost(flops, moved):
    return pl.CostEstimate(flops=flops, bytes_accessed=moved, transcendentals=0)


def near(value):
    return pltpu.with_memory_space_constraint(value, pltpu.VMEM)


def far(value):
    return pltpu.with_memory_space_constraint(value, pltpu.HBM)


def on_device(controls, perturbations, owner, land_mask, diffusivity):
    slots, height, levels, columns = controls.shape
    members, variables = perturbations.shape[1:3]
    count = lax.axis_size("tm")
    factor = 1.0 / math.sqrt(owner.shape[0] - 1)
    row = (levels, columns)
    f32, bf16 = jnp.float32, jnp.bfloat16
    dma = pltpu.SemaphoreType.DMA

    packet = pltpu.VMEM((unit_count(slots), levels, columns // QUARTERS), jnp.int32)
    my_across, my_within, mine, codes, table = pl.pallas_call(
        pack_kernel,
        out_shape=(
            packet,
            packet,
            pltpu.VMEM(controls.shape, f32),
            pltpu.VMEM((height, columns), jnp.int32),
            pltpu.VMEM((2, levels), f32),
        ),
        in_specs=[ANY, ANY, ANY],
        out_specs=(VMEM,) * 5,
        scratch_shapes=[dma((2 * 2 * slots + 2,))],
        compiler_params=PARAMS,
        name="pack",
    )(far(controls), far(land_mask), far(diffusivity))
    across = swap_across(my_across)
    within = swap_within(my_within)
    mine = near(mine)

    half = pltpu.VMEM((slots, SWEEPS, *row), bf16)
    middle_scratch = [pltpu.VMEM((2, height, columns), jnp.int32)]
    middle_scratch += [pltpu.VMEM((height, *row), f32)] * 4
    middle_scratch += [pltpu.VMEM((SWEEPS - 1, slots, height, *row), f32)]
    kept, coef, halves = pl.pallas_call(
        middle_kernel,
        out_shape=(
            pltpu.VMEM((2, slots, KEPT, *row), f32),
            pltpu.VMEM((2, COEFS, *row), f32),
            pltpu.VMEM((2, *row), f32),
        ),
        in_specs=[VMEM] * 3,
        out_specs=(VMEM,) * 3,
        scratch_shapes=middle_scratch,
        compiler_params=PARAMS,
        cost_estimate=cost(1, 1),
        name="middle",
    )(mine, near(codes), near(table))
    shared = (near(kept), near(coef), near(halves))

    def side(kernel, name, *operands):
        return pl.pallas_call(
            kernel,
            out_shape=half,
            in_specs=[VMEM] * len(operands),
            out_specs=VMEM,
            scratch_shapes=[pltpu.VMEM((SWEEPS + 1, *row), f32)] * 4
            + [pltpu.VMEM((SWEEPS - 1, slots, 2 * SWEEPS, *row), f32)],
            compiler_params=PARAMS,
            cost_estimate=cost(1, 1),
            name=name,
        )(*operands)

    inner = side(inner_kernel, "inner_rows", mine, near(within), *shared)

    def shift(value):
        return [
            near(lax.ppermute(value, "tm", [(i, (i + step) % count) for i in range(count)]))
            for step in range(1, count)
        ]

    inner_arrived = shift(inner)
    outer = side(outer_kernel, "outer_rows", mine, near(across), *shared)
    outer_arrived = shift(outer)

    arrivals = count - 1
    part = pltpu.VMEM((variables, SWEEPS, *row), f32)
    others = pltpu.VMEM((max(arrivals, 1) * slots, variables, SWEEPS, *row), bf16)
    near_part, far_part, near_others, far_others = pl.pallas_call(
        lambda *refs: own_kernel(factor, *refs),
        out_shape=(part, part, others, others),
        in_specs=[VMEM, SMEM, VMEM, VMEM],
        out_specs=(VMEM,) * 4,
        scratch_shapes=[dma((2 * max(arrivals, 1) * slots,))],
        compiler_params=PARAMS,
        cost_estimate=cost(4_000_000, 2_000_000),
        name="own_products",
    )(near(perturbations[0]), owner, near(inner), near(outer))
    result = jax.ShapeDtypeStruct((variables, height, *row), f32)
    scratch = [pltpu.VMEM((variables, SWEEPS, *row), f32), dma((variables,))]
    out = pl.pallas_call(
        lambda *refs: near_kernel(factor, *refs),
        out_shape=result,
        in_specs=[VMEM] * (2 + arrivals),
        out_specs=ANY,
        scratch_shapes=scratch,
        compiler_params=PARAMS,
        cost_estimate=cost(1_000_000, 1_000_000),
        name="near_products",
    )(near(near_part), near(near_others), *inner_arrived)
    out = pl.pallas_call(
        lambda *refs: far_kernel(factor, *refs),
        out_shape=result,
        in_specs=[VMEM] * (2 + arrivals) + [ANY],
        out_specs=ANY,
        scratch_shapes=scratch,
        input_output_aliases={2 + arrivals: 0},
        compiler_params=PARAMS,
        cost_estimate=cost(1_000_000, 1_000_000),
        name="far_products",
    )(near(far_part), near(far_others), *outer_arrived, out)
    return out[None]


def solution(mesh):
    return jax.shard_map(
        on_device,
        mesh=mesh,
        in_specs=(
            P("tm", "tile", None, None),
            P("tm", None, None, "tile", None, None),
            P(),
            P("tile", None),
            P(),
        ),
        out_specs=P("tm", None, "tile", None, None),
        check_vma=False,
    )
```

```python
import functools
import math

import jax
import jax.numpy as jnp
from jax import lax
from jax.experimental import pallas as pl
from jax.experimental.pallas import tpu as pltpu
from jax.sharding import PartitionSpec as P

SWEEPS = 4
VMEM = pl.BlockSpec(memory_space=pltpu.VMEM)
SMEM = pl.BlockSpec(memory_space=pltpu.SMEM)
ANY = pl.BlockSpec(memory_space=pl.ANY)
PARAMS = pltpu.CompilerParams(vmem_limit_bytes=16 * 1024 * 1024)


def parity():
    return lax.rem(lax.axis_index("tile"), 2)


def own_row(odd, j):
    return j + odd * (2 * SWEEPS - 1 - 2 * j)


OUTER, INNER = 0, 1


def row_of(side, odd, k):
    return own_row(odd, k if side == OUTER else 2 * SWEEPS - 1 - k)


def half_row(odd, j):
    return j % SWEEPS + odd * (SWEEPS - 1 - 2 * (j % SWEEPS))


def outer_start(odd):
    return SWEEPS * odd


def inner_start(odd):
    return SWEEPS * (1 - odd)


def swap_within(value):
    pairs = [(i, i + 1) for i in range(0, lax.axis_size("tile"), 2)]
    return lax.ppermute(value, "tile", pairs + [(b, a) for a, b in pairs])


def swap_across(value):
    tiles, times = lax.axis_size("tile"), lax.axis_size("tm")
    pairs = [((i, t), (i + 1, t)) for i in range(1, tiles - 1, 2) for t in range(times)]
    pairs += [((i, t), (i, t + 1)) for i in (0, tiles - 1) for t in range(0, times, 2)]
    flat = [(a * times + t, b * times + u) for (a, t), (b, u) in pairs]
    return lax.ppermute(value, ("tile", "tm"), flat + [(b, a) for a, b in flat])


FRACTION = (16, 16, 12, 12)


def to_fixed(value, bits):
    return jnp.round(value * float(2**bits)).astype(jnp.int32) + (8 << bits)


def from_fixed(value, bits):
    return (value - (8 << bits)).astype(jnp.float32) * float(0.5**bits)


QUARTERS = 4
PAIR_UNITS = 2 * QUARTERS + QUARTERS // 2


def unit_count(slots):
    return QUARTERS * slots + PAIR_UNITS * ((slots + 1) // 2) + 1


def encode(slots, read, code, packet):
    width = packet.shape[2]

    def quarters(value):
        return [value[:, part * width : (part + 1) * width] for part in range(QUARTERS)]

    def halves_together(value):
        parts = quarters(value)
        return [low | (high << 16) for low, high in zip(parts[: QUARTERS // 2], parts[QUARTERS // 2 :])]

    units, pairs = [], []
    for slot in range(slots):
        one, two, three, four = (to_fixed(read(slot, k), FRACTION[k]) for k in range(SWEEPS))
        units += quarters(one | (two << 20))
        rest = two >> 12
        if slot % 2:
            before = pairs.pop()
            pairs.append((before[0] | (three << 16), before[1] | (four << 16), before[2] | (rest << 8)))
        else:
            pairs.append((three, four, rest))
    for three, four, rest in pairs:
        units += quarters(three) + quarters(four) + halves_together(rest)
    for index, unit in enumerate(units):
        packet[index] = unit
    for k in range(SWEEPS):
        for part, unit in enumerate(halves_together(code(k))):
            packet[len(units), pl.ds(k * (QUARTERS // 2) + part, 1), :] = unit


def decode(packet, slots, slot, k):
    base = QUARTERS * slots + PAIR_UNITS * (slot // 2)

    def words(start, count=QUARTERS):
        return jnp.concatenate([packet[start + part] for part in range(count)], axis=1)

    def right(value, bits):
        return lax.shift_right_logical(value, jnp.int32(bits))

    if k == 0:
        value = words(QUARTERS * slot) & 0xFFFFF
    elif k == 1:
        folded = words(base + 2 * QUARTERS, QUARTERS // 2)
        rest = jnp.concatenate([folded, right(folded, 16)], axis=1)
        rest = right(rest, 8) & 0xFF if slot % 2 else rest & 0xFF
        value = right(words(QUARTERS * slot), 20) | (rest << 12)
    else:
        value = words(base + QUARTERS * (k - 2))
        value = right(value, 16) if slot % 2 else value & 0xFFFF
    return from_fixed(value, FRACTION[k])


def decode_codes(packet, slots, k):
    half = QUARTERS // 2
    words = [packet[unit_count(slots) - 1, pl.ds(k * half + part, 1), :] for part in range(half)]
    return jnp.concatenate([word & 0xFFFF for word in words] + [word >> 16 for word in words], axis=1)


def pack_kernel(
    controls, mask, diffusivity, across, within, mine, codes, table, kept, coef, halves, sems, *scratch
):
    odd = parity()
    slots = controls.shape[0]
    copies = [
        pltpu.make_async_copy(mask, codes, sems.at[0]),
        pltpu.make_async_copy(diffusivity, table, sems.at[1]),
    ]
    for start in (outer_start(odd), inner_start(odd)):
        for slot in range(slots):
            for part in range(2):
                rows = pl.ds(start + SWEEPS // 2 * part, SWEEPS // 2)
                copies.append(
                    pltpu.make_async_copy(controls.at[slot, rows], mine.at[slot, rows], sems.at[len(copies)])
                )
    own, outer, inner = copies[:2], copies[2 : 2 + 2 * slots], copies[2 + 2 * slots :]
    for copy in own[:1] + outer + inner + own[1:]:
        copy.start()

    def read(side, arriving, slot, k):
        if k == 0:
            for copy in arriving[2 * slot : 2 * slot + 2]:
                copy.wait()
        return mine[slot, row_of(side, odd, k)]

    def code(side, k):
        if side == OUTER and k == 0:
            for copy in own:
                copy.wait()
        return codes[pl.ds(row_of(side, odd, k), 1), :] + 1

    for side, packet, arriving in ((OUTER, across, outer), (INNER, within, inner)):
        encode(slots, functools.partial(read, side, arriving), functools.partial(code, side), packet)

    @pl.when(starts_first())
    def _():
        own_rows(mine, codes, table, kept, coef, halves, *scratch)


def by_level(table, kind, shape):
    levels = shape[0]
    square = jnp.broadcast_to(table[kind : kind + 1, :], (levels, levels))
    diagonal = lax.broadcasted_iota(jnp.int32, square.shape, 0) == lax.broadcasted_iota(jnp.int32, square.shape, 1)
    return jnp.broadcast_to(jnp.sum(jnp.where(diagonal, square, 0.0), axis=1, keepdims=True), shape)


def kappa_of(code, sea, land):
    return jnp.where(jnp.broadcast_to(code, sea.shape) == 2, land, sea)


def along_row(kappa):
    columns = kappa.shape[1]
    lane = lax.broadcasted_iota(jnp.int32, kappa.shape, 1)
    last = lane == columns - 1
    loss = kappa + jnp.where(last, 0.0, pltpu.roll(kappa, columns - 1, 1))
    east = jnp.where(last, 0.0, loss)
    west = pltpu.roll(east, 1, 1)
    return east, west, loss + jnp.where(lane == 0, kappa, west)


def sideways(centre, east, west, here):
    columns = here.shape[1]
    return centre * here + east * pltpu.roll(here, columns - 1, 1) + west * pltpu.roll(here, 1, 1)


FACE, EAST, WEST, CENTRE, KAPPA, COEFS = 0, 4, 8, 12, 16, 17
PART, VALUE, KEPT = 0, SWEEPS, 2 * SWEEPS - 1


def starts_first():
    return jnp.logical_and(lax.axis_index("tile") == 0, lax.axis_index("tm") == 0)


def middle_kernel(controls, codes, table, *refs):
    kept, coef, halves = refs[3:6]

    @pl.when(jnp.logical_not(starts_first()))
    def _():
        own_rows(controls, codes, table, kept, coef, halves, *refs[6:])


def own_rows(controls, codes, table, kept, coef, halves, shifted, face, centre, east, west, field):
    odd = parity()
    slots, _, levels, columns = controls.shape
    shape = (levels, columns)
    total = 2 * SWEEPS
    for kind in range(2):
        halves[kind] = 0.5 * by_level(table, kind, shape)
    sea, land = halves[0], halves[1]

    lane = lax.broadcasted_iota(jnp.int32, shape, 1)
    first_lane, last_lane = lane == 0, lane == columns - 1
    shifted[0] = pltpu.roll(codes[...], columns - 1, 1)
    shifted[1] = pltpu.roll(codes[...], 1, 1)
    previous = lost = None
    for j in range(total):
        place = pl.ds(own_row(odd, j), 1)
        kappa = kappa_of(codes[place, :] + 1, sea, land)
        to_east = kappa + jnp.where(last_lane, 0.0, kappa_of(shifted[0, place, :] + 1, sea, land))
        to_west = kappa + jnp.where(first_lane, 0.0, kappa_of(shifted[1, place, :] + 1, sea, land))
        loss = to_east + to_west
        e, w = jnp.where(last_lane, 0.0, to_east), jnp.where(first_lane, 0.0, to_west)
        east[j], west[j] = e, w
        if j:
            face[j] = previous + kappa
            centre[j - 1] = 1.0 - (lost + face[j])
            lost = loss + face[j]
        else:
            lost = loss
        previous = kappa
        for side, k in ((OUTER, j), (INNER, total - 1 - j)):
            if k == 0:
                coef[side, KAPPA] = kappa
            if k < SWEEPS:
                coef[side, EAST + k], coef[side, WEST + k] = e, w
    centre[total - 1] = 1.0 - lost
    for k in range(SWEEPS):
        coef[OUTER, CENTRE + k], coef[INNER, CENTRE + k] = centre[k], centre[total - 1 - k]
        if k:
            coef[OUTER, FACE + k], coef[INNER, FACE + k] = face[k], face[total - k]

    def value(slot, sweep, j):
        return field[sweep - 1, slot, j] if sweep else controls[slot, own_row(odd, j)]

    for sweep in range(1, SWEEPS + 1):
        low, high = sweep - 1, total - sweep
        before = [None] * slots
        here = [value(slot, sweep - 1, low) for slot in range(slots)]
        for j in range(low, high + 1):
            c, e, w = centre[j], east[j], west[j]
            below = face[j] if j > low else None
            above = face[j + 1] if j < high else None
            for slot in range(slots):
                after = None
                result = sideways(c, e, w, here[slot])
                if above is not None:
                    after = value(slot, sweep - 1, j + 1)
                    result = result + above * after
                if below is not None:
                    result = result + below * before[slot]
                if j == low:
                    kept[OUTER, slot, PART + sweep - 1] = result
                elif j == high:
                    kept[INNER, slot, PART + sweep - 1] = result
                else:
                    field[sweep - 1, slot, j] = result
                    if j == low + 1:
                        kept[OUTER, slot, VALUE + sweep - 1] = result
                    if j == high - 1:
                        kept[INNER, slot, VALUE + sweep - 1] = result
                before[slot], here[slot] = here[slot], after


def edge_here(odd):
    tile, tiles = lax.axis_index("tile"), lax.axis_size("tile")
    return jnp.where(odd == 1, tile == tiles - 1, tile == 0)


def side_rows(side, odd, controls, neighbour, kept, coef, weights, face, centre, east, west, field):
    slots = controls.shape[0]
    if neighbour is None:
        face[SWEEPS] = coef[side, KAPPA]
    else:
        far, far_kappa = neighbour
        previous = far_kappa(-SWEEPS)
        lost = None
        for k in range(1 - SWEEPS, 1):
            i = k + SWEEPS
            kappa = far_kappa(k) if k else coef[side, KAPPA]
            step = previous + kappa
            face[i] = step
            if lost is not None:
                centre[i - 1] = 1.0 - (lost + step)
            if k:
                e, w, loss = along_row(kappa)
                east[i], west[i] = e, w
                lost = loss + step
            previous = kappa
    centre[SWEEPS] = coef[side, CENTRE] - face[SWEEPS]

    def value(slot, sweep, k):
        if sweep == 0:
            return far(slot, k) if k < 0 else controls[slot, row_of(side, odd, k)]
        if k == sweep:
            return kept[side, slot, VALUE + sweep - 1]
        return field[sweep - 1, slot, k + SWEEPS]

    for sweep in range(1, SWEEPS + 1):
        low = 0 if neighbour is None else sweep - SWEEPS
        before = [None if neighbour is None else value(slot, sweep - 1, low - 1) for slot in range(slots)]
        here = [value(slot, sweep - 1, low) for slot in range(slots)]
        for k in range(low, sweep):
            i = k + SWEEPS
            below = face[i] if k <= 0 else coef[side, FACE + k]
            if k < sweep - 1:
                above = face[i + 1] if k < 0 else coef[side, FACE + k + 1]
                c = centre[i] if k <= 0 else coef[side, CENTRE + k]
                e, w = (east[i], west[i]) if k < 0 else (coef[side, EAST + k], coef[side, WEST + k])
            for slot in range(slots):
                after = None
                if k < sweep - 1:
                    after = value(slot, sweep - 1, k + 1)
                    result = sideways(c, e, w, here[slot]) + above * after
                    if before[slot] is not None:
                        result = result + below * before[slot]
                else:
                    result = kept[side, slot, PART + sweep - 1]
                    if before[slot] is not None:
                        result = result + below * before[slot]
                    if k == 0:
                        result = result - below * here[slot]
                if sweep == SWEEPS:
                    place = half_row(odd, k if side == OUTER else 2 * SWEEPS - 1 - k)
                    weights[slot, place] = result.astype(weights.dtype)
                else:
                    field[sweep - 1, slot, i] = result
                before[slot], here[slot] = here[slot], after


def neighbour_of(packet, slots, halves):
    return (
        lambda slot, k: decode(packet, slots, slot, -1 - k),
        lambda k: kappa_of(decode_codes(packet, slots, -1 - k), halves[0], halves[1]),
    )


def inner_kernel(controls, packet, kept, coef, halves, weights, *scratch):
    neighbour = neighbour_of(packet, controls.shape[0], halves)
    side_rows(INNER, parity(), controls, neighbour, kept, coef, weights, *scratch)


def outer_kernel(controls, packet, kept, coef, halves, weights, *scratch):
    odd = parity()
    edge = edge_here(odd)

    @pl.when(edge)
    def _():
        side_rows(OUTER, odd, controls, None, kept, coef, weights, *scratch)

    @pl.when(jnp.logical_not(edge))
    def _():
        neighbour = neighbour_of(packet, controls.shape[0], halves)
        side_rows(OUTER, odd, controls, neighbour, kept, coef, weights, *scratch)


def products(pert, weight, total):
    return [
        term if old is None else old + term
        for old, term in zip(total, [p.astype(jnp.float32) * weight for p in pert])
    ]


def own_kernel(factor, pert, owner, inner, outer, near_part, far_part, near_others, far_others, sems):
    odd = parity()
    count, here = lax.axis_size("tm"), lax.axis_index("tm")
    slots, variables = inner.shape[0], pert.shape[1]

    def member(step, slot):
        return owner[lax.rem(here - step + count, count) * slots + slot]

    copies = []
    for step in range(1, count):
        for slot in range(slots):
            place = (step - 1) * slots + slot
            for side, (start, others) in enumerate(
                ((inner_start(odd), near_others), (outer_start(odd), far_others))
            ):
                copies.append(
                    pltpu.make_async_copy(
                        pert.at[member(step, slot), :, pl.ds(start, SWEEPS)],
                        others.at[place],
                        sems.at[2 * place + side],
                    )
                )
    for copy in copies:
        copy.start()
    for start, weights, part in (
        (inner_start(odd), inner, near_part),
        (outer_start(odd), outer, far_part),
    ):
        for row in range(SWEEPS):
            total = [None] * variables
            for slot in range(slots):
                weight = weights[slot, row].astype(jnp.float32) * factor
                who = member(0, slot)
                total = products([pert[who, v, start + row] for v in range(variables)], weight, total)
            for v in range(variables):
                part[v, row] = total[v]
    for copy in copies:
        copy.wait()


def add_others(factor, part, others, arrived, row, variables):
    total = [part[v, row] for v in variables]
    for index, weights in enumerate(arrived):
        slots = weights.shape[0]
        for slot in range(slots):
            weight = weights[slot, row].astype(jnp.float32) * factor
            place = index * slots + slot
            total = products([others[place, v, row] for v in variables], weight, total)
    return total


def add_and_write(factor, start, part, others, arrived, out, ready, sems):
    count = part.shape[0]
    half = (count + 1) // 2
    writes = []
    for first in range(0, count, half):
        variables = range(first, min(first + half, count))
        for row in range(SWEEPS):
            for v, total in zip(variables, add_others(factor, part, others, arrived, row, variables)):
                ready[v, row] = total
        for v in variables:
            writes.append(pltpu.make_async_copy(ready.at[v], out.at[v, pl.ds(start, SWEEPS)], sems.at[v]))
            writes[-1].start()
    for copy in writes:
        copy.wait()


def near_kernel(factor, part, others, *refs):
    *arrived, out, ready, sems = refs
    add_and_write(factor, inner_start(parity()), part, others, arrived, out, ready, sems)


def far_kernel(factor, part, others, *refs):
    *arrived, _, out, ready, sems = refs
    add_and_write(factor, outer_start(parity()), part, others, arrived, out, ready, sems)


def cost(flops, moved):
    return pl.CostEstimate(flops=flops, bytes_accessed=moved, transcendentals=0)


def near(value):
    return pltpu.with_memory_space_constraint(value, pltpu.VMEM)


def far(value):
    return pltpu.with_memory_space_constraint(value, pltpu.HBM)


def on_device(controls, perturbations, owner, land_mask, diffusivity):
    slots, height, levels, columns = controls.shape
    members, variables = perturbations.shape[1:3]
    count = lax.axis_size("tm")
    factor = 1.0 / math.sqrt(owner.shape[0] - 1)
    row = (levels, columns)
    f32, bf16 = jnp.float32, jnp.bfloat16
    dma = pltpu.SemaphoreType.DMA

    packet = pltpu.VMEM((unit_count(slots), levels, columns // QUARTERS), jnp.int32)
    middle_scratch = [pltpu.VMEM((2, height, columns), jnp.int32)]
    middle_scratch += [pltpu.VMEM((height, *row), f32)] * 4
    middle_scratch += [pltpu.VMEM((SWEEPS - 1, slots, height, *row), f32)]
    middle_out = (
        pltpu.VMEM((2, slots, KEPT, *row), f32),
        pltpu.VMEM((2, COEFS, *row), f32),
        pltpu.VMEM((2, *row), f32),
    )
    my_across, my_within, mine, codes, table, *middle = pl.pallas_call(
        pack_kernel,
        out_shape=(
            packet,
            packet,
            pltpu.VMEM(controls.shape, f32),
            pltpu.VMEM((height, columns), jnp.int32),
            pltpu.VMEM((2, levels), f32),
            *middle_out,
        ),
        in_specs=[ANY, ANY, ANY],
        out_specs=(VMEM,) * 8,
        scratch_shapes=[dma((4 * slots + 2,)), *middle_scratch],
        compiler_params=PARAMS,
        name="pack",
    )(far(controls), far(land_mask), far(diffusivity))
    across = swap_across(my_across)
    within = swap_within(my_within)
    mine = near(mine)

    half = pltpu.VMEM((slots, SWEEPS, *row), bf16)
    kept, coef, halves = pl.pallas_call(
        middle_kernel,
        out_shape=middle_out,
        in_specs=[VMEM] * 6,
        out_specs=(VMEM,) * 3,
        scratch_shapes=middle_scratch,
        input_output_aliases={3: 0, 4: 1, 5: 2},
        compiler_params=PARAMS,
        cost_estimate=cost(1, 1),
        name="middle",
    )(mine, near(codes), near(table), *map(near, middle))
    shared = (near(kept), near(coef), near(halves))

    def side(kernel, name, *operands):
        return pl.pallas_call(
            kernel,
            out_shape=half,
            in_specs=[VMEM] * len(operands),
            out_specs=VMEM,
            scratch_shapes=[pltpu.VMEM((SWEEPS + 1, *row), f32)] * 4
            + [pltpu.VMEM((SWEEPS - 1, slots, 2 * SWEEPS, *row), f32)],
            compiler_params=PARAMS,
            cost_estimate=cost(1, 1),
            name=name,
        )(*operands)

    inner = side(inner_kernel, "inner_rows", mine, near(within), *shared)

    def shift(value):
        return [
            near(lax.ppermute(value, "tm", [(i, (i + step) % count) for i in range(count)]))
            for step in range(1, count)
        ]

    inner_arrived = shift(inner)
    outer = side(outer_kernel, "outer_rows", mine, near(across), *shared)
    outer_arrived = shift(outer)

    arrivals = count - 1
    part = pltpu.VMEM((variables, SWEEPS, *row), f32)
    others = pltpu.VMEM((max(arrivals, 1) * slots, variables, SWEEPS, *row), bf16)
    near_part, far_part, near_others, far_others = pl.pallas_call(
        lambda *refs: own_kernel(factor, *refs),
        out_shape=(part, part, others, others),
        in_specs=[VMEM, SMEM, VMEM, VMEM],
        out_specs=(VMEM,) * 4,
        scratch_shapes=[dma((2 * max(arrivals, 1) * slots,))],
        compiler_params=PARAMS,
        cost_estimate=cost(4_000_000, 2_000_000),
        name="own_products",
    )(near(perturbations[0]), owner, near(inner), near(outer))
    result = jax.ShapeDtypeStruct((variables, height, *row), f32)
    scratch = [pltpu.VMEM((variables, SWEEPS, *row), f32), dma((variables,))]
    out = pl.pallas_call(
        lambda *refs: near_kernel(factor, *refs),
        out_shape=result,
        in_specs=[VMEM] * (2 + arrivals),
        out_specs=ANY,
        scratch_shapes=scratch,
        compiler_params=PARAMS,
        cost_estimate=cost(1_000_000, 1_000_000),
        name="near_products",
    )(near(near_part), near(near_others), *inner_arrived)
    out = pl.pallas_call(
        lambda *refs: far_kernel(factor, *refs),
        out_shape=result,
        in_specs=[VMEM] * (2 + arrivals) + [ANY],
        out_specs=ANY,
        scratch_shapes=scratch,
        input_output_aliases={2 + arrivals: 0},
        compiler_params=PARAMS,
        cost_estimate=cost(1_000_000, 1_000_000),
        name="far_products",
    )(near(far_part), near(far_others), *outer_arrived, out)
    return out[None]


def solution(mesh):
    return jax.shard_map(
        on_device,
        mesh=mesh,
        in_specs=(
            P("tm", "tile", None, None),
            P("tm", None, None, "tile", None, None),
            P(),
            P("tile", None),
            P(),
        ),
        out_specs=P("tm", None, "tile", None, None),
        check_vma=False,
    )
```

```python
import functools
import math

import jax
import jax.numpy as jnp
from jax import lax
from jax.experimental import pallas as pl
from jax.experimental.pallas import tpu as pltpu
from jax.sharding import PartitionSpec as P

SWEEPS = 4
VMEM = pl.BlockSpec(memory_space=pltpu.VMEM)
SMEM = pl.BlockSpec(memory_space=pltpu.SMEM)
ANY = pl.BlockSpec(memory_space=pl.ANY)
PARAMS = pltpu.CompilerParams(vmem_limit_bytes=16 * 1024 * 1024)


def parity():
    return lax.rem(lax.axis_index("tile"), 2)


def own_row(odd, j):
    return j + odd * (2 * SWEEPS - 1 - 2 * j)


OUTER, INNER = 0, 1


def row_of(side, odd, k):
    return own_row(odd, k if side == OUTER else 2 * SWEEPS - 1 - k)


def half_row(odd, j):
    return j % SWEEPS + odd * (SWEEPS - 1 - 2 * (j % SWEEPS))


def outer_start(odd):
    return SWEEPS * odd


def inner_start(odd):
    return SWEEPS * (1 - odd)


def swap_within(value):
    pairs = [(i, i + 1) for i in range(0, lax.axis_size("tile"), 2)]
    return lax.ppermute(value, "tile", pairs + [(b, a) for a, b in pairs])


def swap_across(value):
    tiles, times = lax.axis_size("tile"), lax.axis_size("tm")
    pairs = [((i, t), (i + 1, t)) for i in range(1, tiles - 1, 2) for t in range(times)]
    pairs += [((i, t), (i, t + 1)) for i in (0, tiles - 1) for t in range(0, times, 2)]
    flat = [(a * times + t, b * times + u) for (a, t), (b, u) in pairs]
    return lax.ppermute(value, ("tile", "tm"), flat + [(b, a) for a, b in flat])


FRACTION = (16, 16, 12, 12)


def to_fixed(value, bits):
    return jnp.round(value * float(2**bits)).astype(jnp.int32) + (8 << bits)


def from_fixed(value, bits):
    return (value - (8 << bits)).astype(jnp.float32) * float(0.5**bits)


QUARTERS = 4
PAIR_UNITS = 2 * QUARTERS + QUARTERS // 2


def unit_count(slots):
    return QUARTERS * slots + PAIR_UNITS * ((slots + 1) // 2) + 1


def encode(slots, read, code, packet):
    width = packet.shape[2]

    def quarters(value):
        return [value[:, part * width : (part + 1) * width] for part in range(QUARTERS)]

    def halves_together(value):
        parts = quarters(value)
        return [low | (high << 16) for low, high in zip(parts[: QUARTERS // 2], parts[QUARTERS // 2 :])]

    units, pairs = [], []
    for slot in range(slots):
        one, two, three, four = (to_fixed(read(slot, k), FRACTION[k]) for k in range(SWEEPS))
        units += quarters(one | (two << 20))
        rest = two >> 12
        if slot % 2:
            before = pairs.pop()
            pairs.append((before[0] | (three << 16), before[1] | (four << 16), before[2] | (rest << 8)))
        else:
            pairs.append((three, four, rest))
    for three, four, rest in pairs:
        units += quarters(three) + quarters(four) + halves_together(rest)
    for index, unit in enumerate(units):
        packet[index] = unit
    for k in range(SWEEPS):
        for part, unit in enumerate(halves_together(code(k))):
            packet[len(units), pl.ds(k * (QUARTERS // 2) + part, 1), :] = unit


def decode(packet, slots, slot, k):
    base = QUARTERS * slots + PAIR_UNITS * (slot // 2)

    def words(start, count=QUARTERS):
        return jnp.concatenate([packet[start + part] for part in range(count)], axis=1)

    def right(value, bits):
        return lax.shift_right_logical(value, jnp.int32(bits))

    if k == 0:
        value = words(QUARTERS * slot) & 0xFFFFF
    elif k == 1:
        folded = words(base + 2 * QUARTERS, QUARTERS // 2)
        rest = jnp.concatenate([folded, right(folded, 16)], axis=1)
        rest = right(rest, 8) & 0xFF if slot % 2 else rest & 0xFF
        value = right(words(QUARTERS * slot), 20) | (rest << 12)
    else:
        value = words(base + QUARTERS * (k - 2))
        value = right(value, 16) if slot % 2 else value & 0xFFFF
    return from_fixed(value, FRACTION[k])


def decode_codes(packet, slots, k):
    half = QUARTERS // 2
    words = [packet[unit_count(slots) - 1, pl.ds(k * half + part, 1), :] for part in range(half)]
    return jnp.concatenate([word & 0xFFFF for word in words] + [word >> 16 for word in words], axis=1)


def pack_kernel(controls, mask, diffusivity, across, within, mine, codes, table, sems):
    odd = parity()
    slots = controls.shape[0]
    copies = [
        pltpu.make_async_copy(mask, codes, sems.at[0]),
        pltpu.make_async_copy(diffusivity, table, sems.at[1]),
    ]
    for start in (outer_start(odd), inner_start(odd)):
        for slot in range(slots):
            for part in range(2):
                rows = pl.ds(start + SWEEPS // 2 * part, SWEEPS // 2)
                copies.append(
                    pltpu.make_async_copy(controls.at[slot, rows], mine.at[slot, rows], sems.at[len(copies)])
                )
    own, outer, inner = copies[:2], copies[2 : 2 + 2 * slots], copies[2 + 2 * slots :]
    for copy in own[:1] + outer + inner + own[1:]:
        copy.start()

    def read(side, arriving, slot, k):
        if k == 0:
            for copy in arriving[2 * slot : 2 * slot + 2]:
                copy.wait()
        return mine[slot, row_of(side, odd, k)]

    def code(side, k):
        if side == OUTER and k == 0:
            own[0].wait()
        return codes[pl.ds(row_of(side, odd, k), 1), :] + 1

    for side, packet, arriving in ((OUTER, across, outer), (INNER, within, inner)):
        encode(slots, functools.partial(read, side, arriving), functools.partial(code, side), packet)
    own[1].wait()


def by_level(table, kind, shape):
    levels = shape[0]
    square = jnp.broadcast_to(table[kind : kind + 1, :], (levels, levels))
    diagonal = lax.broadcasted_iota(jnp.int32, square.shape, 0) == lax.broadcasted_iota(jnp.int32, square.shape, 1)
    return jnp.broadcast_to(jnp.sum(jnp.where(diagonal, square, 0.0), axis=1, keepdims=True), shape)


def kappa_of(code, sea, land):
    return jnp.where(jnp.broadcast_to(code, sea.shape) == 2, land, sea)


def along_row(kappa):
    columns = kappa.shape[1]
    lane = lax.broadcasted_iota(jnp.int32, kappa.shape, 1)
    last = lane == columns - 1
    loss = kappa + jnp.where(last, 0.0, pltpu.roll(kappa, columns - 1, 1))
    east = jnp.where(last, 0.0, loss)
    west = pltpu.roll(east, 1, 1)
    return east, west, loss + jnp.where(lane == 0, kappa, west)


def sideways(centre, east, west, here):
    columns = here.shape[1]
    return centre * here + east * pltpu.roll(here, columns - 1, 1) + west * pltpu.roll(here, 1, 1)


FACE, EAST, WEST, CENTRE, KAPPA, COEFS = 0, 4, 8, 12, 16, 17
PART, VALUE, KEPT = 0, SWEEPS, 2 * SWEEPS - 1


def middle_kernel(controls, codes, table, kept, coef, halves, shifted, face, centre, east, west, field):
    odd = parity()
    slots, _, levels, columns = controls.shape
    shape = (levels, columns)
    total = 2 * SWEEPS
    for kind in range(2):
        halves[kind] = 0.5 * by_level(table, kind, shape)
    sea, land = halves[0], halves[1]

    lane = lax.broadcasted_iota(jnp.int32, shape, 1)
    first_lane, last_lane = lane == 0, lane == columns - 1
    shifted[0] = pltpu.roll(codes[...], columns - 1, 1)
    shifted[1] = pltpu.roll(codes[...], 1, 1)
    previous = lost = None
    for j in range(total):
        place = pl.ds(own_row(odd, j), 1)
        kappa = kappa_of(codes[place, :] + 1, sea, land)
        to_east = kappa + jnp.where(last_lane, 0.0, kappa_of(shifted[0, place, :] + 1, sea, land))
        to_west = kappa + jnp.where(first_lane, 0.0, kappa_of(shifted[1, place, :] + 1, sea, land))
        loss = to_east + to_west
        e, w = jnp.where(last_lane, 0.0, to_east), jnp.where(first_lane, 0.0, to_west)
        east[j], west[j] = e, w
        if j:
            face[j] = previous + kappa
            centre[j - 1] = 1.0 - (lost + face[j])
            lost = loss + face[j]
        else:
            lost = loss
        previous = kappa
        for side, k in ((OUTER, j), (INNER, total - 1 - j)):
            if k == 0:
                coef[side, KAPPA] = kappa
            if k < SWEEPS:
                coef[side, EAST + k], coef[side, WEST + k] = e, w
    centre[total - 1] = 1.0 - lost
    for k in range(SWEEPS):
        coef[OUTER, CENTRE + k], coef[INNER, CENTRE + k] = centre[k], centre[total - 1 - k]
        if k:
            coef[OUTER, FACE + k], coef[INNER, FACE + k] = face[k], face[total - k]

    def value(slot, sweep, j):
        return field[sweep - 1, slot, j] if sweep else controls[slot, own_row(odd, j)]

    for sweep in range(1, SWEEPS + 1):
        low, high = sweep - 1, total - sweep
        before = [None] * slots
        here = [value(slot, sweep - 1, low) for slot in range(slots)]
        for j in range(low, high + 1):
            c, e, w = centre[j], east[j], west[j]
            below = face[j] if j > low else None
            above = face[j + 1] if j < high else None
            for slot in range(slots):
                after = None
                result = sideways(c, e, w, here[slot])
                if above is not None:
                    after = value(slot, sweep - 1, j + 1)
                    result = result + above * after
                if below is not None:
                    result = result + below * before[slot]
                if j == low:
                    kept[OUTER, slot, PART + sweep - 1] = result
                elif j == high:
                    kept[INNER, slot, PART + sweep - 1] = result
                else:
                    field[sweep - 1, slot, j] = result
                    if j == low + 1:
                        kept[OUTER, slot, VALUE + sweep - 1] = result
                    if j == high - 1:
                        kept[INNER, slot, VALUE + sweep - 1] = result
                before[slot], here[slot] = here[slot], after


def edge_here(odd):
    tile, tiles = lax.axis_index("tile"), lax.axis_size("tile")
    return jnp.where(odd == 1, tile == tiles - 1, tile == 0)


def side_rows(side, odd, controls, neighbour, kept, coef, weights, face, centre, east, west, field):
    slots = controls.shape[0]
    if neighbour is None:
        face[SWEEPS] = coef[side, KAPPA]
    else:
        far, far_kappa = neighbour
        previous = far_kappa(-SWEEPS)
        lost = None
        for k in range(1 - SWEEPS, 1):
            i = k + SWEEPS
            kappa = far_kappa(k) if k else coef[side, KAPPA]
            step = previous + kappa
            face[i] = step
            if lost is not None:
                centre[i - 1] = 1.0 - (lost + step)
            if k:
                e, w, loss = along_row(kappa)
                east[i], west[i] = e, w
                lost = loss + step
            previous = kappa
    centre[SWEEPS] = coef[side, CENTRE] - face[SWEEPS]

    def value(slot, sweep, k):
        if sweep == 0:
            return far(slot, k) if k < 0 else controls[slot, row_of(side, odd, k)]
        if k == sweep:
            return kept[side, slot, VALUE + sweep - 1]
        return field[sweep - 1, slot, k + SWEEPS]

    for sweep in range(1, SWEEPS + 1):
        low = 0 if neighbour is None else sweep - SWEEPS
        before = [None if neighbour is None else value(slot, sweep - 1, low - 1) for slot in range(slots)]
        here = [value(slot, sweep - 1, low) for slot in range(slots)]
        for k in range(low, sweep):
            i = k + SWEEPS
            below = face[i] if k <= 0 else coef[side, FACE + k]
            if k < sweep - 1:
                above = face[i + 1] if k < 0 else coef[side, FACE + k + 1]
                c = centre[i] if k <= 0 else coef[side, CENTRE + k]
                e, w = (east[i], west[i]) if k < 0 else (coef[side, EAST + k], coef[side, WEST + k])
            for slot in range(slots):
                after = None
                if k < sweep - 1:
                    after = value(slot, sweep - 1, k + 1)
                    result = sideways(c, e, w, here[slot]) + above * after
                    if before[slot] is not None:
                        result = result + below * before[slot]
                else:
                    result = kept[side, slot, PART + sweep - 1]
                    if before[slot] is not None:
                        result = result + below * before[slot]
                    if k == 0:
                        result = result - below * here[slot]
                if sweep == SWEEPS:
                    place = half_row(odd, k if side == OUTER else 2 * SWEEPS - 1 - k)
                    weights[slot, place] = result.astype(weights.dtype)
                else:
                    field[sweep - 1, slot, i] = result
                before[slot], here[slot] = here[slot], after


def neighbour_of(packet, slots, halves):
    return (
        lambda slot, k: decode(packet, slots, slot, -1 - k),
        lambda k: kappa_of(decode_codes(packet, slots, -1 - k), halves[0], halves[1]),
    )


def inner_kernel(controls, packet, kept, coef, halves, weights, *scratch):
    neighbour = neighbour_of(packet, controls.shape[0], halves)
    side_rows(INNER, parity(), controls, neighbour, kept, coef, weights, *scratch)


def outer_kernel(controls, packet, kept, coef, halves, weights, *scratch):
    odd = parity()
    edge = edge_here(odd)

    @pl.when(edge)
    def _():
        side_rows(OUTER, odd, controls, None, kept, coef, weights, *scratch)

    @pl.when(jnp.logical_not(edge))
    def _():
        neighbour = neighbour_of(packet, controls.shape[0], halves)
        side_rows(OUTER, odd, controls, neighbour, kept, coef, weights, *scratch)


def products(pert, weight, total):
    return [
        term if old is None else old + term
        for old, term in zip(total, [p.astype(jnp.float32) * weight for p in pert])
    ]


def own_kernel(factor, pert, owner, inner, outer, near_part, far_part, near_others, far_others, sems):
    odd = parity()
    count, here = lax.axis_size("tm"), lax.axis_index("tm")
    slots, variables = inner.shape[0], pert.shape[1]

    def member(step, slot):
        return owner[lax.rem(here - step + count, count) * slots + slot]

    copies = []
    for step in range(1, count):
        for slot in range(slots):
            place = (step - 1) * slots + slot
            for side, (start, others) in enumerate(
                ((inner_start(odd), near_others), (outer_start(odd), far_others))
            ):
                copies.append(
                    pltpu.make_async_copy(
                        pert.at[member(step, slot), :, pl.ds(start, SWEEPS)],
                        others.at[place],
                        sems.at[2 * place + side],
                    )
                )
    for copy in copies:
        copy.start()
    for start, weights, part in (
        (inner_start(odd), inner, near_part),
        (outer_start(odd), outer, far_part),
    ):
        for row in range(SWEEPS):
            total = [None] * variables
            for slot in range(slots):
                weight = weights[slot, row].astype(jnp.float32) * factor
                who = member(0, slot)
                total = products([pert[who, v, start + row] for v in range(variables)], weight, total)
            for v in range(variables):
                part[v, row] = total[v]
    for copy in copies:
        copy.wait()


def add_others(factor, part, others, arrived, row, variables):
    total = [part[v, row] for v in variables]
    for index, weights in enumerate(arrived):
        slots = weights.shape[0]
        for slot in range(slots):
            weight = weights[slot, row].astype(jnp.float32) * factor
            place = index * slots + slot
            total = products([others[place, v, row] for v in variables], weight, total)
    return total


def add_and_write(factor, start, part, others, arrived, out, ready, sems):
    count = part.shape[0]
    half = (count + 1) // 2
    writes = []
    for first in range(0, count, half):
        variables = range(first, min(first + half, count))
        for row in range(SWEEPS):
            for v, total in zip(variables, add_others(factor, part, others, arrived, row, variables)):
                ready[v, row] = total
        for v in variables:
            writes.append(pltpu.make_async_copy(ready.at[v], out.at[v, pl.ds(start, SWEEPS)], sems.at[v]))
            writes[-1].start()
    for copy in writes:
        copy.wait()


def near_kernel(factor, part, others, *refs):
    *arrived, out, ready, sems = refs
    add_and_write(factor, inner_start(parity()), part, others, arrived, out, ready, sems)


def far_kernel(factor, part, others, *refs):
    *arrived, _, out, ready, sems = refs
    add_and_write(factor, outer_start(parity()), part, others, arrived, out, ready, sems)


def cost(flops, moved):
    return pl.CostEstimate(flops=flops, bytes_accessed=moved, transcendentals=0)


def near(value):
    return pltpu.with_memory_space_constraint(value, pltpu.VMEM)


def far(value):
    return pltpu.with_memory_space_constraint(value, pltpu.HBM)


def on_device(controls, perturbations, owner, land_mask, diffusivity):
    slots, height, levels, columns = controls.shape
    members, variables = perturbations.shape[1:3]
    count = lax.axis_size("tm")
    factor = 1.0 / math.sqrt(owner.shape[0] - 1)
    row = (levels, columns)
    f32, bf16 = jnp.float32, jnp.bfloat16
    dma = pltpu.SemaphoreType.DMA

    packet = pltpu.VMEM((unit_count(slots), levels, columns // QUARTERS), jnp.int32)
    my_across, my_within, mine, codes, table = pl.pallas_call(
        pack_kernel,
        out_shape=(
            packet,
            packet,
            pltpu.VMEM(controls.shape, f32),
            pltpu.VMEM((height, columns), jnp.int32),
            pltpu.VMEM((2, levels), f32),
        ),
        in_specs=[ANY, ANY, ANY],
        out_specs=(VMEM,) * 5,
        scratch_shapes=[dma((2 * 2 * slots + 2,))],
        compiler_params=PARAMS,
        name="pack",
    )(far(controls), far(land_mask), far(diffusivity))
    across = swap_across(my_across)
    within = swap_within(my_within)
    mine = near(mine)

    half = pltpu.VMEM((slots, SWEEPS, *row), bf16)
    middle_scratch = [pltpu.VMEM((2, height, columns), jnp.int32)]
    middle_scratch += [pltpu.VMEM((height, *row), f32)] * 4
    middle_scratch += [pltpu.VMEM((SWEEPS - 1, slots, height, *row), f32)]
    kept, coef, halves = pl.pallas_call(
        middle_kernel,
        out_shape=(
            pltpu.VMEM((2, slots, KEPT, *row), f32),
            pltpu.VMEM((2, COEFS, *row), f32),
            pltpu.VMEM((2, *row), f32),
        ),
        in_specs=[VMEM] * 3,
        out_specs=(VMEM,) * 3,
        scratch_shapes=middle_scratch,
        compiler_params=PARAMS,
        cost_estimate=cost(1, 1),
        name="middle",
    )(mine, near(codes), near(table))
    shared = (near(kept), near(coef), near(halves))

    def side(kernel, name, *operands):
        return pl.pallas_call(
            kernel,
            out_shape=half,
            in_specs=[VMEM] * len(operands),
            out_specs=VMEM,
            scratch_shapes=[pltpu.VMEM((SWEEPS + 1, *row), f32)] * 4
            + [pltpu.VMEM((SWEEPS - 1, slots, 2 * SWEEPS, *row), f32)],
            compiler_params=PARAMS,
            cost_estimate=cost(1, 1),
            name=name,
        )(*operands)

    inner = side(inner_kernel, "inner_rows", mine, near(within), *shared)

    def shift(value):
        return [
            near(lax.ppermute(value, "tm", [(i, (i + step) % count) for i in range(count)]))
            for step in range(1, count)
        ]

    inner_arrived = shift(inner)
    outer = side(outer_kernel, "outer_rows", mine, near(across), *shared)
    outer_arrived = shift(outer)

    arrivals = count - 1
    part = pltpu.VMEM((variables, SWEEPS, *row), f32)
    others = pltpu.VMEM((max(arrivals, 1) * slots, variables, SWEEPS, *row), bf16)
    near_part, far_part, near_others, far_others = pl.pallas_call(
        lambda *refs: own_kernel(factor, *refs),
        out_shape=(part, part, others, others),
        in_specs=[VMEM, SMEM, VMEM, VMEM],
        out_specs=(VMEM,) * 4,
        scratch_shapes=[dma((2 * max(arrivals, 1) * slots,))],
        compiler_params=PARAMS,
        cost_estimate=cost(4_000_000, 2_000_000),
        name="own_products",
    )(near(perturbations[0]), owner, near(inner), near(outer))
    result = jax.ShapeDtypeStruct((variables, height, *row), f32)
    scratch = [pltpu.VMEM((variables, SWEEPS, *row), f32), dma((variables,))]
    out = pl.pallas_call(
        lambda *refs: near_kernel(factor, *refs),
        out_shape=result,
        in_specs=[VMEM] * (2 + arrivals),
        out_specs=ANY,
        scratch_shapes=scratch,
        compiler_params=PARAMS,
        cost_estimate=cost(1_000_000, 1_000_000),
        name="near_products",
    )(near(near_part), near(near_others), *inner_arrived)
    out = pl.pallas_call(
        lambda *refs: far_kernel(factor, *refs),
        out_shape=result,
        in_specs=[VMEM] * (2 + arrivals) + [ANY],
        out_specs=ANY,
        scratch_shapes=scratch,
        input_output_aliases={2 + arrivals: 0},
        compiler_params=PARAMS,
        cost_estimate=cost(1_000_000, 1_000_000),
        name="far_products",
    )(near(far_part), near(far_others), *outer_arrived, out)
    return out[None]


def solution(mesh):
    return jax.shard_map(
        on_device,
        mesh=mesh,
        in_specs=(
            P("tm", "tile", None, None),
            P("tm", None, None, "tile", None, None),
            P(),
            P("tile", None),
            P(),
        ),
        out_specs=P("tm", None, "tile", None, None),
        check_vma=False,
    )
```
